128 devices in a mesh: head: 2 (over x_hi), blk: 64 (over x_lo, y, z, core).
Axes of the slice: x: 4 (x_hi: 2, x_lo: 2; x = x_hi * 2 + x_lo), y: 4, z: 4, core: 2. Of those that a mesh axis runs over, the one named last changes fastest.
Arguments:
- acts: bfloat16 [16384, 1536], P(('head', 'blk')), may hold values from -6 to 6
- teacher: bfloat16 [16384, 1536], P(('head', 'blk')), may hold values from -6 to 6
- valid: int32 [1], replicated, may hold values from 8192 to 16384
- doc_starts: int32 [16], replicated, may hold values from 0 to 16383, as said below
- routes: int32 [16384, 4], P(('head', 'blk')), may hold values from 0 to 31, all different within a row; in each aligned block of 128 rows (0 to 127, 128 to 255, ...) at most 24 rows name the same one
- gates: float32 [16384, 4], P(('head', 'blk')), as said below
- w_query: bfloat16 [1536, 1536], P(('head', 'blk')), may hold values from -0.15625 to 0.15625
- key_weight: bfloat16 [1536, 256], P(('head', 'blk')), may hold values from -0.15625 to 0.15625
- value_weight: bfloat16 [1536, 256], P(('head', 'blk')), may hold values from -0.15625 to 0.15625
- w_out: bfloat16 [1536, 1536], P(('head', 'blk')), may hold values from -4 to 4
- gain_attn: bfloat16 [1536], P(('head', 'blk')), may hold values from 0.5 to 1.5
- gain_ffn: bfloat16 [1536], P(('head', 'blk')), may hold values from 0.5 to 1.5
- w_gate: bfloat16 [1536, 24576], P(None, 'blk'), may hold values from -0.15625 to 0.15625
- w_up: bfloat16 [1536, 24576], P(None, 'blk'), may hold values from -0.15625 to 0.15625
- w_down: bfloat16 [24576, 1536], P('blk'), may hold values from -0.875 to 0.875
Outputs:
- activations: bfloat16 [16384, 1536], P(('head', 'blk'))
- grad_acts: float32 [16384, 1536], P(('head', 'blk'))
- grad_query: float32 [1536, 1536], P(('head', 'blk'))
- grad_key: float32 [1536, 256], P(('head', 'blk'))
- grad_value: float32 [1536, 256], P(('head', 'blk'))
- grad_out: float32 [1536, 1536], P(('head', 'blk'))
- grad_gain_attn: float32 [1536], P(('head', 'blk'))
- grad_gain_ffn: float32 [1536], P(('head', 'blk'))
- grad_gate: float32 [1536, 24576], P(None, 'blk')
- grad_up: float32 [1536, 24576], P(None, 'blk')
- grad_down: float32 [24576, 1536], P('blk')
The draws below stay inside these ranges and needn't reach their ends.
Inputs may be any that keep to these rules, and one draw needn't show every extreme that they name: `doc_starts`: the first entry is 0 and the entries never fall; one document begins before token 128 and covers every token up to 8319. `routes`: a row names 4 different experts; among the rows of one device no expert is named more than 24 times. `gates`: each row is positive and sums to one.
All inputs are finite; a program needn't handle non-finite values.
Results may differ from the reference program's by a relative error of at most 0.023.
Values may be sent and summed in bfloat16 or wider, within the bound.
No kernel may reach another device: no remote copies, remote signals or barrier semaphores. Data moves between devices by JAX's collectives and lax.ppermute only.
A program may use at most 192 MiB of HBM per device.

```python
import math
import jax
import jax.numpy as jnp
import numpy as np
from jax import lax

MODEL_WIDTH = 1536
QUERY_HEADS = 12
KEY_VALUE_HEADS = 2
HEAD_SIZE = 128
FFE = 768
TOP = 4
WINDOW = 4096
TOK_DEV = 128
NDOC = 16
EXPERTS = 32
CAP = 24
STREAM_TOKENS = 16384
N_HEAD = 2
N_BLK = 64


def draw_doc_starts(key, part):
    key = jax.random.fold_in(key, 11)
    first_key, last_key, rest_key = jax.random.split(key, 3)
    first_doc = jax.random.randint(first_key, (1,), 1, TOK_DEV)
    long_end = jax.random.randint(last_key, (1,), STREAM_TOKENS // 2 + TOK_DEV, STREAM_TOKENS * 3 // 4)
    others = jnp.sort(jax.random.randint(rest_key, (NDOC - 3,), STREAM_TOKENS * 3 // 4, STREAM_TOKENS))
    return jnp.concatenate([jnp.zeros((1,), jnp.int32), first_doc, long_end, others]).astype(jnp.int32)


def draw_gates(key, part):
    key = jax.random.fold_in(key, 7)
    logits = jax.random.normal(key, (STREAM_TOKENS, TOP), jnp.float32) * 0.5
    return jax.nn.softmax(logits, axis=-1).astype(jnp.float32)


def levels(own_key, extent, cuts, least, largest):
    gain, own = 1.0, jax.random.fold_in(own_key, 6)
    for axis_at, parts in cuts:
        steps = jnp.exp(jax.random.uniform(jax.random.fold_in(own, axis_at), (parts,), jnp.float32, least / len(cuts), largest / len(cuts)))
        gain = gain * jnp.repeat(steps, extent[axis_at] // parts).reshape([-1 if axis == axis_at else 1 for axis in range(len(extent))])
    return gain


def shared_out(own_key, own, number, rows, number_of, top, limit, slope):
    order = jax.random.permutation(own_key, number_of)
    packed, common = load_shares(number_of, rows * top, limit, slope, True), load_shares(number_of, rows * top, limit, slope, False)
    places = jnp.arange(number_of)

    def named(tallies, rotation):
        used = int((tallies > 0).sum())
        fixed = max(1, used // 4)
        shifted = fixed + (places - fixed + rotation * (used - fixed)) % max(1, number_of - fixed)
        return jnp.zeros((number_of,), jnp.int32).at[order[jnp.where(places < fixed, places, shifted)]].set(jnp.asarray(tallies, jnp.int32))

    tallies = jnp.where(number % 4 == 0, named(packed, number // 4), named(common, number - number // 4 - 1))
    mixed = jax.random.permutation(jax.random.fold_in(own, 3), number_of)
    donor, sink = mixed[0:number_of // 2 * 2:2], mixed[1:number_of // 2 * 2:2]
    slack = jnp.minimum(tallies[donor] - 1, limit - tallies[sink]) // 2
    slack = jnp.where((donor == order[0]) | (sink == order[0]) | (tallies[sink] == 0), 0, jnp.maximum(slack, 0))
    shifted = jax.random.randint(jax.random.fold_in(own, 4), (number_of // 2,), 0, 1 << 20) % (slack + 1)
    tallies = tallies.at[donor].add(-shifted).at[sink].add(shifted)
    items = jnp.searchsorted(jnp.cumsum(tallies), jnp.arange(rows * top), side="right").astype(jnp.int32)
    table = items.reshape(top, rows).T
    table = table[jax.random.permutation(jax.random.fold_in(own, 1), rows)]
    rotation = jax.random.randint(jax.random.fold_in(own, 2), (rows, 1), 0, top)
    return jnp.take_along_axis(table, (jnp.arange(top)[None, :] + rotation) % top, axis=1)


def load_shares(number_of, total, reach, lean, full):
    loads = [(1 << 20) // math.isqrt(standing ** lean) + 1 for standing in range(1, number_of + 1)]
    largest = reach if full else min(reach, max(-(-total // number_of), total * loads[0] // sum(loads)))
    least = 1 if total - largest >= number_of - 1 else 0
    given, rest = [largest] + [least] * (number_of - 1), total - largest - least * (number_of - 1)
    while rest > 0:
        movable = [i for i in range(1, number_of) if given[i] < largest] or [i for i in range(1, number_of) if given[i] < reach]
        pool, budget = sum([loads[i] for i in movable]), rest
        for i in movable:
            addition = min(reach - given[i], max(1, budget * loads[i] // pool), rest)
            given[i] = given[i] + addition
            rest = rest - addition
    return np.array(given)


def gaussian(rng, extent, width, limit, cuts=(), kind=jnp.bfloat16):
    factor_of = levels(rng, extent, cuts, -0.22, 0.18) if cuts else 1.0
    values = jax.random.normal(rng, extent, jnp.float32) * width * factor_of
    return jnp.minimum(jnp.maximum(values, -limit), limit).astype(kind)


def setup_inputs(seed: int = 0) -> dict:
    arg_keys = jax.random.split(jax.random.key(seed), 16)
    acts = gaussian(arg_keys[0], (STREAM_TOKENS, MODEL_WIDTH), 1.0, 6.0, ((0, 128),))
    teacher = gaussian(arg_keys[1], (STREAM_TOKENS, MODEL_WIDTH), 1.0, 6.0, ((0, 128),))
    valid = jax.random.randint(arg_keys[2], (1,), STREAM_TOKENS // 2, STREAM_TOKENS + 1).astype(jnp.int32)
    doc_starts = draw_doc_starts(jax.random.fold_in(arg_keys[15], 71), 0)
    routes_keys = jax.random.split(jax.random.fold_in(arg_keys[4], 1), STREAM_TOKENS // TOK_DEV)
    routes_turns = jax.random.permutation(jax.random.fold_in(arg_keys[4], 3), STREAM_TOKENS // TOK_DEV)
    routes = jax.vmap(lambda own, number: shared_out(jax.random.fold_in(arg_keys[4], 2), own, number, TOK_DEV, EXPERTS, TOP, CAP, 1))(routes_keys, routes_turns).reshape((STREAM_TOKENS, TOP))
    gates = draw_gates(jax.random.fold_in(arg_keys[15], 71), 0)
    w_query = gaussian(arg_keys[6], (MODEL_WIDTH, MODEL_WIDTH), MODEL_WIDTH ** -0.5, 0.15625, ((0, 128),))
    key_weight = gaussian(arg_keys[7], (MODEL_WIDTH, KEY_VALUE_HEADS * HEAD_SIZE), MODEL_WIDTH ** -0.5, 0.15625, ((0, 128),))
    value_weight = gaussian(arg_keys[8], (MODEL_WIDTH, KEY_VALUE_HEADS * HEAD_SIZE), MODEL_WIDTH ** -0.5, 0.15625, ((0, 128),))
    w_out = gaussian(arg_keys[9], (MODEL_WIDTH, MODEL_WIDTH), 2 ** -0.5, 4.0, ((0, 128),))
    gain_attn = jnp.clip(1.0 + 0.1 * jax.random.normal(arg_keys[10], (MODEL_WIDTH,), jnp.float32), 0.5, 1.5).astype(jnp.bfloat16)
    gain_ffn = jnp.clip(1.0 + 0.1 * jax.random.normal(arg_keys[11], (MODEL_WIDTH,), jnp.float32), 0.5, 1.5).astype(jnp.bfloat16)
    w_gate = gaussian(arg_keys[12], (MODEL_WIDTH, EXPERTS * FFE), MODEL_WIDTH ** -0.5, 0.15625, ((1, 64),))
    w_up = gaussian(arg_keys[13], (MODEL_WIDTH, EXPERTS * FFE), MODEL_WIDTH ** -0.5, 0.15625, ((1, 64),))
    w_down = gaussian(arg_keys[14], (EXPERTS * FFE, MODEL_WIDTH), (FFE // 16) ** -0.5, 0.875, ((0, 64),))
    return dict(acts=acts, teacher=teacher, valid=valid, doc_starts=doc_starts, routes=routes, gates=gates, w_query=w_query, key_weight=key_weight, value_weight=value_weight, w_out=w_out, gain_attn=gain_attn, gain_ffn=gain_ffn, w_gate=w_gate, w_up=w_up, w_down=w_down)


@jax.custom_vjp
def lower_precision(v):
    return lax.optimization_barrier(v.astype(jnp.bfloat16)).astype(jnp.float32)

@jax.custom_vjp
def lower_precision_back(v):
    return v

def low_keep(v):
    return (lower_precision(v), None)

def low_pass(kept, grad):
    return (grad,)

def back_keep(v):
    return (v, None)

def back_low(kept, grad):
    return (lower_precision(grad),)
lower_precision.defvjp(low_keep, low_pass)
lower_precision_back.defvjp(back_keep, back_low)
NORM_EPS = 1e-06
ROPE_BASE = 1000000.0
MASKED = -1e+30
QUERY_BLOCK_ROWS = 512
TOP_PRECISION = lax.Precision.HIGHEST

def doc_table(positions, doc_starts):
    before = doc_starts[None, :] <= positions[:, None]
    doc_id = lax.optimization_barrier(jnp.sum(before.astype(jnp.int32), axis=-1))
    doc_begin = lax.optimization_barrier(jnp.max(jnp.where(before, doc_starts[None, :], 0), axis=-1))
    return (doc_id, positions - doc_begin)

def rope_tables(offset, head_width):
    inv_freq = jnp.exp(jnp.arange(head_width // 2, dtype=jnp.float32) * (-2.0 * math.log(ROPE_BASE) / head_width))
    angle = offset.astype(jnp.float32)[:, None] * inv_freq[None, :]
    return (jnp.cos(angle), jnp.sin(angle))

def rotate(values, cosine_table, sine_table):
    half_width = values.shape[-1] // 2
    first_half = values[..., :half_width]
    second_half = values[..., half_width:]
    cos_rows = cosine_table[:, None, :]
    sin_rows = sine_table[:, None, :]
    return jnp.concatenate([first_half * cos_rows - second_half * sin_rows, second_half * cos_rows + first_half * sin_rows], axis=-1)

def rms_norm(values, gain_vec):
    return values * lax.rsqrt(lax.optimization_barrier(jnp.mean(values * values, axis=-1, keepdims=True)) + NORM_EPS) * gain_vec

def attention(query_rows_all, key_rows, rows_of_value, doc_id, positions):
    score_scale = HEAD_SIZE ** (-0.5)
    heads_per_group = QUERY_HEADS // KEY_VALUE_HEADS
    blocks_of_query = query_rows_all.reshape(STREAM_TOKENS // QUERY_BLOCK_ROWS, QUERY_BLOCK_ROWS, KEY_VALUE_HEADS, heads_per_group, HEAD_SIZE)
    pos_blocks = positions.reshape(-1, QUERY_BLOCK_ROWS)
    doc_blocks = doc_id.reshape(-1, QUERY_BLOCK_ROWS)

    def one_block(block_args):
        query_part, pos_part, doc_part = block_args
        scores = jnp.einsum('tkgd,skd->kgts', query_part, key_rows, precision=TOP_PRECISION) * score_scale
        scores = lower_precision_back(scores)
        distance = pos_part[:, None] - positions[None, :]
        allowed = (doc_part[:, None] == doc_id[None, :]) & (distance >= 0) & (distance < WINDOW)
        scores = jnp.where(allowed[None, None], scores, MASKED)
        row_max = lax.optimization_barrier(jnp.max(scores, axis=-1, keepdims=True))
        weights = jnp.exp(scores - row_max)
        weights = weights / lax.optimization_barrier(jnp.sum(weights, axis=-1, keepdims=True))
        weights = lower_precision(weights)
        return jnp.einsum('kgts,skd->tkgd', weights, rows_of_value, precision=TOP_PRECISION)
    result = lax.map(jax.checkpoint(one_block), (blocks_of_query, pos_blocks, doc_blocks))
    return result.reshape(STREAM_TOKENS, QUERY_HEADS, HEAD_SIZE)

def experts_mix(normed_two, routes, gates, w_gate, w_up, w_down):
    devices = N_HEAD * N_BLK
    flat_routes = routes.reshape(devices, TOK_DEV * TOP)
    chosen = (flat_routes[:, :, None] == jnp.arange(EXPERTS, dtype=jnp.int32)[None, None, :]).astype(jnp.int32)
    slot_index = lax.optimization_barrier(jnp.sum((jnp.cumsum(chosen, axis=1) - chosen) * chosen, axis=-1))
    target = (flat_routes * CAP + slot_index).astype(jnp.int32)
    pair_owner = jnp.arange(TOK_DEV * TOP, dtype=jnp.int32) // TOP
    local_rows = normed_two.reshape(devices, TOK_DEV, MODEL_WIDTH)
    picked_in = local_rows[:, pair_owner]
    device_ids = jnp.arange(devices, dtype=jnp.int32)[:, None]
    buffer = jnp.zeros((devices, EXPERTS * CAP, MODEL_WIDTH), jnp.float32).at[device_ids, target].add(picked_in)
    buffer = buffer.reshape(devices, EXPERTS, CAP, MODEL_WIDTH).transpose(1, 0, 2, 3).reshape(EXPERTS, devices * CAP, MODEL_WIDTH)
    half_units = FFE // 2
    gate_w = w_gate.reshape(MODEL_WIDTH, EXPERTS, 2, half_units).transpose(1, 2, 0, 3)
    up_w = w_up.reshape(MODEL_WIDTH, EXPERTS, 2, half_units).transpose(1, 2, 0, 3)
    down_w = w_down.reshape(EXPERTS, 2, half_units, MODEL_WIDTH)

    def one_expert(expert_args):
        rows_in, gate_part, up_part, down_part = expert_args
        summed = jnp.zeros(rows_in.shape, jnp.float32)
        for piece_index in range(2):
            routed = lower_precision_back(rows_in)
            gate_pre = lower_precision_back(jnp.dot(routed, gate_part[piece_index], precision=TOP_PRECISION))
            up_pre = lower_precision_back(jnp.dot(routed, up_part[piece_index], precision=TOP_PRECISION))
            hidden_units = lower_precision(jax.nn.silu(gate_pre) * up_pre)
            summed = summed + lower_precision(lower_precision_back(jnp.dot(hidden_units, down_part[piece_index], precision=TOP_PRECISION)))
        return summed
    expert_rows = lax.map(jax.checkpoint(one_expert), (buffer, gate_w, up_w, down_w))
    expert_rows = expert_rows.reshape(EXPERTS, devices, CAP, MODEL_WIDTH).transpose(1, 0, 2, 3).reshape(devices, EXPERTS * CAP, MODEL_WIDTH)
    picked = expert_rows[device_ids, target]
    weighted = picked.reshape(devices, TOK_DEV, TOP, MODEL_WIDTH) * gates.reshape(devices, TOK_DEV, TOP, 1)
    return lax.optimization_barrier(jnp.sum(weighted, axis=2)).reshape(STREAM_TOKENS, MODEL_WIDTH)

def reference(acts, teacher, valid, doc_starts, routes, gates, w_query, key_weight, value_weight, w_out, gain_attn, gain_ffn, w_gate, w_up, w_down):
    positions = jnp.arange(STREAM_TOKENS, dtype=jnp.int32)
    doc_id, offset = doc_table(positions, doc_starts)
    cosine_table, sine_table = rope_tables(offset, HEAD_SIZE)
    gate_values = gates.astype(jnp.float32)
    floats = [item.astype(jnp.float32) for item in (acts, w_query, key_weight, value_weight, w_out, gain_attn, gain_ffn, w_gate, w_up, w_down)]

    def forward(values_in, wq_full, full_key_weight, full_value_weight, wo_full, gain_one, gain_two, wg_full, wu_full, wd_full):
        normalized_input = lower_precision(rms_norm(values_in, gain_one))
        query_lin = lower_precision_back(jnp.dot(normalized_input, wq_full, precision=TOP_PRECISION)).reshape(STREAM_TOKENS, QUERY_HEADS, HEAD_SIZE)
        linear_key = lower_precision_back(jnp.dot(normalized_input, full_key_weight, precision=TOP_PRECISION)).reshape(STREAM_TOKENS, KEY_VALUE_HEADS, HEAD_SIZE)
        rows_of_value = lower_precision(lower_precision_back(jnp.dot(normalized_input, full_value_weight, precision=TOP_PRECISION))).reshape(STREAM_TOKENS, KEY_VALUE_HEADS, HEAD_SIZE)
        query_rows_all = lower_precision(lower_precision_back(rotate(query_lin, cosine_table, sine_table)))
        key_rows = lower_precision(lower_precision_back(rotate(linear_key, cosine_table, sine_table)))
        attended = lower_precision(lower_precision_back(attention(query_rows_all, key_rows, rows_of_value, doc_id, positions)))
        branch = lower_precision_back(jnp.dot(attended.reshape(STREAM_TOKENS, MODEL_WIDTH), wo_full, precision=TOP_PRECISION))
        hidden_one = values_in + branch
        normed_two = lower_precision(rms_norm(hidden_one, gain_two))
        return hidden_one + experts_mix(normed_two, routes, gate_values, wg_full, wu_full, wd_full)
    hidden_two, pullback = jax.vjp(forward, *floats)
    valid_count = valid[0]
    live_rows = positions < valid_count
    cotangent = jnp.where(live_rows[:, None], STREAM_TOKENS / valid_count.astype(jnp.float32) * (hidden_two - teacher.astype(jnp.float32)), 0.0)
    grads = pullback(cotangent)
    return (hidden_two.astype(jnp.bfloat16), grads[0], grads[1], grads[2], grads[3], grads[4], grads[5], grads[6], grads[7], grads[8], grads[9])
```

```python
import math

import jax
import jax.numpy as jnp
import numpy as np
from jax import lax
from jax.experimental import pallas as pl
from jax.experimental.pallas import tpu as pltpu
from jax.sharding import PartitionSpec as P

HEAD_SIZE = 128
GROUP = 6
HALF_WIDTH = GROUP * HEAD_SIZE
WINDOW = 4096
CAP = 24

NORM_EPS = 1e-06
ROPE_BASE = 1000000.0
MASKED = -1e30
SCALE = HEAD_SIZE ** (-0.5)
SCALE_LOG2 = SCALE * math.log2(math.e)

ALL = ("xh", "xl", "y", "z", "c")
CHIPS = ("xh", "xl", "y", "z")
HALF_CHIPS = ("xl", "y", "z")
PLANE_CHIPS = ("y", "z")
SWAP = [(0, 1), (1, 0)]

f32 = jnp.float32
bf16 = jnp.bfloat16


def dot(a, b, dims=((1,), (0,))):
    return lax.dot_general(a, b, (dims, ((), ())), preferred_element_type=f32)


NT = ((1,), (1,))
TN = ((0,), (0,))


def core_swap(value):
    return lax.ppermute(value, "c", SWAP)


def exchange(value, axes):
    return lax.all_to_all(value, axes, 0, 0, tiled=True)


def in_order(core, own, other):
    return jnp.concatenate([jnp.where(core == 0, own, other), jnp.where(core == 0, other, own)])


def doc_begin(positions, doc_starts):
    before = doc_starts[None, :] <= positions[:, None]
    return jnp.max(jnp.where(before, doc_starts[None, :], 0), axis=-1)


def rope_tables(offset):
    inv_freq = jnp.exp(
        jnp.arange(HEAD_SIZE // 2, dtype=f32) * (-2.0 * math.log(ROPE_BASE) / HEAD_SIZE)
    )
    angle = offset.astype(f32)[:, None] * inv_freq[None, :]
    cosine, sine = jnp.cos(angle), jnp.sin(angle)
    return jnp.concatenate([cosine, cosine], axis=1), jnp.concatenate([-sine, sine], axis=1)


def rotate(values, cosine, sine):
    half = HEAD_SIZE // 2
    turned = jnp.concatenate([values[..., half:], values[..., :half]], axis=-1)
    return values * cosine + turned * sine


def rotate_heads(values, cosine, sine):
    heads = values.reshape(values.shape[0], -1, HEAD_SIZE)
    return rotate(heads, cosine[:, None, :], sine[:, None, :]).reshape(values.shape)


def norm_backward(values, inverse, gain_row, incoming_grad):
    scaled = incoming_grad * gain_row
    input_grad = inverse * scaled - values * inverse * inverse * inverse * jnp.mean(
        scaled * values, axis=-1, keepdims=True
    )
    gain_grad = jnp.sum(incoming_grad * values * inverse, axis=0, keepdims=True)
    return (input_grad, gain_grad)


def allowed_pairs(start, first_query, low_ref, shape):
    key_pos = start + lax.broadcasted_iota(jnp.int32, shape, 0)
    query_pos = first_query + lax.broadcasted_iota(jnp.int32, shape, 1)
    return (key_pos >= low_ref[0:1, :]) & (key_pos <= query_pos)


def attend_kernel(meta_ref, low_ref, query_ref, keys_ref, own_ref, out_ref, low_out_ref, log_ref, score_ref):
    blocks, rows = keys_ref.shape[0] + 1, query_ref.shape[0]
    query = query_ref[...]

    def block_of(j):
        return own_ref if j == blocks - 1 else keys_ref.at[j]

    top = None
    for j in range(blocks):
        key = block_of(j)[:, :HEAD_SIZE]
        score_ref[j] = dot(key, query, NT)

        @pl.when(meta_ref[1, j] == 1)
        def _(j=j):
            allowed = allowed_pairs(meta_ref[0, j], meta_ref[0, blocks], low_ref, (rows, rows))
            score_ref[j] = jnp.where(allowed, score_ref[j], MASKED)

        part = jnp.max(score_ref[j].reshape(rows // 8, 8, rows), axis=0)
        top = part if top is None else jnp.maximum(top, part)
    top = jnp.max(top, axis=0, keepdims=True) * SCALE_LOG2
    total = jnp.zeros((8, rows), f32)
    mixed = jnp.zeros((HEAD_SIZE, rows), f32)
    for j in range(blocks):
        weights = jnp.exp2(score_ref[j] * SCALE_LOG2 - top)
        total = total + jnp.sum(weights.reshape(rows // 8, 8, rows), axis=0)
        mixed = mixed + dot(block_of(j)[:, HEAD_SIZE:], weights.astype(bf16), TN)
    total = jnp.sum(total, axis=0, keepdims=True)
    log_ref[0] = jnp.broadcast_to(top + jnp.log2(total), (8, rows))
    mixed = (mixed / total).T
    out_ref[...] = mixed
    low_out_ref[...] = mixed.astype(bf16)


def attend(meta, low, query, keys, own):
    blocks, rows = keys.shape[0] + 1, query.shape[0]
    whole = lambda *shape: pl.BlockSpec(shape, lambda h, meta: (0,) * len(shape))
    by_head = pl.BlockSpec((rows, HEAD_SIZE), lambda h, meta: (0, h))
    return pl.pallas_call(
        attend_kernel,
        grid_spec=pltpu.PrefetchScalarGridSpec(
            num_scalar_prefetch=1,
            grid=(GROUP,),
            in_specs=[whole(8, rows), by_head, whole(*keys.shape), whole(*own.shape)],
            out_specs=[by_head, by_head, pl.BlockSpec((1, 8, rows), lambda h, meta: (h, 0, 0))],
            scratch_shapes=[pltpu.VMEM((blocks, rows, rows), f32)],
        ),
        out_shape=[
            jax.ShapeDtypeStruct((rows, HALF_WIDTH), f32),
            jax.ShapeDtypeStruct((rows, HALF_WIDTH), bf16),
            jax.ShapeDtypeStruct((GROUP, 8, rows), f32),
        ],
        compiler_params=pltpu.CompilerParams(vmem_limit_bytes=48 * 1024 * 1024),
        name="attend",
    )(meta, low, query, keys, own)


def attend_back_kernel(
    meta_ref, low_ref, query_ref, keys_ref, out_ref, grad_ref, log_ref,
    query_grad_ref, keys_grad_ref, delta_ref, sum_ref,
):
    j, blocks, rows = pl.program_id(0), pl.num_programs(0), query_ref.shape[0]

    @pl.when(j == 0)
    def _():
        sum_ref[...] = jnp.zeros_like(sum_ref)
        for h in range(GROUP):
            at = slice(h * HEAD_SIZE, (h + 1) * HEAD_SIZE)
            product = (grad_ref[:, at].astype(f32) * out_ref[:, at]).T
            delta_ref[h] = jnp.broadcast_to(jnp.sum(product, axis=0, keepdims=True), (8, rows))

    key, value = keys_ref[0, :, :HEAD_SIZE], keys_ref[0, :, HEAD_SIZE:]

    def step(masked):
        key_grad = jnp.zeros((rows, HEAD_SIZE), f32)
        value_grad = jnp.zeros((rows, HEAD_SIZE), f32)
        turned_key = key.T
        for h in range(GROUP):
            at = slice(h * HEAD_SIZE, (h + 1) * HEAD_SIZE)
            query, out_grad = query_ref[:, at], grad_ref[:, at]
            weights = jnp.exp2(dot(key, query, NT) * SCALE_LOG2 - log_ref[h, 0:1, :])
            if masked:
                allowed = allowed_pairs(meta_ref[0, j], meta_ref[0, blocks], low_ref, (rows, rows))
                weights = jnp.where(allowed, weights, 0.0)
            score_grad = (weights * (dot(value, out_grad, NT) - delta_ref[h, 0:1, :])).astype(bf16)
            sum_ref[h] = sum_ref[h] + dot(turned_key, score_grad)
            key_grad = key_grad + dot(score_grad, query)
            value_grad = value_grad + dot(weights.astype(bf16), out_grad)
        keys_grad_ref[0, :, :HEAD_SIZE] = (key_grad * SCALE).astype(bf16)
        keys_grad_ref[0, :, HEAD_SIZE:] = value_grad.astype(bf16)

    @pl.when(meta_ref[1, j] == 1)
    def _():
        step(True)

    @pl.when(meta_ref[1, j] == 0)
    def _():
        step(False)

    @pl.when(j == blocks - 1)
    def _():
        for h in range(GROUP):
            query_grad_ref[:, h * HEAD_SIZE : (h + 1) * HEAD_SIZE] = (sum_ref[h] * SCALE).T


def attend_back(meta, low, query, keys, out, out_grad, log_total):
    blocks, rows = keys.shape[0], query.shape[0]
    whole = lambda *shape: pl.BlockSpec(shape, lambda j, meta: (0,) * len(shape))
    by_block = pl.BlockSpec((1, rows, 2 * HEAD_SIZE), lambda j, meta: (j, 0, 0))
    wide = whole(rows, HALF_WIDTH)
    return pl.pallas_call(
        attend_back_kernel,
        grid_spec=pltpu.PrefetchScalarGridSpec(
            num_scalar_prefetch=1,
            grid=(blocks,),
            in_specs=[whole(8, rows), wide, by_block, wide, wide, whole(GROUP, 8, rows)],
            out_specs=[wide, by_block],
            scratch_shapes=[
                pltpu.VMEM((GROUP, 8, rows), f32),
                pltpu.VMEM((GROUP, HEAD_SIZE, rows), f32),
            ],
        ),
        out_shape=[
            jax.ShapeDtypeStruct((rows, HALF_WIDTH), f32),
            jax.ShapeDtypeStruct(keys.shape, bf16),
        ],
        compiler_params=pltpu.CompilerParams(vmem_limit_bytes=48 * 1024 * 1024),
        name="attend_back",
    )(meta, low, query, keys, out, out_grad, log_total)


def to_column_halves(value, half, core):
    width = value.shape[1] // 2
    left, right = value[:, :width], value[:, width:]
    same = lax.ppermute(
        jnp.where(core == 0, left, right), ("xh", "c"), [(a * 2 + k, k * 2 + a) for a in range(2) for k in range(2)]
    )
    cross = lax.ppermute(
        jnp.where(core == 0, right, left), ("xh", "c"), [(a * 2 + k, (1 - k) * 2 + a) for a in range(2) for k in range(2)]
    )
    return jnp.concatenate([jnp.where(half == 0, same, cross), jnp.where(half == 0, cross, same)])


def from_column_halves(value, half, core):
    rows = value.shape[0] // 2
    upper, lower = value[:rows], value[rows:]
    same = lax.ppermute(
        jnp.where(half == 0, upper, lower), ("xh", "c"), [(h * 2 + c, c * 2 + h) for h in range(2) for c in range(2)]
    )
    cross = lax.ppermute(
        jnp.where(half == 0, lower, upper), ("xh", "c"), [(h * 2 + c, c * 2 + 1 - h) for h in range(2) for c in range(2)]
    )
    return jnp.concatenate(
        [jnp.where(core == 0, same, cross), jnp.where(core == 0, cross, same)], axis=1
    )


def body(
    acts, teacher, valid, doc_starts, routes, gates,
    w_query, key_weight, value_weight, w_out, gain_attn, gain_ffn, w_gate, w_up, w_down,
):
    half, core = lax.axis_index("xh"), lax.axis_index("c")
    plane, spot = lax.axis_index(("xh", "xl")), lax.axis_index(PLANE_CHIPS)
    chip = lax.axis_index(CHIPS)
    tok_rows, model_dim = acts.shape
    chip_rows = 2 * tok_rows
    spots = lax.axis_size(PLANE_CHIPS)
    planes = lax.axis_size(("xh", "xl"))
    chips = spots * planes
    total_tokens = chips * chip_rows
    shard_rows = w_query.shape[0]

    gain_pair = jnp.pad(jnp.stack([gain_attn, gain_ffn], axis=1), ((0, 0), (0, HEAD_SIZE - 2)))
    by_core = jnp.stack(
        [
            jnp.concatenate(
                [
                    key_weight[:, k * HEAD_SIZE : (k + 1) * HEAD_SIZE],
                    value_weight[:, k * HEAD_SIZE : (k + 1) * HEAD_SIZE],
                    gain_pair,
                    w_query[:, k * HALF_WIDTH : (k + 1) * HALF_WIDTH],
                ],
                axis=1,
            )
            for k in range(2)
        ]
    )
    own_weights = exchange(by_core, "c").reshape(2 * shard_rows, -1)
    kv_width = 3 * HEAD_SIZE
    kv_part, query_part = own_weights[:, :kv_width], own_weights[:, kv_width:]
    full_kv = exchange(jnp.broadcast_to(kv_part[None], (chips,) + kv_part.shape), CHIPS).reshape(
        model_dim, kv_width
    )
    out_part = to_column_halves(w_out, half, core)
    gathered = lax.all_gather(jnp.concatenate([query_part, out_part], axis=1), CHIPS)
    full_query = gathered.reshape(model_dim, -1)[:, :HALF_WIDTH]
    full_out = gathered.reshape(2, HALF_WIDTH, -1)[:, :, HALF_WIDTH:]

    pick = (np.arange(kv_width)[None, :] == 2 * HEAD_SIZE + np.arange(2)[:, None]).astype(np.float32)
    gain_rows = dot(jnp.asarray(pick, bf16), full_kv, NT)
    gain_one, gain_two = gain_rows[0:1], gain_rows[1:2]

    first_token = chip * chip_rows
    chip_pos = first_token + jnp.arange(chip_rows, dtype=jnp.int32)
    begin = doc_begin(chip_pos, doc_starts)
    cosine, sine = rope_tables(chip_pos - begin)
    low = jnp.maximum(begin, chip_pos - (WINDOW - 1))
    low_rows = jnp.broadcast_to(low[None, :], (8, chip_rows))
    block_at = jnp.arange(spots, dtype=jnp.int32)
    block_plane = jnp.where(block_at < spot, plane, plane - 1)
    starts = jnp.concatenate([(block_plane * spots + block_at) * chip_rows, first_token[None]])
    needs_mask = ((starts < jnp.max(low)) | (starts + chip_rows > first_token)).astype(jnp.int32)
    meta = jnp.stack(
        [
            jnp.concatenate([starts, first_token[None]]),
            jnp.concatenate([needs_mask, jnp.zeros((1,), jnp.int32)]),
        ]
    )

    experts = 32
    all_slots = experts * CAP
    flat_routes = routes.reshape(-1)
    chosen = (flat_routes[:, None] == jnp.arange(experts, dtype=jnp.int32)[None, :]).astype(jnp.int32)
    slot_index = jnp.sum((jnp.cumsum(chosen, axis=0) - chosen) * chosen, axis=1)
    target = (flat_routes * CAP + slot_index).reshape(routes.shape)
    hits = target[None, :, :] == jnp.arange(all_slots, dtype=jnp.int32)[:, None, None]
    placed = jnp.any(hits, axis=2).astype(bf16)
    slot_gate = jnp.sum(jnp.where(hits, gates[None], 0.0), axis=(1, 2))[:, None]
    hits_by_token = target[:, None, :] == jnp.arange(all_slots, dtype=jnp.int32)[None, :, None]
    token_gate = jnp.sum(jnp.where(hits_by_token, gates[:, None, :], 0.0), axis=2)
    token_gate_high = token_gate.astype(bf16)
    token_gate_low = (token_gate - token_gate_high.astype(f32)).astype(bf16)
    placed_by_token = jnp.any(hits_by_token, axis=2).astype(bf16)

    chip_acts = in_order(core, acts, core_swap(acts)).astype(f32)
    inverse_one = lax.rsqrt(jnp.mean(chip_acts * chip_acts, axis=-1, keepdims=True) + NORM_EPS)
    normed_one = (chip_acts * inverse_one * gain_one).astype(bf16)
    kv_lin = dot(normed_one, full_kv[:, : 2 * HEAD_SIZE])
    key_seq = rotate(kv_lin[:, :HEAD_SIZE], cosine, sine).astype(bf16)
    own_kv = jnp.concatenate([key_seq, kv_lin[:, HEAD_SIZE:].astype(bf16)], axis=1)
    before_kv = lax.ppermute(own_kv, ("xh", "xl"), [(p, p + 1) for p in range(planes - 1)])
    later = (block_at > spot)[:, None, None]
    seen_kv = exchange(jnp.where(later, own_kv[None], before_kv[None]), PLANE_CHIPS)
    query_lin = dot(normed_one, full_query)
    query_seq = rotate_heads(query_lin, cosine, sine).astype(bf16)
    attn_wide, attn, log_total = attend(meta, low_rows, query_seq, seen_kv, own_kv)

    branch = jnp.concatenate([dot(attn, full_out[0]), dot(attn, full_out[1])], axis=1)
    upper, lower = branch[:tok_rows], branch[tok_rows:]
    branch = jnp.where(core == 0, upper, lower) + core_swap(jnp.where(core == 0, lower, upper))
    values_in = acts.astype(f32)
    hidden_one = values_in + branch
    inverse_two = lax.rsqrt(jnp.mean(hidden_one * hidden_one, axis=-1, keepdims=True) + NORM_EPS)
    normed_two = (hidden_one * inverse_two * gain_two).astype(bf16)

    def to_experts(rows):
        mine = exchange(rows.reshape(experts, CAP, model_dim), HALF_CHIPS).reshape(all_slots, model_dim)
        return mine, core_swap(mine)

    def from_experts(mine, theirs):
        both = mine + core_swap(theirs.astype(bf16)).astype(f32)
        both = both.astype(bf16).reshape(experts, CAP, model_dim)
        return exchange(both, HALF_CHIPS).reshape(all_slots, model_dim)

    def expert_forward(rows):
        gate_pre, up_pre = dot(rows, w_gate), dot(rows, w_up)
        hidden = (jax.nn.silu(gate_pre) * up_pre).astype(bf16)
        return gate_pre, up_pre, hidden, dot(hidden, w_down)

    def expert_backward(kept, grad_rows):
        gate_pre, up_pre = kept[0], kept[1]
        grad_hidden = dot(grad_rows, w_down, NT)
        sigmoid = jax.nn.sigmoid(gate_pre)
        grad_gate = (grad_hidden * up_pre * sigmoid * (1.0 + gate_pre * (1.0 - sigmoid))).astype(bf16)
        grad_up = (grad_hidden * gate_pre * sigmoid).astype(bf16)
        return grad_gate, grad_up, dot(grad_gate, w_gate, NT) + dot(grad_up, w_up, NT)

    rows_mine, rows_theirs = to_experts(dot(placed, normed_two).astype(bf16))
    kept_theirs = expert_forward(rows_theirs)
    kept_mine = expert_forward(rows_mine)
    returned = from_experts(kept_mine[3], kept_theirs[3])
    mixture = dot(token_gate_high, returned) + dot(token_gate_low, returned)
    hidden_two = hidden_one + mixture

    valid_count = valid[0]
    own_pos = first_token + core * tok_rows + jnp.arange(tok_rows, dtype=jnp.int32)
    grad_two = jnp.where(
        (own_pos < valid_count)[:, None],
        total_tokens / valid_count.astype(f32) * (hidden_two - teacher.astype(f32)),
        0.0,
    )
    grad_two_high = grad_two.astype(bf16)
    grad_two_low = (grad_two - grad_two_high.astype(f32)).astype(bf16)
    grad_slots = (slot_gate * (dot(placed, grad_two_high) + dot(placed, grad_two_low))).astype(bf16)
    grads_mine, grads_theirs = to_experts(grad_slots)
    back_theirs = expert_backward(kept_theirs, grads_theirs)
    back_mine = expert_backward(kept_mine, grads_mine)
    grad_returned = from_experts(back_mine[2], back_theirs[2])

    def both_halves(partial):
        partial = partial.astype(bf16)
        return partial.astype(f32) + lax.ppermute(partial, "xh", SWAP).astype(f32)

    grad_w_down = both_halves(dot(kept_mine[2], grads_mine, TN) + dot(kept_theirs[2], grads_theirs, TN))
    grad_w_gate = both_halves(dot(rows_mine, back_mine[0], TN) + dot(rows_theirs, back_theirs[0], TN))
    grad_w_up = both_halves(dot(rows_mine, back_mine[1], TN) + dot(rows_theirs, back_theirs[1], TN))

    grad_normed_two = dot(placed_by_token, grad_returned)
    norm_two_grad, gain_two_grad = norm_backward(hidden_one, inverse_two, gain_two, grad_normed_two)
    grad_one = grad_two + norm_two_grad
    grad_branch = grad_one.astype(bf16)
    chip_branch = in_order(core, grad_branch, core_swap(grad_branch))
    left, right = chip_branch[:, :HALF_WIDTH], chip_branch[:, HALF_WIDTH:]
    grad_attn = (dot(left, full_out[0], NT) + dot(right, full_out[1], NT)).astype(bf16)

    def chip_sums(partial):
        pieces = partial.astype(bf16).reshape(chips, 2 * shard_rows, -1)
        return jnp.sum(exchange(pieces, CHIPS).astype(f32), axis=0)

    out_sums = chip_sums(jnp.stack([dot(attn, left, TN), dot(attn, right, TN)]))
    grad_w_out = from_column_halves(out_sums, half, core)

    every_kv = jnp.concatenate([seen_kv, own_kv[None]])
    query_grad, kv_grad = attend_back(
        meta, low_rows, query_seq, every_kv, attn_wide, grad_attn, log_total
    )
    query_lin_grad = rotate_heads(query_grad.astype(bf16).astype(f32), cosine, -sine).astype(bf16)
    came = exchange(kv_grad[:spots], PLANE_CHIPS).astype(f32)
    from_later = jnp.sum(jnp.where((block_at > spot)[:, None, None], came, 0.0), axis=0)
    from_before = jnp.sum(jnp.where((block_at <= spot)[:, None, None], came, 0.0), axis=0)
    from_next = lax.ppermute(from_before, ("xh", "xl"), [(p + 1, p) for p in range(planes - 1)])
    kv_sum = (from_later + from_next + kv_grad[spots].astype(f32)).astype(bf16)
    key_lin_grad = rotate(kv_sum[:, :HEAD_SIZE].astype(f32), cosine, -sine).astype(bf16)
    kv_lin_grad = jnp.concatenate([key_lin_grad, kv_sum[:, HEAD_SIZE:]], axis=1)

    normed_grad = dot(query_lin_grad, full_query, NT) + dot(kv_lin_grad, full_kv[:, : 2 * HEAD_SIZE], NT)
    upper, lower = normed_grad[:tok_rows], normed_grad[tok_rows:]
    normed_grad = jnp.where(core == 0, upper, lower) + core_swap(jnp.where(core == 0, lower, upper))
    own_inverse = jnp.where(core == 0, inverse_one[:tok_rows], inverse_one[tok_rows:])
    input_norm_grad, gain_one_grad = norm_backward(values_in, own_inverse, gain_one, normed_grad)
    grad_acts = grad_one + input_norm_grad

    query_sums = chip_sums(dot(normed_one, query_lin_grad, TN))
    gain_grads = jnp.concatenate([gain_one_grad, gain_two_grad]).astype(bf16)
    gain_columns = dot(gain_grads, jnp.asarray(np.eye(2, HEAD_SIZE), bf16), TN)
    kv_sums = chip_sums(jnp.concatenate([dot(normed_one, kv_lin_grad, TN), gain_columns], axis=1))
    sums = jnp.concatenate([kv_sums, query_sums], axis=1).reshape(2, shard_rows, -1)
    sums = exchange(sums, "c")

    def columns(begin_at, width):
        return jnp.concatenate([sums[k, :, begin_at : begin_at + width] for k in range(2)], axis=1)

    gain_sums = sums[0, :, 2 * HEAD_SIZE : 2 * HEAD_SIZE + 2] + sums[1, :, 2 * HEAD_SIZE : 2 * HEAD_SIZE + 2]
    return (
        hidden_two.astype(bf16),
        grad_acts,
        columns(kv_width, HALF_WIDTH),
        columns(0, HEAD_SIZE),
        columns(HEAD_SIZE, HEAD_SIZE),
        grad_w_out,
        gain_sums[:, 0],
        gain_sums[:, 1],
        grad_w_gate,
        grad_w_up,
        grad_w_down,
    )


def solution(mesh):
    fine_mesh = jax.sharding.Mesh(mesh.devices.reshape(2, 2, 4, 4, 2), ALL)
    rows, vector = P(ALL, None), P(ALL)
    wide, tall = P(None, ("xl", "y", "z", "c")), P(("xl", "y", "z", "c"), None)
    return jax.shard_map(
        body,
        mesh=fine_mesh,
        in_specs=(
            rows, rows, P(), P(), rows, rows, rows, rows, rows, rows, vector, vector, wide, wide, tall,
        ),
        out_specs=(rows, rows, rows, rows, rows, rows, vector, vector, wide, wide, tall),
        check_vma=False,
    )
```

```python
import math

import jax
import jax.numpy as jnp
import numpy as np
from jax import lax
from jax.experimental import pallas as pl
from jax.experimental.pallas import tpu as pltpu
from jax.sharding import PartitionSpec as P

HEAD_SIZE = 128
GROUP = 6
HALF_WIDTH = GROUP * HEAD_SIZE
WINDOW = 4096
CAP = 24
EXPERTS = 32

NORM_EPS = 1e-06
ROPE_BASE = 1000000.0
MASKED = -1e30
SCALE = HEAD_SIZE ** (-0.5)
SCALE_LOG2 = SCALE * math.log2(math.e)

ALL = ("xh", "xl", "y", "z", "c")
CHIPS = ("xh", "xl", "y", "z")
HALF_CHIPS = ("xl", "y", "z")
PLANE_CHIPS = ("y", "z")
SWAP = [(0, 1), (1, 0)]
PAIR = [(0, 1), (1, 0), (2, 3), (3, 2)]

f32 = jnp.float32
bf16 = jnp.bfloat16


def dot(a, b, dims=((1,), (0,))):
    return lax.dot_general(a, b, (dims, ((), ())), preferred_element_type=f32)


NT = ((1,), (1,))
TN = ((0,), (0,))


def core_swap(value):
    return lax.ppermute(value, "c", SWAP)


def exchange(value, axes):
    return lax.all_to_all(value, axes, 0, 0, tiled=True)


def gather_ring(value, axes, size):
    pieces = [value] + [
        lax.ppermute(value, axes, [((i + k) % size, i) for i in range(size)]) for k in range(1, size)
    ]
    return pieces


def in_ring_order(pieces, place):
    size = len(pieces)
    ordered = jnp.zeros((size,) + pieces[0].shape, pieces[0].dtype)
    for k, piece in enumerate(pieces):
        ordered = lax.dynamic_update_index_in_dim(ordered, piece, (place + k) % size, 0)
    return ordered


def in_order(core, own, other):
    return jnp.concatenate([jnp.where(core == 0, own, other), jnp.where(core == 0, other, own)])


def of_core(core, rows, own):
    upper, lower = jnp.split(rows, 2)
    return jnp.where((core == 0) == own, upper, lower)


def doc_begin(positions, doc_starts):
    before = doc_starts[None, :] <= positions[:, None]
    return jnp.max(jnp.where(before, doc_starts[None, :], 0), axis=-1)


def rope_tables(offset):
    column = jnp.arange(HEAD_SIZE, dtype=jnp.int32)
    half = HEAD_SIZE // 2
    inv_freq = jnp.exp((column % half).astype(f32) * (-2.0 * math.log(ROPE_BASE) / HEAD_SIZE))
    angle = offset.astype(f32)[:, None] * inv_freq[None, :]
    return jnp.cos(angle), jnp.where(column[None, :] < half, -1.0, 1.0) * jnp.sin(angle)


def rotate(values, cosine, sine):
    half = HEAD_SIZE // 2
    turned = jnp.concatenate([values[..., half:], values[..., :half]], axis=-1)
    return values * cosine + turned * sine


def norm_backward(values, inverse, gain_row, incoming_grad):
    scaled = incoming_grad * gain_row
    input_grad = inverse * scaled - values * inverse * inverse * inverse * jnp.mean(
        scaled * values, axis=-1, keepdims=True
    )
    gain_grad = jnp.sum(incoming_grad * values * inverse, axis=0, keepdims=True)
    return (input_grad, gain_grad)


def block_mask(low, t, blocks, rows, key_axis):
    key_at = lax.broadcasted_iota(jnp.int32, (rows, rows), key_axis)
    allowed = key_at >= low - t * rows
    if t == blocks - 1:
        allowed = allowed & (key_at <= lax.broadcasted_iota(jnp.int32, (rows, rows), 1 - key_axis))
    return allowed


def seen_block(spot, keys_ref, own_ref, t):
    spots = keys_ref.shape[0]
    return own_ref if t == spots else keys_ref.at[lax.rem(spot + t, spots)]


def attend_kernel(
    spot_ref, low_ref, query_ref, keys_ref, own_ref, out_ref, low_out_ref, log_ref, score_ref
):
    blocks, rows = keys_ref.shape[0] + 1, query_ref.shape[0]
    query = query_ref[...]
    low = low_ref[:, 0:1]
    top = None
    for t in range(blocks):
        score = dot(query, seen_block(spot_ref[0], keys_ref, own_ref, t)[:, :HEAD_SIZE], NT)
        score = jnp.where(block_mask(low, t, blocks, rows, 1), score, MASKED)
        score_ref[t] = score
        part = jnp.maximum(score[:, :HEAD_SIZE], score[:, HEAD_SIZE:])
        top = part if top is None else jnp.maximum(top, part)
    top = jnp.max(top, axis=1, keepdims=True) * SCALE_LOG2
    total = jnp.zeros((rows, HEAD_SIZE), f32)
    mixed = jnp.zeros((rows, HEAD_SIZE), f32)
    for t in range(blocks):
        weights = jnp.exp2(score_ref[t] * SCALE_LOG2 - top)
        total = total + weights[:, :HEAD_SIZE] + weights[:, HEAD_SIZE:]
        value = seen_block(spot_ref[0], keys_ref, own_ref, t)[:, HEAD_SIZE:]
        mixed = mixed + dot(weights.astype(bf16), value)
    total = jnp.sum(total, axis=1, keepdims=True)
    log_ref[0] = jnp.broadcast_to(top + jnp.log2(total), (rows, HEAD_SIZE)).T[:8]
    mixed = mixed / total
    out_ref[...] = mixed
    low_out_ref[...] = mixed.astype(bf16)


def attend(spot, low, query, keys, own):
    blocks, rows = keys.shape[0] + 1, query.shape[0]
    whole = lambda *shape: pl.BlockSpec(shape, lambda h, spot: (0,) * len(shape))
    by_head = pl.BlockSpec((rows, HEAD_SIZE), lambda h, spot: (0, h))
    return pl.pallas_call(
        attend_kernel,
        grid_spec=pltpu.PrefetchScalarGridSpec(
            num_scalar_prefetch=1,
            grid=(GROUP,),
            in_specs=[whole(rows, HEAD_SIZE), by_head, whole(*keys.shape), whole(*own.shape)],
            out_specs=[by_head, by_head, pl.BlockSpec((1, 8, rows), lambda h, spot: (h, 0, 0))],
            scratch_shapes=[pltpu.VMEM((blocks, rows, rows), f32)],
        ),
        out_shape=[
            jax.ShapeDtypeStruct((rows, HALF_WIDTH), f32),
            jax.ShapeDtypeStruct((rows, HALF_WIDTH), bf16),
            jax.ShapeDtypeStruct((GROUP, 8, rows), f32),
        ],
        compiler_params=pltpu.CompilerParams(vmem_limit_bytes=56 * 1024 * 1024),
        cost_estimate=pl.CostEstimate(flops=20_000_000_000, bytes_accessed=4_000_000, transcendentals=7_000_000),
        name="attend",
    )(spot, low, query, keys, own)


def place_rows_kernel(route_ref, gate_ref, placed_ref, placed_by_token_ref, gate_high_ref, gate_low_ref, slot_gate_ref):
    tokens, top = route_ref.shape
    slots = EXPERTS * CAP
    expert = lax.broadcasted_iota(jnp.int32, (tokens, HEAD_SIZE), 1)
    chosen = jnp.zeros((tokens, HEAD_SIZE), f32)
    gate = jnp.zeros((tokens, HEAD_SIZE), f32)
    for k in range(top):
        hit = route_ref[:, k : k + 1] == expert
        chosen = chosen + jnp.where(hit, 1.0, 0.0)
        gate = gate + jnp.where(hit, gate_ref[:, k : k + 1], 0.0)
    square = (tokens, tokens)
    earlier = lax.broadcasted_iota(jnp.int32, square, 1) < lax.broadcasted_iota(jnp.int32, square, 0)
    chosen = chosen.astype(bf16)
    before = dot(jnp.where(earlier, 1.0, 0.0).astype(bf16), chosen)
    first = lax.broadcasted_iota(jnp.int32, (HEAD_SIZE, slots), 0) * CAP
    slot = lax.broadcasted_iota(jnp.int32, (HEAD_SIZE, slots), 1)
    within = (slot >= first) & (slot < first + CAP)
    spread = jnp.where(within, 1.0, 0.0).astype(bf16)
    slot_in = jnp.sum(jnp.where(within, slot - first, 0).astype(f32), axis=0, keepdims=True)
    here = (dot(chosen, spread) > 0.5) & (jnp.abs(dot(before.astype(bf16), spread) - slot_in) < 0.5)
    high = gate.astype(bf16)
    low = (gate - high.astype(f32)).astype(bf16)
    high_at = jnp.where(here, dot(high, spread), 0.0)
    low_at = jnp.where(here, dot(low, spread), 0.0)
    placed = jnp.where(here, 1.0, 0.0)
    placed_by_token_ref[...] = placed.astype(bf16)
    placed_ref[...] = placed.T.astype(bf16)
    gate_high_ref[...] = high_at.astype(bf16)
    gate_low_ref[...] = low_at.astype(bf16)
    total = jnp.sum((high_at + low_at).T, axis=1, keepdims=True)
    slot_gate_ref[...] = jnp.broadcast_to(total, (slots, HEAD_SIZE))


def place_rows(routes, gates):
    tokens, slots = routes.shape[0], EXPERTS * CAP
    by_token = jax.ShapeDtypeStruct((tokens, slots), bf16)
    return pl.pallas_call(
        place_rows_kernel,
        out_shape=[
            jax.ShapeDtypeStruct((slots, tokens), bf16),
            by_token,
            by_token,
            by_token,
            jax.ShapeDtypeStruct((slots, HEAD_SIZE), f32),
        ],
        name="place_rows",
    )(routes, gates)


def normed_rows(values, gain_row):
    inverse = lax.rsqrt(jnp.mean(values * values, axis=-1, keepdims=True) + NORM_EPS)
    return (values * inverse * gain_row).astype(bf16)


def project_keys_kernel(acts_ref, weight_ref, cosine_ref, sine_ref, normed_ref, kv_ref, gain_ref):
    pick = lax.broadcasted_iota(jnp.int32, (16, HEAD_SIZE), 0) == lax.broadcasted_iota(jnp.int32, (16, HEAD_SIZE), 1)
    gains = dot(pick.astype(bf16), weight_ref[:, 2 * HEAD_SIZE :], NT)
    gain_ref[...] = gains[:8]
    normed = normed_rows(acts_ref[...].astype(f32), gains[0:1])
    normed_ref[...] = normed
    linear = dot(normed, weight_ref[:, : 2 * HEAD_SIZE])
    key = linear[:, :HEAD_SIZE]
    turned = key * cosine_ref[...] + pltpu.roll(key, HEAD_SIZE // 2, 1) * sine_ref[...]
    kv_ref[:, :HEAD_SIZE] = turned.astype(bf16)
    kv_ref[:, HEAD_SIZE:] = linear[:, HEAD_SIZE:].astype(bf16)


def project_keys(acts, weights, tables):
    rows, width = acts.shape
    whole = lambda *shape: pl.BlockSpec(shape, lambda i: (0,) * len(shape))
    return pl.pallas_call(
        project_keys_kernel,
        grid=(1,),
        in_specs=[whole(rows, width), whole(width, 3 * HEAD_SIZE)] + [whole(rows, HEAD_SIZE)] * 2,
        out_specs=[whole(rows, width), whole(rows, 2 * HEAD_SIZE), whole(8, width)],
        out_shape=[
            jax.ShapeDtypeStruct((rows, width), bf16),
            jax.ShapeDtypeStruct((rows, 2 * HEAD_SIZE), bf16),
            jax.ShapeDtypeStruct((8, width), f32),
        ],
        compiler_params=pltpu.CompilerParams(vmem_limit_bytes=32 * 1024 * 1024),
        name="project_keys",
    )(acts, weights, *tables)


def project_kernel(
    own_ref, acts_ref, gain_ref, weight_ref, own_cosine_ref, own_sine_ref, cosine_ref, sine_ref,
    normed_ref, own_out_ref, out_ref,
):
    normed_ref[...] = normed_rows(acts_ref[...].astype(f32), gain_ref[0:1, :])
    for rows_ref, cos_ref, sin_ref, target in (
        (own_ref, own_cosine_ref, own_sine_ref, own_out_ref),
        (normed_ref, cosine_ref, sine_ref, out_ref),
    ):
        linear = dot(rows_ref[...], weight_ref[...])
        for h in range(GROUP // 2):
            at = slice(h * HEAD_SIZE, (h + 1) * HEAD_SIZE)
            head = linear[:, at]
            turned = head * cos_ref[...] + pltpu.roll(head, HEAD_SIZE // 2, 1) * sin_ref[...]
            target[:, at] = turned.astype(bf16)


def project(own_rows, pair_acts, gains, weight, own_tables, pair_tables):
    shape = jax.ShapeDtypeStruct((own_rows.shape[0], weight.shape[1]), bf16)
    return pl.pallas_call(
        project_kernel,
        out_shape=[jax.ShapeDtypeStruct(own_rows.shape, bf16), shape, shape],
        compiler_params=pltpu.CompilerParams(vmem_limit_bytes=32 * 1024 * 1024),
        name="project",
    )(own_rows, pair_acts, gains, weight, *own_tables, *pair_tables)


def piece_at(place_ref, k, shape):
    depth, width = shape
    row_half = lax.rem(place_ref[1] + k % 2, 2)
    column_half = lax.rem(place_ref[0] + k // 2, 2)
    return (
        pl.ds(pl.multiple_of(row_half * depth, HEAD_SIZE), depth),
        pl.ds(pl.multiple_of(column_half * width, HEAD_SIZE), width),
    )


def out_project_kernel(place_ref, attn_ref, *refs):
    pieces, (own_ref, other_ref, sum_ref) = refs[:-3], refs[-3:]
    rows = own_ref.shape[0]
    sum_ref[...] = jnp.zeros_like(sum_ref)
    for k, piece in enumerate(pieces):
        features, columns = piece_at(place_ref, k, piece.shape)
        sum_ref[:, columns] += dot(attn_ref[:, features], piece[...])
    core = place_ref[2]
    own_ref[...] = sum_ref[pl.ds(pl.multiple_of(core * rows, rows), rows), :]
    other_ref[...] = sum_ref[pl.ds(pl.multiple_of((1 - core) * rows, rows), rows), :]


def out_project(place, attn, pieces):
    rows, width = attn.shape[0], 2 * pieces[0].shape[1]
    shape = jax.ShapeDtypeStruct((rows // 2, width), f32)
    vmem = pl.BlockSpec(memory_space=pltpu.VMEM)
    return pl.pallas_call(
        out_project_kernel,
        in_specs=[pl.BlockSpec(memory_space=pltpu.SMEM)] + [vmem] * (1 + len(pieces)),
        out_specs=[vmem, vmem],
        out_shape=[shape, shape],
        scratch_shapes=[pltpu.VMEM((rows, width), f32)],
        compiler_params=pltpu.CompilerParams(vmem_limit_bytes=32 * 1024 * 1024),
        name="out_project",
    )(place, attn, *pieces)


def out_project_back_kernel(place_ref, grad_ref, *refs):
    pieces, (out_ref, sum_ref) = refs[:-2], refs[-2:]
    sum_ref[...] = jnp.zeros_like(sum_ref)
    for k, piece in enumerate(pieces):
        features, columns = piece_at(place_ref, k, piece.shape)
        sum_ref[:, features] += dot(grad_ref[:, columns], piece[...], NT)
    out_ref[...] = sum_ref[...].astype(bf16)


def out_project_back(place, grad, pieces):
    rows, width = grad.shape[0], 2 * pieces[0].shape[0]
    vmem = pl.BlockSpec(memory_space=pltpu.VMEM)
    return pl.pallas_call(
        out_project_back_kernel,
        in_specs=[pl.BlockSpec(memory_space=pltpu.SMEM)] + [vmem] * (1 + len(pieces)),
        out_specs=vmem,
        out_shape=jax.ShapeDtypeStruct((rows, width), bf16),
        scratch_shapes=[pltpu.VMEM((rows, width), f32)],
        compiler_params=pltpu.CompilerParams(vmem_limit_bytes=32 * 1024 * 1024),
        name="out_project_back",
    )(place, grad, *pieces)


def attend_back_kernel(
    spot_ref, low_ref, query_ref, cosine_ref, sine_ref, keys_ref, own_ref, out_ref, grad_ref, log_ref,
    query_grad_ref, keys_grad_ref, own_grad_ref, sum_ref, turned_key_ref, weight_ref, score_ref,
):
    h, heads = pl.program_id(0), pl.num_programs(0)
    blocks, rows = keys_ref.shape[0] + 1, query_ref.shape[0]
    spot = spot_ref[0]

    @pl.when(h == 0)
    def _():
        sum_ref[...] = jnp.zeros_like(sum_ref)
        for t in range(blocks):
            turned_key_ref[t] = seen_block(spot, keys_ref, own_ref, t)[:, :HEAD_SIZE].T

    query, out_grad = query_ref[...], grad_ref[...]
    delta = jnp.sum((out_grad.astype(f32) * out_ref[...]).T, axis=0, keepdims=True)
    log_total, low = log_ref[0, 0:1, :], low_ref[0:1, :]
    for t in range(blocks):
        block = seen_block(spot, keys_ref, own_ref, t)
        key, value = block[:, :HEAD_SIZE], block[:, HEAD_SIZE:]
        weights = jnp.exp2(dot(key, query, NT) * SCALE_LOG2 - log_total)
        weights = jnp.where(block_mask(low, t, blocks, rows, 0), weights, 0.0)
        weight_ref[t] = weights.astype(bf16)
        score_ref[t] = (weights * (dot(value, out_grad, NT) - delta)).astype(bf16)
    query_grad = jnp.zeros((HEAD_SIZE, rows), f32)
    for t in range(blocks):
        query_grad = query_grad + dot(turned_key_ref[t], score_ref[t])
    query_grad = (query_grad * SCALE).T.astype(bf16).astype(f32)
    turned = query_grad * cosine_ref[...] - pltpu.roll(query_grad, HEAD_SIZE // 2, 1) * sine_ref[...]
    query_grad_ref[...] = turned.astype(bf16)
    for t in range(blocks):
        sum_ref[t, :, :HEAD_SIZE] += dot(score_ref[t], query)
        sum_ref[t, :, HEAD_SIZE:] += dot(weight_ref[t], out_grad)

    @pl.when(h == heads - 1)
    def _():
        for t in range(blocks):
            target = seen_block(spot, keys_grad_ref, own_grad_ref, t)
            target[:, :HEAD_SIZE] = (sum_ref[t, :, :HEAD_SIZE] * SCALE).astype(bf16)
            target[:, HEAD_SIZE:] = sum_ref[t, :, HEAD_SIZE:].astype(bf16)


def attend_back(spot, low, query, cosine, sine, keys, own, out, out_grad, log_total):
    blocks, rows = keys.shape[0] + 1, query.shape[0]
    whole = lambda *shape: pl.BlockSpec(shape, lambda h, spot: (0,) * len(shape))
    by_head = pl.BlockSpec((rows, HEAD_SIZE), lambda h, spot: (0, h))
    table = whole(rows, HEAD_SIZE)
    return pl.pallas_call(
        attend_back_kernel,
        grid_spec=pltpu.PrefetchScalarGridSpec(
            num_scalar_prefetch=1,
            grid=(GROUP,),
            in_specs=[
                whole(8, rows), by_head, table, table, whole(*keys.shape), whole(*own.shape), by_head, by_head,
                pl.BlockSpec((1, 8, rows), lambda h, spot: (h, 0, 0)),
            ],
            out_specs=[by_head, whole(*keys.shape), whole(*own.shape)],
            scratch_shapes=[
                pltpu.VMEM((blocks, rows, 2 * HEAD_SIZE), f32),
                pltpu.VMEM((blocks, HEAD_SIZE, rows), bf16),
                pltpu.VMEM((blocks, rows, rows), bf16),
                pltpu.VMEM((blocks, rows, rows), bf16),
            ],
        ),
        out_shape=[
            jax.ShapeDtypeStruct((rows, HALF_WIDTH), bf16),
            jax.ShapeDtypeStruct(keys.shape, bf16),
            jax.ShapeDtypeStruct(own.shape, bf16),
        ],
        compiler_params=pltpu.CompilerParams(vmem_limit_bytes=56 * 1024 * 1024),
        cost_estimate=pl.CostEstimate(flops=28_000_000_000, bytes_accessed=8_000_000, transcendentals=7_000_000),
        name="attend_back",
    )(spot, low, query, cosine, sine, keys, own, out, out_grad, log_total)


def body(
    acts, teacher, valid, doc_starts, routes, gates,
    w_query, key_weight, value_weight, w_out, gain_attn, gain_ffn, w_gate, w_up, w_down,
):
    half, core = lax.axis_index("xh"), lax.axis_index("c")
    plane, spot = lax.axis_index(("xh", "xl")), lax.axis_index(PLANE_CHIPS)
    chip = lax.axis_index(CHIPS)
    tok_rows, model_dim = acts.shape
    chip_rows = 2 * tok_rows
    spots = lax.axis_size(PLANE_CHIPS)
    planes = lax.axis_size(("xh", "xl"))
    chips = spots * planes
    total_tokens = chips * chip_rows
    shard_rows = w_query.shape[0]

    chip_acts = in_order(core, acts, core_swap(acts))
    pair_acts = lax.ppermute(acts, "z", PAIR)
    pair_acts = in_order(core, pair_acts, core_swap(pair_acts))

    gain_pair = jnp.pad(jnp.stack([gain_attn, gain_ffn], axis=1), ((0, 0), (0, HEAD_SIZE - 2)))
    by_core = jnp.stack(
        [
            jnp.concatenate(
                [
                    key_weight[:, k * HEAD_SIZE : (k + 1) * HEAD_SIZE],
                    value_weight[:, k * HEAD_SIZE : (k + 1) * HEAD_SIZE],
                    gain_pair,
                    w_query[:, k * HALF_WIDTH : (k + 1) * HALF_WIDTH],
                    w_out[:, k * HALF_WIDTH : (k + 1) * HALF_WIDTH],
                ],
                axis=1,
            )
            for k in range(2)
        ]
    )
    own_weights = exchange(by_core, "c").reshape(2 * shard_rows, -1)
    kv_width = 3 * HEAD_SIZE
    kv_part, query_part = own_weights[:, :kv_width], own_weights[:, kv_width : kv_width + HALF_WIDTH]
    side = chip % 2
    quarter = HALF_WIDTH // 2
    by_side = jnp.stack(
        [jnp.concatenate([kv_part, query_part[:, k * quarter : (k + 1) * quarter]], axis=1) for k in range(2)]
    )
    out_pieces = gather_ring(own_weights[:, kv_width + HALF_WIDTH :], "z", 4)
    by_side, out_pieces = lax.optimization_barrier((by_side, out_pieces))
    weights = exchange(
        jnp.broadcast_to(by_side[None], (chips // 2,) + by_side.shape).reshape((chips,) + by_side.shape[1:]), CHIPS
    )
    out_pieces = gather_ring(in_ring_order(out_pieces, lax.axis_index("z")), "y", 4)
    out_pieces = in_ring_order(out_pieces, lax.axis_index("y"))

    first_token = chip * chip_rows
    chip_pos = first_token + jnp.arange(chip_rows, dtype=jnp.int32)
    begin = doc_begin(chip_pos, doc_starts)
    cosine, sine = rope_tables(chip_pos - begin)
    pair_pos = chip_pos + (1 - 2 * side) * chip_rows
    pair_tables = rope_tables(pair_pos - doc_begin(pair_pos, doc_starts))
    low = jnp.maximum(begin, chip_pos - (WINDOW - 1)) - (first_token - WINDOW)
    low_rows = jnp.broadcast_to(low[None, :], (8, chip_rows))
    low_columns = jnp.broadcast_to(low[:, None], (chip_rows, HEAD_SIZE))
    block_at = jnp.arange(spots, dtype=jnp.int32)

    weights, out_pieces, chip_acts, pair_acts = lax.optimization_barrier((weights, out_pieces, chip_acts, pair_acts))
    weights = weights.reshape(model_dim, -1)
    full_kv, half_query = weights[:, :kv_width], weights[:, kv_width:]

    normed_one, own_kv, gain_rows = project_keys(chip_acts, weights, (cosine, sine))
    gain_one, gain_two = gain_rows[0:1], gain_rows[1:2]
    before_kv = lax.ppermute(own_kv, ("xh", "xl"), [(p, p + 1) for p in range(planes - 1)])
    later = (block_at > spot)[:, None, None]
    kv_sent, out_pieces = lax.optimization_barrier(
        (jnp.where(later, own_kv[None], before_kv[None]), out_pieces)
    )
    seen_kv = exchange(kv_sent, PLANE_CHIPS)
    all_slots = EXPERTS * CAP
    placed, placed_by_token, token_gate_high, token_gate_low, slot_gate = place_rows(routes, gates)

    out_pieces = out_pieces.reshape(-1, HALF_WIDTH)
    out_pieces = [
        lax.ppermute(
            out_pieces,
            ("xh", "xl", "c"),
            [
                (c * 4 + (l ^ k % 2) * 2 + (h ^ k // 2), h * 4 + l * 2 + c)
                for h in range(2)
                for l in range(2)
                for c in range(2)
            ],
        )
        for k in range(4)
    ]
    seen_kv, out_pieces = lax.optimization_barrier((seen_kv, out_pieces))

    pair_normed, query_mine, query_theirs = project(
        normed_one, pair_acts, gain_rows, half_query, (cosine, sine), pair_tables
    )
    query_theirs = lax.ppermute(query_theirs, "z", PAIR)
    query_seq = jnp.concatenate(
        [jnp.where(side == 0, query_mine, query_theirs), jnp.where(side == 0, query_theirs, query_mine)], axis=1
    )
    query_seq, placed, slot_gate, token_gate_high, token_gate_low, placed_by_token = lax.optimization_barrier(
        (query_seq, placed, slot_gate, token_gate_high, token_gate_low, placed_by_token)
    )
    spot_word = spot.astype(jnp.int32).reshape(1)
    attn_wide, attn, log_total = attend(spot_word, low_columns, query_seq, seen_kv, own_kv)

    place = jnp.stack([half, lax.axis_index("xl"), core]).astype(jnp.int32)
    branch, other_branch = out_project(place, attn, out_pieces)
    branch = branch + core_swap(other_branch)
    values_in = acts.astype(f32)
    hidden_one = values_in + branch
    inverse_two = lax.rsqrt(jnp.mean(hidden_one * hidden_one, axis=-1, keepdims=True) + NORM_EPS)
    normed_two = (hidden_one * inverse_two * gain_two).astype(bf16)

    def to_experts(rows):
        mine = exchange(rows.reshape(EXPERTS, CAP, model_dim), HALF_CHIPS).reshape(all_slots, model_dim)
        return mine, core_swap(mine)

    def from_experts(mine, theirs):
        both = mine + core_swap(theirs.astype(bf16)).astype(f32)
        both = both.astype(bf16).reshape(EXPERTS, CAP, model_dim)
        return exchange(both, HALF_CHIPS).reshape(all_slots, model_dim)

    units = w_gate.shape[1]
    gate_up = jnp.concatenate([w_gate, w_up], axis=1)

    def expert_hidden(rows):
        both = dot(rows, gate_up)
        gate_pre, up_pre = both[:, :units], both[:, units:]
        return gate_pre, up_pre, (jax.nn.silu(gate_pre) * up_pre).astype(bf16)

    def hidden_backward(kept, grad_rows):
        gate_pre, up_pre = kept[0], kept[1]
        grad_hidden = dot(grad_rows, w_down, NT)
        sigmoid = jax.nn.sigmoid(gate_pre)
        grad_gate = (grad_hidden * up_pre * sigmoid * (1.0 + gate_pre * (1.0 - sigmoid))).astype(bf16)
        grad_up = (grad_hidden * gate_pre * sigmoid).astype(bf16)
        return jnp.concatenate([grad_gate, grad_up], axis=1)

    def rows_backward(back):
        return dot(back, gate_up, NT)

    rows_mine, rows_theirs = to_experts(dot(placed, normed_two).astype(bf16))
    kept_mine = expert_hidden(rows_mine)
    kept_mine, rows_theirs = lax.optimization_barrier((kept_mine, rows_theirs))
    kept_theirs = expert_hidden(rows_theirs)
    returned = from_experts(dot(kept_mine[2], w_down), dot(kept_theirs[2], w_down))
    mixture = dot(token_gate_high, returned) + dot(token_gate_low, returned)
    hidden_two = hidden_one + mixture

    valid_count = valid[0]
    own_pos = first_token + core * tok_rows + jnp.arange(tok_rows, dtype=jnp.int32)
    grad_two = jnp.where(
        (own_pos < valid_count)[:, None],
        total_tokens / valid_count.astype(f32) * (hidden_two - teacher.astype(f32)),
        0.0,
    )
    grad_two_high = grad_two.astype(bf16)
    grad_two_low = (grad_two - grad_two_high.astype(f32)).astype(bf16)
    grad_slots = (slot_gate[:, :1] * (dot(placed, grad_two_high) + dot(placed, grad_two_low))).astype(bf16)
    grads_mine, grads_theirs = to_experts(grad_slots)
    back_mine = hidden_backward(kept_mine, grads_mine)
    back_mine, grads_theirs = lax.optimization_barrier((back_mine, grads_theirs))
    back_theirs = hidden_backward(kept_theirs, grads_theirs)
    grad_returned = from_experts(rows_backward(back_mine), rows_backward(back_theirs))

    expert_parts = (
        (dot(rows_mine, back_mine, TN) + dot(rows_theirs, back_theirs, TN)).astype(bf16),
        (dot(kept_mine[2], grads_mine, TN) + dot(kept_theirs[2], grads_theirs, TN)).astype(bf16),
    )
    expert_parts, grad_returned = lax.optimization_barrier((expert_parts, grad_returned))

    grad_normed_two = dot(placed_by_token, grad_returned)
    norm_two_grad, gain_two_grad = norm_backward(hidden_one, inverse_two, gain_two, grad_normed_two)
    grad_one = grad_two + norm_two_grad
    grad_branch = grad_one.astype(bf16)
    chip_branch = in_order(core, grad_branch, core_swap(grad_branch))
    left, right = chip_branch[:, :HALF_WIDTH], chip_branch[:, HALF_WIDTH:]
    grad_attn = out_project_back(place, chip_branch, out_pieces)

    def send_to_chips(partial):
        return exchange(partial.astype(bf16).reshape(chips, 2 * shard_rows, -1), CHIPS)

    gate_up_other = lax.ppermute(expert_parts[0], "xh", SWAP)
    down_other = lax.ppermute(expert_parts[1], "xh", SWAP)
    out_partial = jnp.stack([dot(attn, left, TN), dot(attn, right, TN)]).astype(bf16)
    out_partial = out_partial.reshape(planes, spots, 2 * shard_rows, -1).transpose(1, 0, 2, 3)
    out_received = exchange(out_partial, PLANE_CHIPS)

    query_lin_grad, kv_grad, own_kv_grad = attend_back(
        spot_word, low_rows, query_seq, cosine, sine, seen_kv, own_kv, attn_wide, grad_attn, log_total
    )
    query_left, query_right = query_lin_grad[:, :quarter], query_lin_grad[:, quarter:]
    pair_query_grad = lax.ppermute(jnp.where(side == 0, query_right, query_left), "z", PAIR)
    kv_grad, out_received, gate_up_other, pair_query_grad = lax.optimization_barrier(
        (kv_grad, out_received, gate_up_other, pair_query_grad)
    )
    came = exchange(kv_grad, PLANE_CHIPS)
    side_query_grad = jnp.where(side == 0, query_left, query_right)
    pair_normed_grad = dot(pair_query_grad, half_query, NT)
    pair_normed_grad = of_core(core, pair_normed_grad, True) + core_swap(of_core(core, pair_normed_grad, False))
    back_normed_grad = lax.ppermute(pair_normed_grad.astype(bf16), "z", PAIR)
    query_partial = (dot(normed_one, side_query_grad, TN) + dot(pair_normed, pair_query_grad, TN)).astype(bf16)
    side_normed_grad = dot(side_query_grad, half_query, NT)
    came, down_other, query_partial, side_normed_grad, back_normed_grad = lax.optimization_barrier(
        (came, down_other, query_partial, side_normed_grad, back_normed_grad)
    )
    came = came.astype(f32)
    from_later = jnp.sum(jnp.where((block_at > spot)[:, None, None], came, 0.0), axis=0)
    from_before = jnp.sum(jnp.where((block_at <= spot)[:, None, None], came, 0.0), axis=0)
    from_next = lax.ppermute(from_before.astype(bf16), ("xh", "xl"), [(p + 1, p) for p in range(planes - 1)])
    kv_sum = (from_later + from_next.astype(f32) + own_kv_grad.astype(f32)).astype(bf16)
    key_lin_grad = rotate(kv_sum[:, :HEAD_SIZE].astype(f32), cosine, -sine).astype(bf16)
    kv_lin_grad = jnp.concatenate([key_lin_grad, kv_sum[:, HEAD_SIZE:]], axis=1)

    normed_grad = side_normed_grad + dot(kv_lin_grad, full_kv[:, : 2 * HEAD_SIZE], NT)
    normed_grad = of_core(core, normed_grad, True) + core_swap(of_core(core, normed_grad, False))
    normed_grad = normed_grad + back_normed_grad.astype(f32)
    own_inverse = lax.rsqrt(jnp.mean(values_in * values_in, axis=-1, keepdims=True) + NORM_EPS)
    input_norm_grad, gain_one_grad = norm_backward(values_in, own_inverse, gain_one, normed_grad)
    grad_acts = grad_one + input_norm_grad

    gain_grads = jnp.concatenate([gain_one_grad, gain_two_grad]).astype(bf16)
    gain_columns = dot(gain_grads, jnp.asarray(np.eye(2, HEAD_SIZE), bf16), TN)
    kv_partial = jnp.concatenate([dot(normed_one, kv_lin_grad, TN), gain_columns], axis=1).astype(bf16)
    partial = jnp.concatenate([kv_partial, query_partial], axis=1)
    partial, gate_up_other, down_other, out_received = lax.optimization_barrier(
        (partial, gate_up_other, down_other, out_received)
    )
    received = send_to_chips(partial)
    gate_up_grad = expert_parts[0].astype(f32) + gate_up_other.astype(f32)
    expert_grads = (
        gate_up_grad[:, :units],
        gate_up_grad[:, units:],
        expert_parts[1].astype(f32) + down_other.astype(f32),
    )
    plane_sums = jnp.sum(out_received.astype(f32), axis=0).astype(bf16)
    plane_sums = plane_sums.reshape(2, 2, 2, shard_rows, -1)
    grad_w_out = 0.0
    for k in range(4):
        piece = lax.dynamic_index_in_dim(plane_sums, (lax.axis_index("xl") + k) % 2, 1, False)
        piece = lax.dynamic_index_in_dim(piece, (half + k // 2) % 2, 1, False)
        piece = lax.ppermute(
            piece,
            ("xh", "xl", "c"),
            [
                (h * 4 + l * 2 + c, c * 4 + (l ^ k % 2) * 2 + (h ^ k // 2))
                for h in range(2)
                for l in range(2)
                for c in range(2)
            ],
        )
        grad_w_out = grad_w_out + piece.astype(f32)
    grad_w_out = jnp.concatenate([grad_w_out[0], grad_w_out[1]], axis=1)
    received = received.astype(f32).reshape(chips // 2, 2, 2 * shard_rows, -1)
    sums = jnp.sum(received, axis=0)
    sums = jnp.concatenate(
        [sums[0, :, :kv_width] + sums[1, :, :kv_width], sums[0, :, kv_width:], sums[1, :, kv_width:]], axis=1
    ).reshape(2, shard_rows, -1)
    sums = exchange(sums, "c")

    def columns(begin_at, width):
        return jnp.concatenate([sums[k, :, begin_at : begin_at + width] for k in range(2)], axis=1)

    gain_sums = sums[0, :, 2 * HEAD_SIZE : 2 * HEAD_SIZE + 2] + sums[1, :, 2 * HEAD_SIZE : 2 * HEAD_SIZE + 2]
    return (
        hidden_two.astype(bf16),
        grad_acts,
        columns(kv_width, HALF_WIDTH),
        columns(0, HEAD_SIZE),
        columns(HEAD_SIZE, HEAD_SIZE),
        grad_w_out,
        gain_sums[:, 0],
        gain_sums[:, 1],
        *expert_grads,
    )


def solution(mesh):
    fine_mesh = jax.sharding.Mesh(mesh.devices.reshape(2, 2, 4, 4, 2), ALL)
    rows, vector = P(ALL, None), P(ALL)
    wide, tall = P(None, ("xl", "y", "z", "c")), P(("xl", "y", "z", "c"), None)
    return jax.shard_map(
        body,
        mesh=fine_mesh,
        in_specs=(
            rows, rows, P(), P(), rows, rows, rows, rows, rows, rows, vector, vector, wide, wide, tall,
        ),
        out_specs=(rows, rows, rows, rows, rows, rows, vector, vector, wide, wide, tall),
        check_vma=False,
    )
```

```python
import math

import jax
import jax.numpy as jnp
import numpy as np
from jax import lax
from jax.experimental import pallas as pl
from jax.experimental.pallas import tpu as pltpu
from jax.sharding import PartitionSpec as P

HEAD_SIZE = 128
GROUP = 6
HALF_WIDTH = GROUP * HEAD_SIZE
WINDOW = 4096
CAP = 24
EXPERTS = 32
FAR_BYTES = 60 * 1024 * 1024
NEAR_BYTES = 24 * 1024 * 1024

NORM_EPS = 1e-06
ROPE_BASE = 1000000.0
MASKED = -1e30
SCALE = HEAD_SIZE ** (-0.5)
SCALE_LOG2 = SCALE * math.log2(math.e)

ALL = ("xh", "xl", "y", "z", "c")
CHIPS = ("xh", "xl", "y", "z")
HALF_CHIPS = ("xl", "y", "z")
PLANE_CHIPS = ("y", "z")
SWAP = [(0, 1), (1, 0)]
PAIR = [(0, 1), (1, 0), (2, 3), (3, 2)]

f32 = jnp.float32
bf16 = jnp.bfloat16


def dot(a, b, dims=((1,), (0,))):
    return lax.dot_general(a, b, (dims, ((), ())), preferred_element_type=f32)


NT = ((1,), (1,))
TN = ((0,), (0,))


def core_swap(value):
    return lax.ppermute(value, "c", SWAP)


def exchange(value, axes):
    return lax.all_to_all(value, axes, 0, 0, tiled=True)


def of_core(core, rows, own):
    upper, lower = jnp.split(rows, 2)
    return jnp.where((core == 0) == own, upper, lower)


def doc_begin(positions, doc_starts):
    before = doc_starts[None, :] <= positions[:, None]
    return jnp.max(jnp.where(before, doc_starts[None, :], 0), axis=-1)


def rope_tables(offset):
    column = jnp.arange(HEAD_SIZE, dtype=jnp.int32)
    half = HEAD_SIZE // 2
    inv_freq = jnp.exp((column % half).astype(f32) * (-2.0 * math.log(ROPE_BASE) / HEAD_SIZE))
    angle = offset.astype(f32)[:, None] * inv_freq[None, :]
    return jnp.cos(angle), jnp.where(column[None, :] < half, -1.0, 1.0) * jnp.sin(angle)


def norm_backward(values, inverse, gain_row, incoming_grad):
    scaled = incoming_grad * gain_row
    input_grad = inverse * scaled - values * inverse * inverse * inverse * jnp.mean(
        scaled * values, axis=-1, keepdims=True
    )
    gain_grad = jnp.sum(incoming_grad * values * inverse, axis=0, keepdims=True)
    return (input_grad, gain_grad)


def block_mask(low, t, blocks, rows, key_axis):
    key_at = lax.broadcasted_iota(jnp.int32, (rows, rows), key_axis)
    allowed = key_at >= low - t * rows
    if t == blocks - 1:
        allowed = allowed & (key_at <= lax.broadcasted_iota(jnp.int32, (rows, rows), 1 - key_axis))
    return allowed


def seen_block(spot, keys_ref, own_ref, t):
    spots = keys_ref.shape[0]
    return own_ref if t == spots else keys_ref.at[lax.rem(spot + t, spots)]


def side_block(place_ref, mine_ref, theirs_ref):
    mine = pl.program_id(0) // (GROUP // 2) == place_ref[2]
    return jnp.where(mine, mine_ref[...], theirs_ref[...])


def attend_kernel(
    place_ref, low_ref, mine_ref, theirs_ref, keys_ref, own_ref, out_ref, low_out_ref, log_ref, score_ref
):
    blocks, rows = keys_ref.shape[0] + 1, mine_ref.shape[0]
    query = side_block(place_ref, mine_ref, theirs_ref)
    spot = place_ref[1]
    low = low_ref[:, 0:1]
    top = None
    for t in range(blocks):
        score = dot(query, seen_block(spot, keys_ref, own_ref, t)[:, :HEAD_SIZE], NT)
        score = jnp.where(block_mask(low, t, blocks, rows, 1), score, MASKED)
        score_ref[t] = score
        part = jnp.maximum(score[:, :HEAD_SIZE], score[:, HEAD_SIZE:])
        top = part if top is None else jnp.maximum(top, part)
    top = jnp.max(top, axis=1, keepdims=True) * SCALE_LOG2
    total = jnp.zeros((rows, HEAD_SIZE), f32)
    mixed = jnp.zeros((rows, HEAD_SIZE), f32)
    for t in range(blocks):
        weights = jnp.exp2(score_ref[t] * SCALE_LOG2 - top)
        total = total + weights[:, :HEAD_SIZE] + weights[:, HEAD_SIZE:]
        value = seen_block(spot, keys_ref, own_ref, t)[:, HEAD_SIZE:]
        mixed = mixed + dot(weights.astype(bf16), value)
    total = jnp.sum(total, axis=1, keepdims=True)
    log_ref[0] = jnp.broadcast_to(top + jnp.log2(total), (rows, HEAD_SIZE)).T[:8]
    mixed = mixed / total
    out_ref[...] = mixed
    low_out_ref[...] = mixed.astype(bf16)


def attend(place, low, mine, theirs, keys, own):
    blocks, rows = keys.shape[0] + 1, mine.shape[0]
    whole = lambda *shape: pl.BlockSpec(shape, lambda h, place: (0,) * len(shape))
    by_head = pl.BlockSpec((rows, HEAD_SIZE), lambda h, place: (0, h))
    by_half = pl.BlockSpec((rows, HEAD_SIZE), lambda h, place: (0, lax.rem(h, GROUP // 2)))
    return pl.pallas_call(
        attend_kernel,
        grid_spec=pltpu.PrefetchScalarGridSpec(
            num_scalar_prefetch=1,
            grid=(GROUP,),
            in_specs=[whole(rows, HEAD_SIZE), by_half, by_half, whole(*keys.shape), whole(*own.shape)],
            out_specs=[by_head, by_head, pl.BlockSpec((1, 8, rows), lambda h, place: (h, 0, 0))],
            scratch_shapes=[pltpu.VMEM((blocks, rows, rows), f32)],
        ),
        out_shape=[
            jax.ShapeDtypeStruct((rows, HALF_WIDTH), f32),
            jax.ShapeDtypeStruct((rows, HALF_WIDTH), bf16),
            jax.ShapeDtypeStruct((GROUP, 8, rows), f32),
        ],
        compiler_params=pltpu.CompilerParams(vmem_limit_bytes=FAR_BYTES),
        cost_estimate=pl.CostEstimate(flops=20_000_000_000, bytes_accessed=4_000_000, transcendentals=7_000_000),
        name="attend",
    )(place, low, mine, theirs, keys, own)


def pack_kernel(core_ref, key_ref, value_ref, gain_ref, query_ref, out_weight_ref, own_ref, other_ref):
    for k in range(2):
        at = slice(k * HEAD_SIZE, (k + 1) * HEAD_SIZE)
        wide = slice(k * HALF_WIDTH, (k + 1) * HALF_WIDTH)
        parts = [key_ref[:, at], value_ref[:, at], gain_ref[...], query_ref[:, wide], out_weight_ref[:, wide]]
        part = jnp.concatenate(parts, axis=1)

        @pl.when(core_ref[0] == k)
        def _(part=part):
            own_ref[...] = part

        @pl.when(core_ref[0] != k)
        def _(part=part):
            other_ref[...] = part


def unpack_kernel(core_ref, own_ref, other_ref, weights_ref, out_ref):
    rows = own_ref.shape[0]
    at = lax.broadcasted_iota(jnp.int32, (2 * rows, rows), 0) - lax.broadcasted_iota(jnp.int32, (2 * rows, rows), 1)
    place = lambda first: jnp.where(at == first, 1.0, 0.0).astype(bf16)
    core = core_ref[0]
    full = (dot(place(core * rows), own_ref[...]) + dot(place((1 - core) * rows), other_ref[...])).astype(bf16)
    kv_width, quarter = 3 * HEAD_SIZE, HALF_WIDTH // 2
    for k in range(2):
        first = kv_width + k * quarter
        part = jnp.concatenate([full[:, :kv_width], full[:, first : first + quarter]], axis=1)
        for chip in range(k, weights_ref.shape[0], 2):
            weights_ref[chip] = part
    for spot in range(out_ref.shape[0]):
        out_ref[spot] = full[:, kv_width + HALF_WIDTH :]


def place_rows_kernel(route_ref, gate_ref, placed_ref, placed_by_token_ref, token_gate_ref, slot_gate_ref):
    tokens, top = route_ref.shape
    slots = EXPERTS * CAP
    expert = lax.broadcasted_iota(jnp.int32, (tokens, HEAD_SIZE), 1)
    chosen = jnp.zeros((tokens, HEAD_SIZE), f32)
    gate = jnp.zeros((tokens, HEAD_SIZE), f32)
    for k in range(top):
        hit = route_ref[:, k : k + 1] == expert
        chosen = chosen + jnp.where(hit, 1.0, 0.0)
        gate = gate + jnp.where(hit, gate_ref[:, k : k + 1], 0.0)
    square = (tokens, tokens)
    earlier = lax.broadcasted_iota(jnp.int32, square, 1) < lax.broadcasted_iota(jnp.int32, square, 0)
    chosen = chosen.astype(bf16)
    before = dot(jnp.where(earlier, 1.0, 0.0).astype(bf16), chosen)
    first = lax.broadcasted_iota(jnp.int32, (HEAD_SIZE, slots), 0) * CAP
    slot = lax.broadcasted_iota(jnp.int32, (HEAD_SIZE, slots), 1)
    within = (slot >= first) & (slot < first + CAP)
    spread = jnp.where(within, 1.0, 0.0).astype(bf16)
    slot_in = jnp.sum(jnp.where(within, slot - first, 0).astype(f32), axis=0, keepdims=True)
    here = (dot(chosen, spread) > 0.5) & (jnp.abs(dot(before.astype(bf16), spread) - slot_in) < 0.5)
    high = gate.astype(bf16)
    low = (gate - high.astype(f32)).astype(bf16)
    high_at = jnp.where(here, dot(high, spread), 0.0)
    low_at = jnp.where(here, dot(low, spread), 0.0)
    placed = jnp.where(here, 1.0, 0.0)
    placed_by_token_ref[...] = placed.astype(bf16)
    by_slot = placed.T.astype(bf16)
    placed_ref[:, :tokens] = by_slot
    placed_ref[:, tokens:] = by_slot
    token_gate_ref[:tokens] = high_at.astype(bf16)
    token_gate_ref[tokens:] = low_at.astype(bf16)
    total = jnp.sum((high_at + low_at).T, axis=1, keepdims=True)
    slot_gate_ref[...] = jnp.broadcast_to(total, (slots, HEAD_SIZE))


def place_rows(routes, gates):
    tokens, slots = routes.shape[0], EXPERTS * CAP
    by_token = jax.ShapeDtypeStruct((tokens, slots), bf16)
    return pl.pallas_call(
        place_rows_kernel,
        out_shape=[
            jax.ShapeDtypeStruct((slots, 2 * tokens), bf16),
            by_token,
            jax.ShapeDtypeStruct((2 * tokens, slots), bf16),
            jax.ShapeDtypeStruct((slots, HEAD_SIZE), f32),
        ],
        compiler_params=pltpu.CompilerParams(vmem_limit_bytes=NEAR_BYTES),
        name="place_rows",
    )(routes, gates)


def normed_rows(values, gain_row):
    inverse = lax.rsqrt(jnp.mean(values * values, axis=-1, keepdims=True) + NORM_EPS)
    return (values * inverse * gain_row).astype(bf16)


def put_rows(target_ref, core, own, other):
    rows = own.shape[0]
    target_ref[pl.ds(pl.multiple_of(core * rows, rows), rows), :] = own
    target_ref[pl.ds(pl.multiple_of((1 - core) * rows, rows), rows), :] = other


def project_keys_kernel(
    place_ref, own_ref, other_ref, before_own_ref, before_other_ref, weight_ref,
    cosine_ref, sine_ref, before_cosine_ref, before_sine_ref,
    normed_ref, kv_ref, sent_ref, gain_ref, before_normed_ref, before_kv_ref,
):
    core, spot = place_ref[0], place_ref[1]
    pick = lax.broadcasted_iota(jnp.int32, (16, HEAD_SIZE), 0) == lax.broadcasted_iota(jnp.int32, (16, HEAD_SIZE), 1)
    gains = dot(pick.astype(bf16), weight_ref[:, 2 * HEAD_SIZE :], NT)
    gain_ref[...] = gains[:8]
    for rows_refs, tables, normed, target in (
        ((own_ref, other_ref), (cosine_ref, sine_ref), normed_ref, kv_ref),
        ((before_own_ref, before_other_ref), (before_cosine_ref, before_sine_ref), before_normed_ref, before_kv_ref),
    ):
        put_rows(normed, core, *(normed_rows(ref[...].astype(f32), gains[0:1]) for ref in rows_refs))
        linear = dot(normed[...], weight_ref[:, : 2 * HEAD_SIZE])
        key = linear[:, :HEAD_SIZE]
        turned = key * tables[0][...] + pltpu.roll(key, HEAD_SIZE // 2, 1) * tables[1][...]
        target[:, :HEAD_SIZE] = turned.astype(bf16)
        target[:, HEAD_SIZE:] = linear[:, HEAD_SIZE:].astype(bf16)
    for j in range(sent_ref.shape[0]):

        @pl.when(j > spot)
        def _(j=j):
            sent_ref[j] = kv_ref[...]

        @pl.when(j <= spot)
        def _(j=j):
            sent_ref[j] = before_kv_ref[...]


def project_keys(place, acts, before_acts, weights, cosine, sine, spots):
    rows, width = 2 * acts[0].shape[0], acts[0].shape[1]
    whole = lambda *shape: pl.BlockSpec(shape, lambda i: (0,) * len(shape))
    table = lambda k: pl.BlockSpec((rows, HEAD_SIZE), lambda i: (k, 0))
    half = whole(rows // 2, width)
    return pl.pallas_call(
        project_keys_kernel,
        grid=(1,),
        in_specs=[pl.BlockSpec(memory_space=pltpu.SMEM)]
        + [half] * 4
        + [whole(width, 3 * HEAD_SIZE), table(0), table(0), table(2), table(2)],
        out_specs=[
            whole(rows, width), whole(rows, 2 * HEAD_SIZE), whole(spots, rows, 2 * HEAD_SIZE), whole(8, width),
        ],
        out_shape=[
            jax.ShapeDtypeStruct((rows, width), bf16),
            jax.ShapeDtypeStruct((rows, 2 * HEAD_SIZE), bf16),
            jax.ShapeDtypeStruct((spots, rows, 2 * HEAD_SIZE), bf16),
            jax.ShapeDtypeStruct((8, width), f32),
        ],
        scratch_shapes=[pltpu.VMEM((rows, width), bf16), pltpu.VMEM((rows, 2 * HEAD_SIZE), bf16)],
        compiler_params=pltpu.CompilerParams(vmem_limit_bytes=FAR_BYTES),
        name="project_keys",
    )(place, *acts, *before_acts, weights, cosine, sine, cosine, sine)


def project_kernel(
    place_ref, rows_ref, own_ref, other_ref, gain_ref, weight_ref, cosine_ref, sine_ref, pair_cosine_ref, pair_sine_ref,
    normed_ref, out_ref, pair_out_ref,
):
    gain = gain_ref[0:1, :]
    put_rows(normed_ref, place_ref[0], *(normed_rows(ref[...].astype(f32), gain) for ref in (own_ref, other_ref)))
    for values_ref, cos_ref, sin_ref, target in (
        (rows_ref, cosine_ref, sine_ref, out_ref),
        (normed_ref, pair_cosine_ref, pair_sine_ref, pair_out_ref),
    ):
        linear = dot(values_ref[...], weight_ref[...])
        for h in range(GROUP // 2):
            at = slice(h * HEAD_SIZE, (h + 1) * HEAD_SIZE)
            head = linear[:, at]
            turned = head * cos_ref[...] + pltpu.roll(head, HEAD_SIZE // 2, 1) * sin_ref[...]
            target[:, at] = turned.astype(bf16)


def project(place, rows, pair_acts, gains, weights, cosine, sine):
    count, width = rows.shape
    quarter = HALF_WIDTH // 2
    whole = lambda *shape: pl.BlockSpec(shape, lambda i: (0,) * len(shape))
    table = lambda k: pl.BlockSpec((count, HEAD_SIZE), lambda i: (k, 0))
    half = whole(count // 2, width)
    shape = jax.ShapeDtypeStruct((count, quarter), bf16)
    return pl.pallas_call(
        project_kernel,
        grid=(1,),
        in_specs=[
            pl.BlockSpec(memory_space=pltpu.SMEM), whole(count, width), half, half, whole(8, width),
            pl.BlockSpec((width, quarter), lambda i: (0, 1)), table(0), table(0), table(1), table(1),
        ],
        out_specs=[whole(count, width), whole(count, quarter), whole(count, quarter)],
        out_shape=[jax.ShapeDtypeStruct(rows.shape, bf16), shape, shape],
        compiler_params=pltpu.CompilerParams(vmem_limit_bytes=FAR_BYTES),
        name="project",
    )(place, rows, *pair_acts, gains, weights, cosine, sine, cosine, sine)


def dispatch_kernel(branch_ref, came_ref, acts_ref, gain_ref, placed_ref, hidden_ref, rows_ref):
    hidden = acts_ref[...].astype(f32) + branch_ref[...] + came_ref[...]
    hidden_ref[...] = hidden
    rows_ref[...] = dot(placed_ref[:, : hidden.shape[0]], normed_rows(hidden, gain_ref[1:2, :])).astype(bf16)


def combine_kernel(
    valid_ref, scale_ref, returned_ref, token_gate_ref, hidden_ref, teacher_ref, placed_ref, gate_ref,
    out_ref, grad_ref, rows_ref,
):
    mixture = dot(token_gate_ref[...], returned_ref[...])
    tokens = hidden_ref.shape[0]
    hidden = hidden_ref[...] + mixture[:tokens] + mixture[tokens:]
    out_ref[...] = hidden.astype(bf16)
    position = valid_ref[1] + lax.broadcasted_iota(jnp.int32, hidden.shape, 0)
    grad = jnp.where(position < valid_ref[0], scale_ref[0] * (hidden - teacher_ref[...].astype(f32)), 0.0)
    grad_ref[...] = grad
    high = grad.astype(bf16)
    low = (grad - high.astype(f32)).astype(bf16)
    picked = dot(placed_ref[...], jnp.concatenate([high, low]))
    rows_ref[...] = (gate_ref[:, 0:1] * picked).astype(bf16)


def combine(bounds, scale, returned, token_gate, hidden, teacher, placed, gate):
    (slots, width), rows, steps = returned.shape, hidden.shape[0], 3
    whole = lambda shape: pl.BlockSpec(shape, lambda i: (0,) * len(shape))
    columns = lambda count: pl.BlockSpec((count, width // steps), lambda i: (0, i))
    smem = pl.BlockSpec(memory_space=pltpu.SMEM)
    return pl.pallas_call(
        combine_kernel,
        grid=(steps,),
        in_specs=[
            smem, smem, columns(slots), whole(token_gate.shape), columns(rows), columns(rows),
            whole(placed.shape), whole(gate.shape),
        ],
        out_specs=[columns(rows), columns(rows), columns(slots)],
        out_shape=[
            jax.ShapeDtypeStruct(hidden.shape, bf16),
            jax.ShapeDtypeStruct(hidden.shape, f32),
            jax.ShapeDtypeStruct(returned.shape, bf16),
        ],
        compiler_params=pltpu.CompilerParams(vmem_limit_bytes=FAR_BYTES),
        name="combine",
    )(bounds, scale, returned, token_gate, hidden, teacher, placed, gate)


def norm_back_kernel(returned_ref, placed_ref, hidden_ref, gain_ref, grad_ref, out_ref, low_out_ref, gain_grad_ref):
    hidden = hidden_ref[...]
    inverse = lax.rsqrt(jnp.mean(hidden * hidden, axis=-1, keepdims=True) + NORM_EPS)
    input_grad, gain_grad = norm_backward(
        hidden, inverse, gain_ref[1:2, :], dot(placed_ref[...], returned_ref[...])
    )
    total = grad_ref[...] + input_grad
    out_ref[...] = total
    low_out_ref[...] = total.astype(bf16)
    gain_grad_ref[...] = jnp.broadcast_to(gain_grad, gain_grad_ref.shape)


def query_columns_kernel(rows_ref, pair_rows_ref, grad_ref, pair_grad_ref, partial_ref):
    queries = dot(rows_ref[...], grad_ref[...], TN) + dot(pair_rows_ref[...], pair_grad_ref[...], TN)
    partial_ref[...] = queries.astype(bf16)


def split_grads_kernel(place_ref, came_ref, own_ref, later_ref, before_ref):
    spot = place_ref[1]
    later = own_ref[...].astype(f32)
    before = jnp.zeros_like(later)
    for j in range(came_ref.shape[0]):
        grad = came_ref[j].astype(f32)
        later = later + jnp.where(j > spot, grad, 0.0)
        before = before + jnp.where(j > spot, 0.0, grad)
    later_ref[...] = later
    before_ref[...] = before.astype(bf16)


def keys_back_kernel(
    place_ref, later_ref, next_ref, cosine_ref, sine_ref, rows_ref, weight_ref, side_ref,
    partial_ref, own_ref, other_ref, sum_ref,
):
    total = (later_ref[...] + next_ref[...].astype(f32)).astype(bf16)
    key = total[:, :HEAD_SIZE].astype(f32)
    turned = key * cosine_ref[...] - pltpu.roll(key, HEAD_SIZE // 2, 1) * sine_ref[...]
    linear = jnp.concatenate([turned.astype(bf16), total[:, HEAD_SIZE:]], axis=1)
    partial_ref[...] = dot(rows_ref[...], linear, TN).astype(bf16)
    sum_ref[...] = side_ref[...] + dot(linear, weight_ref[...], NT)
    core, rows = place_ref[0], own_ref.shape[0]
    own_ref[...] = sum_ref[pl.ds(pl.multiple_of(core * rows, rows), rows), :]
    other_ref[...] = sum_ref[pl.ds(pl.multiple_of((1 - core) * rows, rows), rows), :]


def acts_back_kernel(
    own_ref, swapped_ref, pair_ref, acts_ref, gain_ref, grad_ref, gain_grad_ref, keys_ref, queries_ref,
    out_ref, partial_ref,
):
    values = acts_ref[...].astype(f32)
    inverse = lax.rsqrt(jnp.mean(values * values, axis=-1, keepdims=True) + NORM_EPS)
    normed_grad = own_ref[...] + swapped_ref[...] + pair_ref[...].astype(f32)
    input_grad, gain_grad = norm_backward(values, inverse, gain_ref[0:1, :], normed_grad)
    out_ref[...] = grad_ref[...] + input_grad
    row = lax.broadcasted_iota(jnp.int32, (16, values.shape[1]), 0)
    gain_rows = jnp.where(row == 0, gain_grad, jnp.where(row == 1, gain_grad_ref[0:1, :], 0.0))
    square = (16, HEAD_SIZE)
    unit = lax.broadcasted_iota(jnp.int32, square, 0) == lax.broadcasted_iota(jnp.int32, square, 1)
    width = keys_ref.shape[1]
    partial_ref[:, :width] = keys_ref[...]
    partial_ref[:, width : width + HEAD_SIZE] = dot(gain_rows.astype(bf16), unit.astype(bf16), TN).astype(bf16)


def whole_call(
    kernel, name, out_shape, *args, words=0, scratch_shapes=(), blocks=(), out_blocks=(), aliases=(), near=True
):
    blocks, out_blocks = dict(blocks), dict(out_blocks)
    whole = lambda shape: pl.BlockSpec(shape, lambda i: (0,) * len(shape))
    specs = [
        pl.BlockSpec(memory_space=pltpu.SMEM) if k < words else blocks.get(k, whole(arg.shape))
        for k, arg in enumerate(args)
    ]
    return pl.pallas_call(
        kernel,
        grid=(1,),
        in_specs=specs,
        out_specs=[out_blocks.get(k, whole(out.shape)) for k, out in enumerate(out_shape)],
        out_shape=out_shape,
        input_output_aliases=dict(aliases),
        scratch_shapes=list(scratch_shapes),
        compiler_params=pltpu.CompilerParams(vmem_limit_bytes=NEAR_BYTES if near else FAR_BYTES),
        name=name,
    )(*args)


def piece_at(place_ref, k, shape):
    depth, width = shape
    row_half = lax.rem(place_ref[4] + k % 2, 2)
    column_half = lax.rem(place_ref[3] + k // 2, 2)
    return (
        pl.ds(pl.multiple_of(row_half * depth, HEAD_SIZE), depth),
        pl.ds(pl.multiple_of(column_half * width, HEAD_SIZE), width),
    )


def out_project_kernel(place_ref, attn_ref, *refs):
    pieces, (own_ref, other_ref, sum_ref) = refs[:-3], refs[-3:]
    rows = own_ref.shape[0]
    sum_ref[...] = jnp.zeros_like(sum_ref)
    for k, piece in enumerate(pieces):
        features, columns = piece_at(place_ref, k, piece.shape)
        sum_ref[:, columns] += dot(attn_ref[:, features], piece[...])
    core = place_ref[0]
    own_ref[...] = sum_ref[pl.ds(pl.multiple_of(core * rows, rows), rows), :]
    other_ref[...] = sum_ref[pl.ds(pl.multiple_of((1 - core) * rows, rows), rows), :]


def out_project(place, attn, pieces):
    rows, width = attn.shape[0], 2 * pieces[0].shape[1]
    shape = jax.ShapeDtypeStruct((rows // 2, width), f32)
    vmem = pl.BlockSpec(memory_space=pltpu.VMEM)
    return pl.pallas_call(
        out_project_kernel,
        in_specs=[pl.BlockSpec(memory_space=pltpu.SMEM)] + [vmem] * (1 + len(pieces)),
        out_specs=[vmem, vmem],
        out_shape=[shape, shape],
        scratch_shapes=[pltpu.VMEM((rows, width), f32)],
        compiler_params=pltpu.CompilerParams(vmem_limit_bytes=NEAR_BYTES),
        name="out_project",
    )(place, attn, *pieces)


def out_project_back_kernel(place_ref, own_ref, other_ref, attn_ref, *refs):
    pieces, (out_ref, partial_ref, grad_ref, sum_ref) = refs[:-4], refs[-4:]
    put_rows(grad_ref, place_ref[0], own_ref[...], other_ref[...])
    sum_ref[...] = jnp.zeros_like(sum_ref)
    for k, piece in enumerate(pieces):
        features, columns = piece_at(place_ref, k, piece.shape)
        sum_ref[:, features] += dot(grad_ref[:, columns], piece[...], NT)
    out_ref[...] = sum_ref[...].astype(bf16)
    spots, planes, rows, width = partial_ref.shape
    for h in range(2):
        partial = dot(attn_ref[...], grad_ref[:, h * width : (h + 1) * width], TN)
        for l in range(planes // 2):
            for j in range(spots):
                first = (l * spots + j) * rows
                partial_ref[j, h * (planes // 2) + l] = partial[first : first + rows].astype(bf16)


def out_project_back(place, own, other, attn, pieces, spots):
    rows, width = attn.shape
    vmem = pl.BlockSpec(memory_space=pltpu.VMEM)
    return pl.pallas_call(
        out_project_back_kernel,
        in_specs=[pl.BlockSpec(memory_space=pltpu.SMEM)] + [vmem] * (3 + len(pieces)),
        out_specs=[vmem, vmem],
        out_shape=[
            jax.ShapeDtypeStruct((rows, width), bf16),
            jax.ShapeDtypeStruct((spots, 4, width // (2 * spots), width), bf16),
        ],
        scratch_shapes=[pltpu.VMEM((rows, 2 * width), bf16), pltpu.VMEM((rows, width), f32)],
        compiler_params=pltpu.CompilerParams(vmem_limit_bytes=FAR_BYTES),
        name="out_project_back",
    )(place, own, other, attn, *pieces)


def attend_back_kernel(
    place_ref, low_ref, mine_ref, theirs_ref, cosine_ref, sine_ref, keys_ref, own_ref, out_ref, grad_ref, log_ref,
    query_grad_ref, keys_grad_ref, own_grad_ref, sum_ref, turned_key_ref, weight_ref, score_ref,
):
    h, heads = pl.program_id(0), pl.num_programs(0)
    blocks, rows = keys_ref.shape[0] + 1, mine_ref.shape[0]
    spot = place_ref[1]

    @pl.when(h == 0)
    def _():
        sum_ref[...] = jnp.zeros_like(sum_ref)
        for t in range(blocks):
            turned_key_ref[t] = seen_block(spot, keys_ref, own_ref, t)[:, :HEAD_SIZE].T

    query, out_grad = side_block(place_ref, mine_ref, theirs_ref), grad_ref[...]
    delta = jnp.sum((out_grad.astype(f32) * out_ref[...]).T, axis=0, keepdims=True)
    log_total, low = log_ref[0, 0:1, :], low_ref[0:1, :]
    for t in range(blocks):
        block = seen_block(spot, keys_ref, own_ref, t)
        key, value = block[:, :HEAD_SIZE], block[:, HEAD_SIZE:]
        weights = jnp.exp2(dot(key, query, NT) * SCALE_LOG2 - log_total)
        weights = jnp.where(block_mask(low, t, blocks, rows, 0), weights, 0.0)
        weight_ref[t] = weights.astype(bf16)
        score_ref[t] = (weights * (dot(value, out_grad, NT) - delta)).astype(bf16)
    query_grad = jnp.zeros((HEAD_SIZE, rows), f32)
    for t in range(blocks):
        query_grad = query_grad + dot(turned_key_ref[t], score_ref[t])
    query_grad = (query_grad * SCALE).T.astype(bf16).astype(f32)
    turned = query_grad * cosine_ref[...] - pltpu.roll(query_grad, HEAD_SIZE // 2, 1) * sine_ref[...]
    query_grad_ref[...] = turned.astype(bf16)
    for t in range(blocks):
        sum_ref[t, :, :HEAD_SIZE] += dot(score_ref[t], query)
        sum_ref[t, :, HEAD_SIZE:] += dot(weight_ref[t], out_grad)

    @pl.when(h == heads - 1)
    def _():
        for t in range(blocks):
            target = seen_block(spot, keys_grad_ref, own_grad_ref, t)
            target[:, :HEAD_SIZE] = (sum_ref[t, :, :HEAD_SIZE] * SCALE).astype(bf16)
            target[:, HEAD_SIZE:] = sum_ref[t, :, HEAD_SIZE:].astype(bf16)


def attend_back(place, low, mine, theirs, cosine, sine, keys, own, out, out_grad, log_total):
    blocks, rows = keys.shape[0] + 1, mine.shape[0]
    whole = lambda *shape: pl.BlockSpec(shape, lambda h, place: (0,) * len(shape))
    by_head = pl.BlockSpec((rows, HEAD_SIZE), lambda h, place: (0, h))
    by_half = pl.BlockSpec((rows, HEAD_SIZE), lambda h, place: (0, lax.rem(h, GROUP // 2)))
    table = pl.BlockSpec((rows, HEAD_SIZE), lambda h, place: (0, 0))
    return pl.pallas_call(
        attend_back_kernel,
        grid_spec=pltpu.PrefetchScalarGridSpec(
            num_scalar_prefetch=1,
            grid=(GROUP,),
            in_specs=[
                whole(8, rows), by_half, by_half, table, table, whole(*keys.shape), whole(*own.shape), by_head, by_head,
                pl.BlockSpec((1, 8, rows), lambda h, place: (h, 0, 0)),
            ],
            out_specs=[by_head, whole(*keys.shape), whole(*own.shape)],
            scratch_shapes=[
                pltpu.VMEM((blocks, rows, 2 * HEAD_SIZE), f32),
                pltpu.VMEM((blocks, HEAD_SIZE, rows), bf16),
                pltpu.VMEM((blocks, rows, rows), bf16),
                pltpu.VMEM((blocks, rows, rows), bf16),
            ],
        ),
        out_shape=[
            jax.ShapeDtypeStruct((rows, HALF_WIDTH), bf16),
            jax.ShapeDtypeStruct(keys.shape, bf16),
            jax.ShapeDtypeStruct(own.shape, bf16),
        ],
        compiler_params=pltpu.CompilerParams(vmem_limit_bytes=FAR_BYTES),
        cost_estimate=pl.CostEstimate(flops=28_000_000_000, bytes_accessed=8_000_000, transcendentals=7_000_000),
        name="attend_back",
    )(place, low, mine, theirs, cosine, sine, keys, own, out, out_grad, log_total)


def body(
    acts, teacher, valid, doc_starts, routes, gates,
    w_query, key_weight, value_weight, w_out, gain_attn, gain_ffn, w_gate, w_up, w_down,
):
    half, core = lax.axis_index("xh"), lax.axis_index("c")
    plane, spot = lax.axis_index(("xh", "xl")), lax.axis_index(PLANE_CHIPS)
    chip = lax.axis_index(CHIPS)
    tok_rows, model_dim = acts.shape
    chip_rows = 2 * tok_rows
    spots = lax.axis_size(PLANE_CHIPS)
    planes = lax.axis_size(("xh", "xl"))
    chips = spots * planes
    total_tokens = chips * chip_rows
    shard_rows = w_query.shape[0]

    side = chip % 2
    place = jnp.stack([core, spot, side, half, lax.axis_index("xl")]).astype(jnp.int32)
    gain_pair = jnp.pad(jnp.stack([gain_attn, gain_ffn], axis=1), ((0, 0), (0, HEAD_SIZE - 2)))
    kv_width = 3 * HEAD_SIZE
    quarter = HALF_WIDTH // 2
    core_word = core.astype(jnp.int32).reshape(1)
    packed = jax.ShapeDtypeStruct((shard_rows, kv_width + 2 * HALF_WIDTH), bf16)
    own_part, other_part = whole_call(
        pack_kernel, "pack", [packed, packed], core_word, key_weight, value_weight, gain_pair, w_query, w_out, words=1
    )
    weights_sent, out_sent = whole_call(
        unpack_kernel, "unpack",
        [
            jax.ShapeDtypeStruct((chips, 2 * shard_rows, kv_width + quarter), bf16),
            jax.ShapeDtypeStruct((spots, 2 * shard_rows, HALF_WIDTH), bf16),
        ],
        core_word, own_part, core_swap(other_part), words=1,
    )
    weights = exchange(weights_sent, CHIPS)

    first_token = chip * chip_rows
    chip_pos = first_token + jnp.arange(chip_rows, dtype=jnp.int32)
    begin = doc_begin(chip_pos, doc_starts)
    table_pos = jnp.concatenate([chip_pos, chip_pos + (1 - 2 * side) * chip_rows, chip_pos - spots * chip_rows])
    cosine, sine = rope_tables(table_pos - doc_begin(table_pos, doc_starts))
    low = jnp.maximum(begin, chip_pos - (WINDOW - 1)) - (first_token - WINDOW)
    low_rows = jnp.broadcast_to(low[None, :], (8, chip_rows))
    low_columns = jnp.broadcast_to(low[:, None], (chip_rows, HEAD_SIZE))
    block_at = jnp.arange(spots, dtype=jnp.int32)

    own_acts, cosine, sine, low_columns, out_sent = lax.optimization_barrier((acts, cosine, sine, low_columns, out_sent))
    chip_acts = (own_acts, core_swap(acts))
    pair_acts = lax.ppermute(own_acts, "z", PAIR)
    pair_acts = (pair_acts, core_swap(pair_acts))
    before_acts = lax.ppermute(own_acts, ("xh", "xl"), [(p, p + 1) for p in range(planes - 1)])
    before_acts = (before_acts, core_swap(before_acts))

    weights, out_sent, chip_acts, pair_acts, before_acts, low_columns, cosine, sine = lax.optimization_barrier(
        (weights, out_sent, chip_acts, pair_acts, before_acts, low_columns, cosine, sine)
    )
    out_rows = exchange(out_sent, PLANE_CHIPS)
    weights = weights.reshape(model_dim, -1)

    normed_one, own_kv, kv_sent, gain_rows = project_keys(
        place, chip_acts, before_acts, weights, cosine, sine, spots
    )
    kv_sent, out_rows = lax.optimization_barrier((kv_sent, out_rows))
    seen_kv = exchange(kv_sent, PLANE_CHIPS)
    placed, placed_by_token, token_gate, slot_gate = place_rows(routes, gates)
    all_slots = EXPERTS * CAP

    out_rows = out_rows.reshape(-1, HALF_WIDTH)
    out_pieces = [
        lax.ppermute(
            out_rows,
            ("xh", "xl", "c"),
            [
                (c * 4 + (l ^ k % 2) * 2 + (h ^ k // 2), h * 4 + l * 2 + c)
                for h in range(2)
                for l in range(2)
                for c in range(2)
            ],
        )
        for k in range(4)
    ]
    seen_kv, out_pieces = lax.optimization_barrier((seen_kv, out_pieces))

    pair_normed, query_mine, query_theirs = project(
        place, normed_one, pair_acts, gain_rows, weights, cosine, sine
    )
    query_theirs = lax.ppermute(query_theirs, "z", PAIR)
    query_theirs, placed, slot_gate, token_gate, placed_by_token = lax.optimization_barrier(
        (query_theirs, placed, slot_gate, token_gate, placed_by_token)
    )
    attn_wide, attn, log_total = attend(place, low_columns, query_mine, query_theirs, seen_kv, own_kv)

    branch, other_branch = out_project(place, attn, out_pieces)
    wide = jax.ShapeDtypeStruct((tok_rows, model_dim), f32)
    slim = jax.ShapeDtypeStruct((tok_rows, model_dim), bf16)
    slot_rows = jax.ShapeDtypeStruct((all_slots, model_dim), bf16)
    hidden_one, sent_rows = whole_call(
        dispatch_kernel, "dispatch", [wide, slot_rows], branch, core_swap(other_branch), acts, gain_rows, placed
    )

    def to_experts(rows):
        mine = exchange(rows.reshape(EXPERTS, CAP, model_dim), HALF_CHIPS).reshape(all_slots, model_dim)
        return mine, core_swap(mine)

    def from_experts(mine, theirs):
        both = mine + core_swap(theirs.astype(bf16)).astype(f32)
        both = both.astype(bf16).reshape(EXPERTS, CAP, model_dim)
        return exchange(both, HALF_CHIPS).reshape(all_slots, model_dim)

    units = w_gate.shape[1]
    gate_up = jnp.concatenate([w_gate, w_up], axis=1)

    def expert_hidden(rows):
        both = dot(rows, gate_up)
        gate_pre, up_pre = both[:, :units], both[:, units:]
        return gate_pre, up_pre, (jax.nn.silu(gate_pre) * up_pre).astype(bf16)

    def hidden_backward(kept, grad_rows):
        gate_pre, up_pre = kept[0], kept[1]
        grad_hidden = dot(grad_rows, w_down, NT)
        sigmoid = jax.nn.sigmoid(gate_pre)
        grad_gate = (grad_hidden * up_pre * sigmoid * (1.0 + gate_pre * (1.0 - sigmoid))).astype(bf16)
        grad_up = (grad_hidden * gate_pre * sigmoid).astype(bf16)
        return jnp.concatenate([grad_gate, grad_up], axis=1)

    def rows_backward(back):
        return dot(back, gate_up, NT)

    rows_mine, rows_theirs = to_experts(sent_rows)
    kept_mine = expert_hidden(rows_mine)
    kept_mine, rows_theirs = lax.optimization_barrier((kept_mine, rows_theirs))
    kept_theirs = expert_hidden(rows_theirs)
    returned = from_experts(dot(kept_mine[2], w_down), dot(kept_theirs[2], w_down))
    bounds = jnp.stack([valid[0], first_token + core * tok_rows]).astype(jnp.int32)
    loss_scale = (total_tokens / valid.astype(f32)).reshape(1)
    activations, grad_two, grad_slots = combine(
        bounds, loss_scale, returned, token_gate, hidden_one, teacher, placed, slot_gate
    )
    grads_mine, grads_theirs = to_experts(grad_slots)
    back_mine = hidden_backward(kept_mine, grads_mine)
    back_mine, grads_theirs = lax.optimization_barrier((back_mine, grads_theirs))
    back_theirs = hidden_backward(kept_theirs, grads_theirs)
    grad_returned = from_experts(rows_backward(back_mine), rows_backward(back_theirs))

    expert_parts = (
        (dot(rows_mine, back_mine, TN) + dot(rows_theirs, back_theirs, TN)).astype(bf16),
        (dot(kept_mine[2], grads_mine, TN) + dot(kept_theirs[2], grads_theirs, TN)).astype(bf16),
    )
    expert_part = jnp.concatenate(
        [expert_parts[0], expert_parts[1][:, :HALF_WIDTH], expert_parts[1][:, HALF_WIDTH:]]
    )

    expert_part, grad_returned = lax.optimization_barrier((expert_part, grad_returned))
    grad_one, grad_branch, gain_two_grad = whole_call(
        norm_back_kernel, "norm_back", [wide, slim, jax.ShapeDtypeStruct((8, model_dim), f32)],
        grad_returned, placed_by_token, hidden_one, gain_rows, grad_two, near=False,
    )
    grad_attn, out_partial = out_project_back(place, grad_branch, core_swap(grad_branch), attn, out_pieces, spots)

    def send_to_chips(partial):
        return exchange(partial.astype(bf16).reshape(chips, 2 * shard_rows, -1), CHIPS)

    expert_other = lax.ppermute(expert_part, "xh", SWAP)
    out_received = exchange(out_partial, PLANE_CHIPS)

    query_lin_grad, kv_grad, own_kv_grad = attend_back(
        place, low_rows, query_mine, query_theirs, cosine, sine, seen_kv, own_kv, attn_wide, grad_attn, log_total
    )
    query_left, query_right = query_lin_grad[:, :quarter], query_lin_grad[:, quarter:]
    pair_query_grad = lax.ppermute(jnp.where(side == 0, query_right, query_left), "z", PAIR)
    kv_grad, out_received = lax.optimization_barrier((kv_grad, out_received))
    came = exchange(kv_grad, PLANE_CHIPS)
    side_query_grad = jnp.where(side == 0, query_left, query_right)
    pair_normed_grad = dot(pair_query_grad, weights[:, kv_width:], NT)
    pair_normed_grad = of_core(core, pair_normed_grad, True) + core_swap(of_core(core, pair_normed_grad, False))
    back_normed_grad = lax.ppermute(pair_normed_grad.astype(bf16), "z", PAIR)
    side_normed_grad = dot(side_query_grad, weights[:, kv_width:], NT)
    came, expert_other, side_query_grad, pair_query_grad = lax.optimization_barrier(
        (came, expert_other, side_query_grad, pair_query_grad)
    )
    square = (chip_rows, 2 * HEAD_SIZE)
    later_grad, before_grad = whole_call(
        split_grads_kernel, "split_grads", [jax.ShapeDtypeStruct(square, f32), jax.ShapeDtypeStruct(square, bf16)],
        place, came, own_kv_grad, words=1,
    )
    next_grad = lax.ppermute(before_grad, ("xh", "xl"), [(p + 1, p) for p in range(planes - 1)])
    (partial,) = whole_call(
        query_columns_kernel, "query_columns", [jax.ShapeDtypeStruct((model_dim, 2 * quarter), bf16)],
        normed_one, pair_normed, side_query_grad, pair_query_grad,
        out_blocks={0: pl.BlockSpec((model_dim, quarter), lambda i: (0, 1))}, near=False,
    )
    next_grad, back_normed_grad, partial = lax.optimization_barrier((next_grad, back_normed_grad, partial))
    table = pl.BlockSpec((chip_rows, HEAD_SIZE), lambda i: (0, 0))
    kv_partial, normed_grad, other_normed_grad = whole_call(
        keys_back_kernel, "keys_back", [jax.ShapeDtypeStruct((model_dim, 2 * HEAD_SIZE), bf16), wide, wide],
        place, later_grad, next_grad, cosine, sine, normed_one, weights, side_normed_grad, words=1,
        blocks={3: table, 4: table, 6: pl.BlockSpec((model_dim, 2 * HEAD_SIZE), lambda i: (0, 0))},
        scratch_shapes=[pltpu.VMEM((chip_rows, model_dim), f32)],
    )
    grad_acts, partial = whole_call(
        acts_back_kernel, "acts_back", [wide, jax.ShapeDtypeStruct(partial.shape, bf16)],
        normed_grad, core_swap(other_normed_grad), back_normed_grad, acts, gain_rows, grad_one, gain_two_grad,
        kv_partial, partial, near=False, blocks={8: pl.BlockSpec((16, HEAD_SIZE), lambda i: (0, 0))},
        out_blocks={1: pl.BlockSpec((model_dim, kv_width), lambda i: (0, 0))}, aliases={8: 1},
    )
    partial, expert_other, out_received = lax.optimization_barrier((partial, expert_other, out_received))
    received = send_to_chips(partial)
    expert_grad = expert_part.astype(f32) + expert_other.astype(f32)
    expert_grads = (
        expert_grad[:model_dim, :units],
        expert_grad[:model_dim, units:],
        jnp.concatenate([expert_grad[model_dim : model_dim + units], expert_grad[model_dim + units :]], axis=1),
    )
    plane_sums = jnp.sum(out_received.astype(f32), axis=0).astype(bf16)
    plane_sums = plane_sums.reshape(2, 2, 2, shard_rows, -1)
    grad_w_out = 0.0
    for k in range(4):
        piece = lax.dynamic_index_in_dim(plane_sums, (lax.axis_index("xl") + k) % 2, 1, False)
        piece = lax.dynamic_index_in_dim(piece, (half + k // 2) % 2, 1, False)
        piece = lax.ppermute(
            piece,
            ("xh", "xl", "c"),
            [
                (h * 4 + l * 2 + c, c * 4 + (l ^ k % 2) * 2 + (h ^ k // 2))
                for h in range(2)
                for l in range(2)
                for c in range(2)
            ],
        )
        grad_w_out = grad_w_out + piece.astype(f32)
    grad_w_out = jnp.concatenate([grad_w_out[0], grad_w_out[1]], axis=1)
    received = received.astype(f32).reshape(chips // 2, 2, 2 * shard_rows, -1)
    sums = jnp.sum(received, axis=0)
    sums = jnp.concatenate(
        [sums[0, :, :kv_width] + sums[1, :, :kv_width], sums[0, :, kv_width:], sums[1, :, kv_width:]], axis=1
    ).reshape(2, shard_rows, -1)
    given = core_swap(jnp.where(core == 0, sums[1], sums[0]))
    kept = jnp.where(core == 0, sums[0], sums[1])
    sums = (jnp.where(core == 0, kept, given), jnp.where(core == 0, given, kept))

    def columns(begin_at, width):
        return jnp.concatenate([part[:, begin_at : begin_at + width] for part in sums], axis=1)

    gain_sums = sums[0][:, 2 * HEAD_SIZE : 2 * HEAD_SIZE + 2] + sums[1][:, 2 * HEAD_SIZE : 2 * HEAD_SIZE + 2]
    return (
        activations,
        grad_acts,
        columns(kv_width, HALF_WIDTH),
        columns(0, HEAD_SIZE),
        columns(HEAD_SIZE, HEAD_SIZE),
        grad_w_out,
        gain_sums[:, 0],
        gain_sums[:, 1],
        *expert_grads,
    )


def solution(mesh):
    fine_mesh = jax.sharding.Mesh(mesh.devices.reshape(2, 2, 4, 4, 2), ALL)
    rows, vector = P(ALL, None), P(ALL)
    wide, tall = P(None, ("xl", "y", "z", "c")), P(("xl", "y", "z", "c"), None)
    return jax.shard_map(
        body,
        mesh=fine_mesh,
        in_specs=(
            rows, rows, P(), P(), rows, rows, rows, rows, rows, rows, vector, vector, wide, wide, tall,
        ),
        out_specs=(rows, rows, rows, rows, rows, rows, vector, vector, wide, wide, tall),
        check_vma=False,
    )
```

```python
import math

import jax
import jax.numpy as jnp
import numpy as np
from jax import lax
from jax.experimental import pallas as pl
from jax.experimental.pallas import tpu as pltpu
from jax.sharding import PartitionSpec as P

HEAD_SIZE = 128
GROUP = 6
HALF_WIDTH = GROUP * HEAD_SIZE
WINDOW = 4096
CAP = 24
EXPERTS = 32
FAR_BYTES = 60 * 1024 * 1024
NEAR_BYTES = 24 * 1024 * 1024

NORM_EPS = 1e-06
ROPE_BASE = 1000000.0
MASKED = -1e30
SCALE = HEAD_SIZE ** (-0.5)
SCALE_LOG2 = SCALE * math.log2(math.e)

ALL = ("xh", "xl", "y", "z", "c")
CHIPS = ("xh", "xl", "y", "z")
HALF_CHIPS = ("xl", "y", "z")
PLANE_CHIPS = ("y", "z")
SWAP = [(0, 1), (1, 0)]
PAIR = [(0, 1), (1, 0), (2, 3), (3, 2)]

f32 = jnp.float32
bf16 = jnp.bfloat16


def dot(a, b, dims=((1,), (0,))):
    return lax.dot_general(a, b, (dims, ((), ())), preferred_element_type=f32)


NT = ((1,), (1,))
TN = ((0,), (0,))


def core_swap(value):
    return lax.ppermute(value, "c", SWAP)


def exchange(value, axes):
    return lax.all_to_all(value, axes, 0, 0, tiled=True)


def of_core(core, rows, own):
    upper, lower = jnp.split(rows, 2)
    return jnp.where((core == 0) == own, upper, lower)


def doc_begin(positions, doc_starts):
    before = doc_starts[None, :] <= positions[:, None]
    return jnp.max(jnp.where(before, doc_starts[None, :], 0), axis=-1)


def rope_tables(offset):
    column = jnp.arange(HEAD_SIZE, dtype=jnp.int32)
    half = HEAD_SIZE // 2
    inv_freq = jnp.exp((column % half).astype(f32) * (-2.0 * math.log(ROPE_BASE) / HEAD_SIZE))
    angle = offset.astype(f32)[:, None] * inv_freq[None, :]
    return jnp.cos(angle), jnp.where(column[None, :] < half, -1.0, 1.0) * jnp.sin(angle)


def norm_backward(values, inverse, gain_row, incoming_grad):
    scaled = incoming_grad * gain_row
    input_grad = inverse * scaled - values * inverse * inverse * inverse * jnp.mean(
        scaled * values, axis=-1, keepdims=True
    )
    gain_grad = jnp.sum(incoming_grad * values * inverse, axis=0, keepdims=True)
    return (input_grad, gain_grad)


def block_mask(low, t, blocks, rows, key_axis):
    key_at = lax.broadcasted_iota(jnp.int32, (rows, rows), key_axis)
    allowed = key_at >= low - t * rows
    if t == blocks - 1:
        allowed = allowed & (key_at <= lax.broadcasted_iota(jnp.int32, (rows, rows), 1 - key_axis))
    return allowed


def seen_block(spot, keys_ref, own_ref, t):
    spots = keys_ref.shape[0]
    return own_ref if t == spots else keys_ref.at[lax.rem(spot + t, spots)]


def side_block(place_ref, mine_ref, theirs_ref):
    mine = pl.program_id(0) // (GROUP // 2) == place_ref[2]
    return jnp.where(mine, mine_ref[...], theirs_ref[...])


def attend_kernel(
    place_ref, low_ref, mine_ref, theirs_ref, keys_ref, own_ref, out_ref, low_out_ref, log_ref, score_ref
):
    blocks, rows = keys_ref.shape[0] + 1, mine_ref.shape[0]
    query = side_block(place_ref, mine_ref, theirs_ref)
    spot = place_ref[1]
    low = low_ref[:, 0:1]
    top = None
    for t in range(blocks):
        score = dot(query, seen_block(spot, keys_ref, own_ref, t)[:, :HEAD_SIZE], NT)
        score = jnp.where(block_mask(low, t, blocks, rows, 1), score, MASKED)
        score_ref[t] = score
        part = jnp.maximum(score[:, :HEAD_SIZE], score[:, HEAD_SIZE:])
        top = part if top is None else jnp.maximum(top, part)
    top = jnp.max(top, axis=1, keepdims=True) * SCALE_LOG2
    total = jnp.zeros((rows, HEAD_SIZE), f32)
    mixed = jnp.zeros((rows, HEAD_SIZE), f32)
    for t in range(blocks):
        weights = jnp.exp2(score_ref[t] * SCALE_LOG2 - top)
        total = total + weights[:, :HEAD_SIZE] + weights[:, HEAD_SIZE:]
        value = seen_block(spot, keys_ref, own_ref, t)[:, HEAD_SIZE:]
        mixed = mixed + dot(weights.astype(bf16), value)
    total = jnp.sum(total, axis=1, keepdims=True)
    log_ref[0] = jnp.broadcast_to(top + jnp.log2(total), (rows, HEAD_SIZE)).T[:8]
    mixed = mixed / total
    out_ref[...] = mixed
    low_out_ref[...] = mixed.astype(bf16)


def attend(place, low, mine, theirs, keys, own):
    blocks, rows = keys.shape[0] + 1, mine.shape[0]
    whole = lambda *shape: pl.BlockSpec(shape, lambda h, place: (0,) * len(shape))
    by_head = pl.BlockSpec((rows, HEAD_SIZE), lambda h, place: (0, h))
    by_half = pl.BlockSpec((rows, HEAD_SIZE), lambda h, place: (0, lax.rem(h, GROUP // 2)))
    return pl.pallas_call(
        attend_kernel,
        grid_spec=pltpu.PrefetchScalarGridSpec(
            num_scalar_prefetch=1,
            grid=(GROUP,),
            in_specs=[whole(rows, HEAD_SIZE), by_half, by_half, whole(*keys.shape), whole(*own.shape)],
            out_specs=[by_head, by_head, pl.BlockSpec((1, 8, rows), lambda h, place: (h, 0, 0))],
            scratch_shapes=[pltpu.VMEM((blocks, rows, rows), f32)],
        ),
        out_shape=[
            jax.ShapeDtypeStruct((rows, HALF_WIDTH), f32),
            jax.ShapeDtypeStruct((rows, HALF_WIDTH), bf16),
            jax.ShapeDtypeStruct((GROUP, 8, rows), f32),
        ],
        compiler_params=pltpu.CompilerParams(vmem_limit_bytes=FAR_BYTES),
        cost_estimate=pl.CostEstimate(flops=20_000_000_000, bytes_accessed=4_000_000, transcendentals=7_000_000),
        name="attend",
    )(place, low, mine, theirs, keys, own)


def pack_kernel(core_ref, key_ref, value_ref, gain_ref, query_ref, out_weight_ref, own_ref, other_ref):
    for k in range(2):
        at = slice(k * HEAD_SIZE, (k + 1) * HEAD_SIZE)
        wide = slice(k * HALF_WIDTH, (k + 1) * HALF_WIDTH)
        parts = [key_ref[:, at], value_ref[:, at], gain_ref[...], query_ref[:, wide], out_weight_ref[:, wide]]
        part = jnp.concatenate(parts, axis=1)

        @pl.when(core_ref[0] == k)
        def _(part=part):
            own_ref[...] = part

        @pl.when(core_ref[0] != k)
        def _(part=part):
            other_ref[...] = part


def unpack_kernel(core_ref, own_ref, other_ref, weights_ref, out_ref):
    rows = own_ref.shape[0]
    at = lax.broadcasted_iota(jnp.int32, (2 * rows, rows), 0) - lax.broadcasted_iota(jnp.int32, (2 * rows, rows), 1)
    place = lambda first: jnp.where(at == first, 1.0, 0.0).astype(bf16)
    core = core_ref[0]
    full = (dot(place(core * rows), own_ref[...]) + dot(place((1 - core) * rows), other_ref[...])).astype(bf16)
    kv_width, quarter = 3 * HEAD_SIZE, HALF_WIDTH // 2
    for k in range(2):
        first = kv_width + k * quarter
        part = jnp.concatenate([full[:, :kv_width], full[:, first : first + quarter]], axis=1)
        for chip in range(k, weights_ref.shape[0], 2):
            weights_ref[chip] = part
    for spot in range(out_ref.shape[0]):
        out_ref[spot] = full[:, kv_width + HALF_WIDTH :]


def place_rows_kernel(route_ref, gate_ref, placed_ref, placed_by_token_ref, token_gate_ref, slot_gate_ref):
    tokens, top = route_ref.shape
    slots = EXPERTS * CAP
    expert = lax.broadcasted_iota(jnp.int32, (tokens, HEAD_SIZE), 1)
    chosen = jnp.zeros((tokens, HEAD_SIZE), f32)
    gate = jnp.zeros((tokens, HEAD_SIZE), f32)
    for k in range(top):
        hit = route_ref[:, k : k + 1] == expert
        chosen = chosen + jnp.where(hit, 1.0, 0.0)
        gate = gate + jnp.where(hit, gate_ref[:, k : k + 1], 0.0)
    square = (tokens, tokens)
    earlier = lax.broadcasted_iota(jnp.int32, square, 1) < lax.broadcasted_iota(jnp.int32, square, 0)
    chosen = chosen.astype(bf16)
    before = dot(jnp.where(earlier, 1.0, 0.0).astype(bf16), chosen)
    first = lax.broadcasted_iota(jnp.int32, (HEAD_SIZE, slots), 0) * CAP
    slot = lax.broadcasted_iota(jnp.int32, (HEAD_SIZE, slots), 1)
    within = (slot >= first) & (slot < first + CAP)
    spread = jnp.where(within, 1.0, 0.0).astype(bf16)
    slot_in = jnp.sum(jnp.where(within, slot - first, 0).astype(f32), axis=0, keepdims=True)
    here = (dot(chosen, spread) > 0.5) & (jnp.abs(dot(before.astype(bf16), spread) - slot_in) < 0.5)
    high = gate.astype(bf16)
    low = (gate - high.astype(f32)).astype(bf16)
    high_at = jnp.where(here, dot(high, spread), 0.0)
    low_at = jnp.where(here, dot(low, spread), 0.0)
    placed = jnp.where(here, 1.0, 0.0)
    placed_by_token_ref[...] = placed.astype(bf16)
    by_slot = placed.T.astype(bf16)
    placed_ref[:, :tokens] = by_slot
    placed_ref[:, tokens:] = by_slot
    token_gate_ref[:tokens] = high_at.astype(bf16)
    token_gate_ref[tokens:] = low_at.astype(bf16)
    total = jnp.sum((high_at + low_at).T, axis=1, keepdims=True)
    slot_gate_ref[...] = jnp.broadcast_to(total, (slots, HEAD_SIZE))


def place_rows(routes, gates):
    tokens, slots = routes.shape[0], EXPERTS * CAP
    by_token = jax.ShapeDtypeStruct((tokens, slots), bf16)
    return pl.pallas_call(
        place_rows_kernel,
        out_shape=[
            jax.ShapeDtypeStruct((slots, 2 * tokens), bf16),
            by_token,
            jax.ShapeDtypeStruct((2 * tokens, slots), bf16),
            jax.ShapeDtypeStruct((slots, HEAD_SIZE), f32),
        ],
        compiler_params=pltpu.CompilerParams(vmem_limit_bytes=NEAR_BYTES),
        name="place_rows",
    )(routes, gates)


def normed_rows(values, gain_row):
    inverse = lax.rsqrt(jnp.mean(values * values, axis=-1, keepdims=True) + NORM_EPS)
    return (values * inverse * gain_row).astype(bf16)


def put_rows(target_ref, core, own, other):
    rows = own.shape[0]
    target_ref[pl.ds(pl.multiple_of(core * rows, rows), rows), :] = own
    target_ref[pl.ds(pl.multiple_of((1 - core) * rows, rows), rows), :] = other


def project_keys_kernel(
    place_ref, own_ref, other_ref, before_own_ref, before_other_ref, weight_ref,
    cosine_ref, sine_ref, before_cosine_ref, before_sine_ref,
    normed_ref, kv_ref, sent_ref, gain_ref, before_normed_ref, before_kv_ref,
):
    core, spot = place_ref[0], place_ref[1]
    pick = lax.broadcasted_iota(jnp.int32, (16, HEAD_SIZE), 0) == lax.broadcasted_iota(jnp.int32, (16, HEAD_SIZE), 1)
    gains = dot(pick.astype(bf16), weight_ref[:, 2 * HEAD_SIZE :], NT)
    gain_ref[...] = gains[:8]
    for rows_refs, tables, normed, target in (
        ((own_ref, other_ref), (cosine_ref, sine_ref), normed_ref, kv_ref),
        ((before_own_ref, before_other_ref), (before_cosine_ref, before_sine_ref), before_normed_ref, before_kv_ref),
    ):
        put_rows(normed, core, *(normed_rows(ref[...].astype(f32), gains[0:1]) for ref in rows_refs))
        linear = dot(normed[...], weight_ref[:, : 2 * HEAD_SIZE])
        key = linear[:, :HEAD_SIZE]
        turned = key * tables[0][...] + pltpu.roll(key, HEAD_SIZE // 2, 1) * tables[1][...]
        target[:, :HEAD_SIZE] = turned.astype(bf16)
        target[:, HEAD_SIZE:] = linear[:, HEAD_SIZE:].astype(bf16)
    for j in range(sent_ref.shape[0]):

        @pl.when(j > spot)
        def _(j=j):
            sent_ref[j] = kv_ref[...]

        @pl.when(j <= spot)
        def _(j=j):
            sent_ref[j] = before_kv_ref[...]


def project_keys(place, acts, before_acts, weights, cosine, sine, spots):
    rows, width = 2 * acts[0].shape[0], acts[0].shape[1]
    whole = lambda *shape: pl.BlockSpec(shape, lambda i: (0,) * len(shape))
    table = lambda k: pl.BlockSpec((rows, HEAD_SIZE), lambda i: (k, 0))
    half = whole(rows // 2, width)
    return pl.pallas_call(
        project_keys_kernel,
        grid=(1,),
        in_specs=[pl.BlockSpec(memory_space=pltpu.SMEM)]
        + [half] * 4
        + [whole(width, 3 * HEAD_SIZE), table(0), table(0), table(2), table(2)],
        out_specs=[
            whole(rows, width), whole(rows, 2 * HEAD_SIZE), whole(spots, rows, 2 * HEAD_SIZE), whole(8, width),
        ],
        out_shape=[
            jax.ShapeDtypeStruct((rows, width), bf16),
            jax.ShapeDtypeStruct((rows, 2 * HEAD_SIZE), bf16),
            jax.ShapeDtypeStruct((spots, rows, 2 * HEAD_SIZE), bf16),
            jax.ShapeDtypeStruct((8, width), f32),
        ],
        scratch_shapes=[pltpu.VMEM((rows, width), bf16), pltpu.VMEM((rows, 2 * HEAD_SIZE), bf16)],
        compiler_params=pltpu.CompilerParams(vmem_limit_bytes=FAR_BYTES),
        name="project_keys",
    )(place, *acts, *before_acts, weights, cosine, sine, cosine, sine)


def project_kernel(
    place_ref, rows_ref, own_ref, other_ref, gain_ref, weight_ref, cosine_ref, sine_ref, pair_cosine_ref, pair_sine_ref,
    normed_ref, out_ref, pair_out_ref,
):
    gain = gain_ref[0:1, :]
    put_rows(normed_ref, place_ref[0], *(normed_rows(ref[...].astype(f32), gain) for ref in (own_ref, other_ref)))
    for values_ref, cos_ref, sin_ref, target in (
        (rows_ref, cosine_ref, sine_ref, out_ref),
        (normed_ref, pair_cosine_ref, pair_sine_ref, pair_out_ref),
    ):
        linear = dot(values_ref[...], weight_ref[...])
        for h in range(GROUP // 2):
            at = slice(h * HEAD_SIZE, (h + 1) * HEAD_SIZE)
            head = linear[:, at]
            turned = head * cos_ref[...] + pltpu.roll(head, HEAD_SIZE // 2, 1) * sin_ref[...]
            target[:, at] = turned.astype(bf16)


def project(place, rows, pair_acts, gains, weights, cosine, sine):
    count, width = rows.shape
    quarter = HALF_WIDTH // 2
    whole = lambda *shape: pl.BlockSpec(shape, lambda i: (0,) * len(shape))
    table = lambda k: pl.BlockSpec((count, HEAD_SIZE), lambda i: (k, 0))
    half = whole(count // 2, width)
    shape = jax.ShapeDtypeStruct((count, quarter), bf16)
    return pl.pallas_call(
        project_kernel,
        grid=(1,),
        in_specs=[
            pl.BlockSpec(memory_space=pltpu.SMEM), whole(count, width), half, half, whole(8, width),
            pl.BlockSpec((width, quarter), lambda i: (0, 1)), table(0), table(0), table(1), table(1),
        ],
        out_specs=[whole(count, width), whole(count, quarter), whole(count, quarter)],
        out_shape=[jax.ShapeDtypeStruct(rows.shape, bf16), shape, shape],
        compiler_params=pltpu.CompilerParams(vmem_limit_bytes=FAR_BYTES),
        name="project",
    )(place, rows, *pair_acts, gains, weights, cosine, sine, cosine, sine)


def dispatch_kernel(branch_ref, came_ref, acts_ref, gain_ref, placed_ref, hidden_ref, rows_ref):
    hidden = acts_ref[...].astype(f32) + branch_ref[...] + came_ref[...]
    hidden_ref[...] = hidden
    rows_ref[...] = dot(placed_ref[:, : hidden.shape[0]], normed_rows(hidden, gain_ref[1:2, :])).astype(bf16)


def combine_kernel(
    valid_ref, scale_ref, returned_ref, token_gate_ref, hidden_ref, teacher_ref, placed_ref, gate_ref,
    out_ref, grad_ref, rows_ref,
):
    mixture = dot(token_gate_ref[...], returned_ref[...])
    tokens = hidden_ref.shape[0]
    hidden = hidden_ref[...] + mixture[:tokens] + mixture[tokens:]
    out_ref[...] = hidden.astype(bf16)
    position = valid_ref[1] + lax.broadcasted_iota(jnp.int32, hidden.shape, 0)
    grad = jnp.where(position < valid_ref[0], scale_ref[0] * (hidden - teacher_ref[...].astype(f32)), 0.0)
    grad_ref[...] = grad
    high = grad.astype(bf16)
    low = (grad - high.astype(f32)).astype(bf16)
    picked = dot(placed_ref[...], jnp.concatenate([high, low]))
    rows_ref[...] = (gate_ref[:, 0:1] * picked).astype(bf16)


def combine(bounds, scale, returned, token_gate, hidden, teacher, placed, gate):
    (slots, width), rows, steps = returned.shape, hidden.shape[0], 3
    whole = lambda shape: pl.BlockSpec(shape, lambda i: (0,) * len(shape))
    columns = lambda count: pl.BlockSpec((count, width // steps), lambda i: (0, i))
    smem = pl.BlockSpec(memory_space=pltpu.SMEM)
    return pl.pallas_call(
        combine_kernel,
        grid=(steps,),
        in_specs=[
            smem, smem, columns(slots), whole(token_gate.shape), columns(rows), columns(rows),
            whole(placed.shape), whole(gate.shape),
        ],
        out_specs=[columns(rows), columns(rows), columns(slots)],
        out_shape=[
            jax.ShapeDtypeStruct(hidden.shape, bf16),
            jax.ShapeDtypeStruct(hidden.shape, f32),
            jax.ShapeDtypeStruct(returned.shape, bf16),
        ],
        compiler_params=pltpu.CompilerParams(vmem_limit_bytes=FAR_BYTES),
        name="combine",
    )(bounds, scale, returned, token_gate, hidden, teacher, placed, gate)


def norm_back_kernel(returned_ref, placed_ref, hidden_ref, gain_ref, grad_ref, out_ref, low_out_ref, gain_grad_ref):
    hidden = hidden_ref[...]
    inverse = lax.rsqrt(jnp.mean(hidden * hidden, axis=-1, keepdims=True) + NORM_EPS)
    input_grad, gain_grad = norm_backward(
        hidden, inverse, gain_ref[1:2, :], dot(placed_ref[...], returned_ref[...])
    )
    total = grad_ref[...] + input_grad
    out_ref[...] = total
    low_out_ref[...] = total.astype(bf16)
    gain_grad_ref[...] = jnp.broadcast_to(gain_grad, gain_grad_ref.shape)


def query_columns_kernel(rows_ref, pair_rows_ref, grad_ref, pair_grad_ref, before_ref, partial_ref):
    del before_ref
    queries = dot(rows_ref[...], grad_ref[...], TN) + dot(pair_rows_ref[...], pair_grad_ref[...], TN)
    partial_ref[...] = queries.astype(bf16)


def split_grads_kernel(place_ref, came_ref, own_ref, later_ref, before_ref):
    spot, (spots, rows, width) = place_ref[1], came_ref.shape
    step = rows // 8
    for first in range(0, rows, step):
        at = slice(first, first + step)
        add = lambda j, total, at=at: total + came_ref[j, at, :].astype(f32)
        before = lax.fori_loop(0, spot + 1, add, jnp.zeros((step, width), f32))
        before_ref[at, :] = before.astype(bf16)
        later_ref[at, :] = lax.fori_loop(spot + 1, spots, add, own_ref[at, :].astype(f32))


def keys_back_kernel(
    place_ref, later_ref, next_ref, cosine_ref, sine_ref, rows_ref, weight_ref, side_ref,
    partial_ref, own_ref, other_ref, sum_ref,
):
    total = (later_ref[...] + next_ref[...].astype(f32)).astype(bf16)
    key = total[:, :HEAD_SIZE].astype(f32)
    turned = key * cosine_ref[...] - pltpu.roll(key, HEAD_SIZE // 2, 1) * sine_ref[...]
    linear = jnp.concatenate([turned.astype(bf16), total[:, HEAD_SIZE:]], axis=1)
    partial_ref[...] = dot(rows_ref[...], linear, TN).astype(bf16)
    sum_ref[...] = side_ref[...] + dot(linear, weight_ref[...], NT)
    core, rows = place_ref[0], own_ref.shape[0]
    own_ref[...] = sum_ref[pl.ds(pl.multiple_of(core * rows, rows), rows), :]
    other_ref[...] = sum_ref[pl.ds(pl.multiple_of((1 - core) * rows, rows), rows), :]


def gain_columns_kernel(own_ref, swapped_ref, pair_ref, acts_ref, gain_grad_ref, before_ref, partial_ref):
    del before_ref
    values = acts_ref[...].astype(f32)
    inverse = lax.rsqrt(jnp.mean(values * values, axis=-1, keepdims=True) + NORM_EPS)
    normed_grad = own_ref[...] + swapped_ref[...] + pair_ref[...].astype(f32)
    gain_grad = jnp.sum(normed_grad * values * inverse, axis=0, keepdims=True)
    row = lax.broadcasted_iota(jnp.int32, (16, values.shape[1]), 0)
    gain_rows = jnp.where(row == 0, gain_grad, jnp.where(row == 1, gain_grad_ref[0:1, :], 0.0))
    square = (16, HEAD_SIZE)
    unit = lax.broadcasted_iota(jnp.int32, square, 0) == lax.broadcasted_iota(jnp.int32, square, 1)
    partial_ref[...] = dot(gain_rows.astype(bf16), unit.astype(bf16), TN).astype(bf16)


def acts_back_kernel(own_ref, swapped_ref, pair_ref, acts_ref, gain_ref, grad_ref, out_ref):
    values = acts_ref[...].astype(f32)
    inverse = lax.rsqrt(jnp.mean(values * values, axis=-1, keepdims=True) + NORM_EPS)
    normed_grad = own_ref[...] + swapped_ref[...] + pair_ref[...].astype(f32)
    out_ref[...] = grad_ref[...] + norm_backward(values, inverse, gain_ref[0:1, :], normed_grad)[0]


def whole_call(
    kernel, name, out_shape, *args, words=0, scratch_shapes=(), blocks=(), out_blocks=(), aliases=(), near=True
):
    blocks, out_blocks = dict(blocks), dict(out_blocks)
    whole = lambda shape: pl.BlockSpec(shape, lambda i: (0,) * len(shape))
    specs = [
        pl.BlockSpec(memory_space=pltpu.SMEM) if k < words else blocks.get(k, whole(arg.shape))
        for k, arg in enumerate(args)
    ]
    return pl.pallas_call(
        kernel,
        grid=(1,),
        in_specs=specs,
        out_specs=[out_blocks.get(k, whole(out.shape)) for k, out in enumerate(out_shape)],
        out_shape=out_shape,
        input_output_aliases=dict(aliases),
        scratch_shapes=list(scratch_shapes),
        compiler_params=pltpu.CompilerParams(vmem_limit_bytes=NEAR_BYTES if near else FAR_BYTES),
        name=name,
    )(*args)


def piece_at(place_ref, k, shape):
    depth, width = shape
    row_half = lax.rem(place_ref[4] + k % 2, 2)
    column_half = lax.rem(place_ref[3] + k // 2, 2)
    return (
        pl.ds(pl.multiple_of(row_half * depth, HEAD_SIZE), depth),
        pl.ds(pl.multiple_of(column_half * width, HEAD_SIZE), width),
    )


def out_project_kernel(place_ref, attn_ref, *refs):
    pieces, (own_ref, other_ref, sum_ref) = refs[:-3], refs[-3:]
    rows = own_ref.shape[0]
    sum_ref[...] = jnp.zeros_like(sum_ref)
    for k, piece in enumerate(pieces):
        features, columns = piece_at(place_ref, k, piece.shape)
        sum_ref[:, columns] += dot(attn_ref[:, features], piece[...])
    core = place_ref[0]
    own_ref[...] = sum_ref[pl.ds(pl.multiple_of(core * rows, rows), rows), :]
    other_ref[...] = sum_ref[pl.ds(pl.multiple_of((1 - core) * rows, rows), rows), :]


def out_project(place, attn, pieces):
    rows, width = attn.shape[0], 2 * pieces[0].shape[1]
    shape = jax.ShapeDtypeStruct((rows // 2, width), f32)
    vmem = pl.BlockSpec(memory_space=pltpu.VMEM)
    return pl.pallas_call(
        out_project_kernel,
        in_specs=[pl.BlockSpec(memory_space=pltpu.SMEM)] + [vmem] * (1 + len(pieces)),
        out_specs=[vmem, vmem],
        out_shape=[shape, shape],
        scratch_shapes=[pltpu.VMEM((rows, width), f32)],
        compiler_params=pltpu.CompilerParams(vmem_limit_bytes=NEAR_BYTES),
        name="out_project",
    )(place, attn, *pieces)


def out_project_back_kernel(place_ref, own_ref, other_ref, attn_ref, *refs):
    pieces, (out_ref, partial_ref, grad_ref, sum_ref) = refs[:-4], refs[-4:]
    put_rows(grad_ref, place_ref[0], own_ref[...], other_ref[...])
    sum_ref[...] = jnp.zeros_like(sum_ref)
    for k, piece in enumerate(pieces):
        features, columns = piece_at(place_ref, k, piece.shape)
        sum_ref[:, features] += dot(grad_ref[:, columns], piece[...], NT)
    out_ref[...] = sum_ref[...].astype(bf16)
    spots, planes, rows, width = partial_ref.shape
    for h in range(2):
        partial = dot(attn_ref[...], grad_ref[:, h * width : (h + 1) * width], TN)
        for l in range(planes // 2):
            for j in range(spots):
                first = (l * spots + j) * rows
                partial_ref[j, h * (planes // 2) + l] = partial[first : first + rows].astype(bf16)


def out_project_back(place, own, other, attn, pieces, spots):
    rows, width = attn.shape
    vmem = pl.BlockSpec(memory_space=pltpu.VMEM)
    return pl.pallas_call(
        out_project_back_kernel,
        in_specs=[pl.BlockSpec(memory_space=pltpu.SMEM)] + [vmem] * (3 + len(pieces)),
        out_specs=[vmem, vmem],
        out_shape=[
            jax.ShapeDtypeStruct((rows, width), bf16),
            jax.ShapeDtypeStruct((spots, 4, width // (2 * spots), width), bf16),
        ],
        scratch_shapes=[pltpu.VMEM((rows, 2 * width), bf16), pltpu.VMEM((rows, width), f32)],
        compiler_params=pltpu.CompilerParams(vmem_limit_bytes=FAR_BYTES),
        name="out_project_back",
    )(place, own, other, attn, *pieces)


def attend_back_kernel(
    place_ref, low_ref, mine_ref, theirs_ref, cosine_ref, sine_ref, keys_ref, own_ref, out_ref, grad_ref, log_ref,
    query_grad_ref, keys_grad_ref, own_grad_ref, sum_ref, turned_key_ref, weight_ref, score_ref,
):
    h, heads = pl.program_id(0), pl.num_programs(0)
    blocks, rows = keys_ref.shape[0] + 1, mine_ref.shape[0]
    spot = place_ref[1]

    @pl.when(h == 0)
    def _():
        sum_ref[...] = jnp.zeros_like(sum_ref)
        for t in range(blocks):
            turned_key_ref[t] = seen_block(spot, keys_ref, own_ref, t)[:, :HEAD_SIZE].T

    query, out_grad = side_block(place_ref, mine_ref, theirs_ref), grad_ref[...]
    delta = jnp.sum((out_grad.astype(f32) * out_ref[...]).T, axis=0, keepdims=True)
    log_total, low = log_ref[0, 0:1, :], low_ref[0:1, :]
    for t in range(blocks):
        block = seen_block(spot, keys_ref, own_ref, t)
        key, value = block[:, :HEAD_SIZE], block[:, HEAD_SIZE:]
        weights = jnp.exp2(dot(key, query, NT) * SCALE_LOG2 - log_total)
        weights = jnp.where(block_mask(low, t, blocks, rows, 0), weights, 0.0)
        weight_ref[t] = weights.astype(bf16)
        score_ref[t] = (weights * (dot(value, out_grad, NT) - delta)).astype(bf16)
    query_grad = jnp.zeros((HEAD_SIZE, rows), f32)
    for t in range(blocks):
        query_grad = query_grad + dot(turned_key_ref[t], score_ref[t])
    query_grad = (query_grad * SCALE).T.astype(bf16).astype(f32)
    turned = query_grad * cosine_ref[...] - pltpu.roll(query_grad, HEAD_SIZE // 2, 1) * sine_ref[...]
    query_grad_ref[...] = turned.astype(bf16)
    for t in range(blocks):
        sum_ref[t, :, :HEAD_SIZE] += dot(score_ref[t], query)
        sum_ref[t, :, HEAD_SIZE:] += dot(weight_ref[t], out_grad)

    @pl.when(h == heads - 1)
    def _():
        for t in range(blocks):
            target = seen_block(spot, keys_grad_ref, own_grad_ref, t)
            target[:, :HEAD_SIZE] = (sum_ref[t, :, :HEAD_SIZE] * SCALE).astype(bf16)
            target[:, HEAD_SIZE:] = sum_ref[t, :, HEAD_SIZE:].astype(bf16)


def attend_back(place, low, mine, theirs, cosine, sine, keys, own, out, out_grad, log_total):
    blocks, rows = keys.shape[0] + 1, mine.shape[0]
    whole = lambda *shape: pl.BlockSpec(shape, lambda h, place: (0,) * len(shape))
    by_head = pl.BlockSpec((rows, HEAD_SIZE), lambda h, place: (0, h))
    by_half = pl.BlockSpec((rows, HEAD_SIZE), lambda h, place: (0, lax.rem(h, GROUP // 2)))
    table = pl.BlockSpec((rows, HEAD_SIZE), lambda h, place: (0, 0))
    return pl.pallas_call(
        attend_back_kernel,
        grid_spec=pltpu.PrefetchScalarGridSpec(
            num_scalar_prefetch=1,
            grid=(GROUP,),
            in_specs=[
                whole(8, rows), by_half, by_half, table, table, whole(*keys.shape), whole(*own.shape), by_head, by_head,
                pl.BlockSpec((1, 8, rows), lambda h, place: (h, 0, 0)),
            ],
            out_specs=[by_head, whole(*keys.shape), whole(*own.shape)],
            scratch_shapes=[
                pltpu.VMEM((blocks, rows, 2 * HEAD_SIZE), f32),
                pltpu.VMEM((blocks, HEAD_SIZE, rows), bf16),
                pltpu.VMEM((blocks, rows, rows), bf16),
                pltpu.VMEM((blocks, rows, rows), bf16),
            ],
        ),
        out_shape=[
            jax.ShapeDtypeStruct((rows, HALF_WIDTH), bf16),
            jax.ShapeDtypeStruct(keys.shape, bf16),
            jax.ShapeDtypeStruct(own.shape, bf16),
        ],
        compiler_params=pltpu.CompilerParams(vmem_limit_bytes=FAR_BYTES),
        cost_estimate=pl.CostEstimate(flops=28_000_000_000, bytes_accessed=8_000_000, transcendentals=7_000_000),
        name="attend_back",
    )(place, low, mine, theirs, cosine, sine, keys, own, out, out_grad, log_total)


def body(
    acts, teacher, valid, doc_starts, routes, gates,
    w_query, key_weight, value_weight, w_out, gain_attn, gain_ffn, w_gate, w_up, w_down,
):
    half, core = lax.axis_index("xh"), lax.axis_index("c")
    plane, spot = lax.axis_index(("xh", "xl")), lax.axis_index(PLANE_CHIPS)
    chip = lax.axis_index(CHIPS)
    tok_rows, model_dim = acts.shape
    chip_rows = 2 * tok_rows
    spots = lax.axis_size(PLANE_CHIPS)
    planes = lax.axis_size(("xh", "xl"))
    chips = spots * planes
    total_tokens = chips * chip_rows
    shard_rows = w_query.shape[0]

    side = chip % 2
    place = jnp.stack([core, spot, side, half, lax.axis_index("xl")]).astype(jnp.int32)
    gain_pair = jnp.pad(jnp.stack([gain_attn, gain_ffn], axis=1), ((0, 0), (0, HEAD_SIZE - 2)))
    kv_width = 3 * HEAD_SIZE
    quarter = HALF_WIDTH // 2
    core_word = core.astype(jnp.int32).reshape(1)
    packed = jax.ShapeDtypeStruct((shard_rows, kv_width + 2 * HALF_WIDTH), bf16)
    own_part, other_part = whole_call(
        pack_kernel, "pack", [packed, packed], core_word, key_weight, value_weight, gain_pair, w_query, w_out, words=1,
        near=False,
    )
    weights_sent, out_sent = whole_call(
        unpack_kernel, "unpack",
        [
            jax.ShapeDtypeStruct((chips, 2 * shard_rows, kv_width + quarter), bf16),
            jax.ShapeDtypeStruct((spots, 2 * shard_rows, HALF_WIDTH), bf16),
        ],
        core_word, own_part, core_swap(other_part), words=1, near=False,
    )
    pair_acts = lax.ppermute(acts, "z", PAIR)
    before_acts = lax.ppermute(acts, ("xh", "xl"), [(p, p + 1) for p in range(planes - 1)])
    weights_sent, pair_acts, before_acts = lax.optimization_barrier((weights_sent, pair_acts, before_acts))
    weights = exchange(weights_sent, CHIPS)
    chip_acts = (acts, core_swap(acts))
    pair_acts = (pair_acts, core_swap(pair_acts))
    before_acts = (before_acts, core_swap(before_acts))

    first_token = chip * chip_rows
    chip_pos = first_token + jnp.arange(chip_rows, dtype=jnp.int32)
    begin = doc_begin(chip_pos, doc_starts)
    table_pos = jnp.concatenate([chip_pos, chip_pos + (1 - 2 * side) * chip_rows, chip_pos - spots * chip_rows])
    cosine, sine = rope_tables(table_pos - doc_begin(table_pos, doc_starts))
    low = jnp.maximum(begin, chip_pos - (WINDOW - 1)) - (first_token - WINDOW)
    low_rows = jnp.broadcast_to(low[None, :], (8, chip_rows))
    low_columns = jnp.broadcast_to(low[:, None], (chip_rows, HEAD_SIZE))
    block_at = jnp.arange(spots, dtype=jnp.int32)

    weights, out_sent, chip_acts, pair_acts, before_acts, low_columns, cosine, sine = lax.optimization_barrier(
        (weights, out_sent, chip_acts, pair_acts, before_acts, low_columns, cosine, sine)
    )
    out_rows = exchange(out_sent, PLANE_CHIPS)
    weights = weights.reshape(model_dim, -1)

    normed_one, own_kv, kv_sent, gain_rows = project_keys(
        place, chip_acts, before_acts, weights, cosine, sine, spots
    )
    kv_sent, out_rows = lax.optimization_barrier((kv_sent, out_rows))
    seen_kv = exchange(kv_sent, PLANE_CHIPS)
    placed, placed_by_token, token_gate, slot_gate = place_rows(routes, gates)
    all_slots = EXPERTS * CAP

    out_rows = out_rows.reshape(-1, HALF_WIDTH)
    out_pieces = [
        lax.ppermute(
            out_rows,
            ("xh", "xl", "c"),
            [
                (c * 4 + (l ^ k % 2) * 2 + (h ^ k // 2), h * 4 + l * 2 + c)
                for h in range(2)
                for l in range(2)
                for c in range(2)
            ],
        )
        for k in range(4)
    ]
    seen_kv, out_pieces = lax.optimization_barrier((seen_kv, out_pieces))

    pair_normed, query_mine, query_theirs = project(
        place, normed_one, pair_acts, gain_rows, weights, cosine, sine
    )
    query_theirs = lax.ppermute(query_theirs, "z", PAIR)
    query_theirs, placed, slot_gate, token_gate, placed_by_token = lax.optimization_barrier(
        (query_theirs, placed, slot_gate, token_gate, placed_by_token)
    )
    attn_wide, attn, log_total = attend(place, low_columns, query_mine, query_theirs, seen_kv, own_kv)

    branch, other_branch = out_project(place, attn, out_pieces)
    wide = jax.ShapeDtypeStruct((tok_rows, model_dim), f32)
    slim = jax.ShapeDtypeStruct((tok_rows, model_dim), bf16)
    slot_rows = jax.ShapeDtypeStruct((all_slots, model_dim), bf16)
    hidden_one, sent_rows = whole_call(
        dispatch_kernel, "dispatch", [wide, slot_rows], branch, core_swap(other_branch), acts, gain_rows, placed
    )

    def to_experts(rows):
        mine = exchange(rows.reshape(EXPERTS, CAP, model_dim), HALF_CHIPS).reshape(all_slots, model_dim)
        return mine, core_swap(mine)

    def from_experts(mine, theirs):
        mine, came = lax.optimization_barrier((mine.astype(bf16), core_swap(theirs.astype(bf16))))
        both = mine.astype(f32) + came.astype(f32)
        both = both.astype(bf16).reshape(EXPERTS, CAP, model_dim)
        return exchange(both, HALF_CHIPS).reshape(all_slots, model_dim)

    units = w_gate.shape[1]
    gate_up = jnp.concatenate([w_gate, w_up], axis=1)

    def expert_hidden(rows):
        both = dot(rows, gate_up)
        gate_pre, up_pre = both[:, :units], both[:, units:]
        return gate_pre, up_pre, (jax.nn.silu(gate_pre) * up_pre).astype(bf16)

    def hidden_backward(kept, grad_rows):
        gate_pre, up_pre = kept[0], kept[1]
        grad_hidden = dot(grad_rows, w_down, NT)
        sigmoid = jax.nn.sigmoid(gate_pre)
        grad_gate = (grad_hidden * up_pre * sigmoid * (1.0 + gate_pre * (1.0 - sigmoid))).astype(bf16)
        grad_up = (grad_hidden * gate_pre * sigmoid).astype(bf16)
        return jnp.concatenate([grad_gate, grad_up], axis=1)

    def rows_backward(back):
        return dot(back, gate_up, NT)

    rows_mine, rows_theirs = to_experts(sent_rows)
    kept_mine = expert_hidden(rows_mine)
    kept_mine, rows_theirs = lax.optimization_barrier((kept_mine, rows_theirs))
    kept_theirs = expert_hidden(rows_theirs)
    returned = from_experts(dot(kept_mine[2], w_down), dot(kept_theirs[2], w_down))
    bounds = jnp.stack([valid[0], first_token + core * tok_rows]).astype(jnp.int32)
    loss_scale = (total_tokens / valid.astype(f32)).reshape(1)
    activations, grad_two, grad_slots = combine(
        bounds, loss_scale, returned, token_gate, hidden_one, teacher, placed, slot_gate
    )
    grads_mine, grads_theirs = to_experts(grad_slots)
    back_mine = hidden_backward(kept_mine, grads_mine)
    back_mine, grads_theirs = lax.optimization_barrier((back_mine, grads_theirs))
    back_theirs = hidden_backward(kept_theirs, grads_theirs)
    grad_returned = from_experts(rows_backward(back_mine), rows_backward(back_theirs))

    expert_parts = (
        (dot(rows_mine, back_mine, TN) + dot(rows_theirs, back_theirs, TN)).astype(bf16),
        (dot(kept_mine[2], grads_mine, TN) + dot(kept_theirs[2], grads_theirs, TN)).astype(bf16),
    )
    expert_part = jnp.concatenate(
        [expert_parts[0], expert_parts[1][:, :HALF_WIDTH], expert_parts[1][:, HALF_WIDTH:]]
    )

    expert_part, grad_returned = lax.optimization_barrier((expert_part, grad_returned))
    grad_one, grad_branch, gain_two_grad = whole_call(
        norm_back_kernel, "norm_back", [wide, slim, jax.ShapeDtypeStruct((8, model_dim), f32)],
        grad_returned, placed_by_token, hidden_one, gain_rows, grad_two, near=False,
    )
    grad_attn, out_partial = out_project_back(place, grad_branch, core_swap(grad_branch), attn, out_pieces, spots)

    def send_to_chips(partial):
        return exchange(partial.astype(bf16).reshape(chips, 2 * shard_rows, -1), CHIPS)

    expert_other = lax.ppermute(expert_part, "xh", SWAP)
    out_received = exchange(out_partial, PLANE_CHIPS)

    query_lin_grad, kv_grad, own_kv_grad = attend_back(
        place, low_rows, query_mine, query_theirs, cosine, sine, seen_kv, own_kv, attn_wide, grad_attn, log_total
    )
    query_left, query_right = query_lin_grad[:, :quarter], query_lin_grad[:, quarter:]
    pair_query_grad = lax.ppermute(jnp.where(side == 0, query_right, query_left), "z", PAIR)
    kv_grad, out_received = lax.optimization_barrier((kv_grad, out_received))
    came = exchange(kv_grad, PLANE_CHIPS)
    side_query_grad = jnp.where(side == 0, query_left, query_right)
    pair_normed_grad = dot(pair_query_grad, weights[:, kv_width:], NT)
    pair_normed_grad = of_core(core, pair_normed_grad, True) + core_swap(of_core(core, pair_normed_grad, False))
    back_normed_grad = lax.ppermute(pair_normed_grad.astype(bf16), "z", PAIR)
    side_normed_grad = dot(side_query_grad, weights[:, kv_width:], NT)
    came, expert_other, side_query_grad, pair_query_grad = lax.optimization_barrier(
        (came, expert_other, side_query_grad, pair_query_grad)
    )
    square = (chip_rows, 2 * HEAD_SIZE)
    later_grad, before_grad = whole_call(
        split_grads_kernel, "split_grads", [jax.ShapeDtypeStruct(square, f32), jax.ShapeDtypeStruct(square, bf16)],
        place, came, own_kv_grad, words=1,
    )
    next_grad = lax.ppermute(before_grad, ("xh", "xl"), [(p + 1, p) for p in range(planes - 1)])
    next_grad, back_normed_grad = lax.optimization_barrier((next_grad, back_normed_grad))
    table = pl.BlockSpec((chip_rows, HEAD_SIZE), lambda i: (0, 0))
    partial_shape = jax.ShapeDtypeStruct((model_dim, kv_width + quarter), bf16)
    unread = pl.BlockSpec((16, HEAD_SIZE), lambda i: (0, 0))
    partial, normed_grad, other_normed_grad = whole_call(
        keys_back_kernel, "keys_back", [partial_shape, wide, wide],
        place, later_grad, next_grad, cosine, sine, normed_one, weights, side_normed_grad, words=1,
        blocks={3: table, 4: table, 6: pl.BlockSpec((model_dim, 2 * HEAD_SIZE), lambda i: (0, 0))},
        out_blocks={0: pl.BlockSpec((model_dim, 2 * HEAD_SIZE), lambda i: (0, 0))},
        scratch_shapes=[pltpu.VMEM((chip_rows, model_dim), f32)],
    )
    swapped_grad = core_swap(other_normed_grad)
    (partial,) = whole_call(
        query_columns_kernel, "query_columns", [partial_shape],
        normed_one, pair_normed, side_query_grad, pair_query_grad, partial, blocks={4: unread},
        out_blocks={0: pl.BlockSpec((model_dim, quarter), lambda i: (0, 1))}, aliases={4: 0}, near=False,
    )
    (partial,) = whole_call(
        gain_columns_kernel, "gain_columns", [partial_shape],
        normed_grad, swapped_grad, back_normed_grad, acts, gain_two_grad, partial, blocks={5: unread},
        out_blocks={0: pl.BlockSpec((model_dim, HEAD_SIZE), lambda i: (0, 2))}, aliases={5: 0}, near=False,
    )
    partial, expert_other, out_received, grad_one = lax.optimization_barrier(
        (partial, expert_other, out_received, grad_one)
    )
    (grad_acts,) = whole_call(
        acts_back_kernel, "acts_back", [wide],
        normed_grad, swapped_grad, back_normed_grad, acts, gain_rows, grad_one, near=False,
    )
    received = send_to_chips(partial)
    expert_grad = expert_part.astype(f32) + expert_other.astype(f32)
    expert_grads = (
        expert_grad[:model_dim, :units],
        expert_grad[:model_dim, units:],
        jnp.concatenate([expert_grad[model_dim : model_dim + units], expert_grad[model_dim + units :]], axis=1),
    )
    plane_sums = jnp.sum(out_received.astype(f32), axis=0).astype(bf16)
    plane_sums = plane_sums.reshape(2, 2, 2, shard_rows, -1)
    grad_w_out = 0.0
    for k in range(4):
        piece = lax.dynamic_index_in_dim(plane_sums, (lax.axis_index("xl") + k) % 2, 1, False)
        piece = lax.dynamic_index_in_dim(piece, (half + k // 2) % 2, 1, False)
        piece = lax.ppermute(
            piece,
            ("xh", "xl", "c"),
            [
                (h * 4 + l * 2 + c, c * 4 + (l ^ k % 2) * 2 + (h ^ k // 2))
                for h in range(2)
                for l in range(2)
                for c in range(2)
            ],
        )
        grad_w_out = grad_w_out + piece.astype(f32)
    grad_w_out = jnp.concatenate([grad_w_out[0], grad_w_out[1]], axis=1)
    received = received.astype(f32).reshape(chips // 2, 2, 2 * shard_rows, -1)
    sums = jnp.sum(received, axis=0)
    sums = jnp.concatenate(
        [sums[0, :, :kv_width] + sums[1, :, :kv_width], sums[0, :, kv_width:], sums[1, :, kv_width:]], axis=1
    ).reshape(2, shard_rows, -1)
    given = core_swap(jnp.where(core == 0, sums[1], sums[0]))
    kept = jnp.where(core == 0, sums[0], sums[1])
    sums = (jnp.where(core == 0, kept, given), jnp.where(core == 0, given, kept))

    def columns(begin_at, width):
        return jnp.concatenate([part[:, begin_at : begin_at + width] for part in sums], axis=1)

    gain_sums = sums[0][:, 2 * HEAD_SIZE : 2 * HEAD_SIZE + 2] + sums[1][:, 2 * HEAD_SIZE : 2 * HEAD_SIZE + 2]
    return (
        activations,
        grad_acts,
        columns(kv_width, HALF_WIDTH),
        columns(0, HEAD_SIZE),
        columns(HEAD_SIZE, HEAD_SIZE),
        grad_w_out,
        gain_sums[:, 0],
        gain_sums[:, 1],
        *expert_grads,
    )


def solution(mesh):
    fine_mesh = jax.sharding.Mesh(mesh.devices.reshape(2, 2, 4, 4, 2), ALL)
    rows, vector = P(ALL, None), P(ALL)
    wide, tall = P(None, ("xl", "y", "z", "c")), P(("xl", "y", "z", "c"), None)
    return jax.shard_map(
        body,
        mesh=fine_mesh,
        in_specs=(
            rows, rows, P(), P(), rows, rows, rows, rows, rows, rows, vector, vector, wide, wide, tall,
        ),
        out_specs=(rows, rows, rows, rows, rows, rows, vector, vector, wide, wide, tall),
        check_vma=False,
    )
```

```python
import math

import jax
import jax.numpy as jnp
import numpy as np
from jax import lax
from jax.experimental import pallas as pl
from jax.experimental.pallas import tpu as pltpu
from jax.sharding import PartitionSpec as P

HEAD_SIZE = 128
GROUP = 6
HALF_WIDTH = GROUP * HEAD_SIZE
WINDOW = 4096
CAP = 24
EXPERTS = 32
FAR_BYTES = 60 * 1024 * 1024
NEAR_BYTES = 24 * 1024 * 1024

NORM_EPS = 1e-06
ROPE_BASE = 1000000.0
MASKED = -1e30
SCALE = HEAD_SIZE ** (-0.5)
SCALE_LOG2 = SCALE * math.log2(math.e)

ALL = ("xh", "xl", "y", "z", "c")
CHIPS = ("xh", "xl", "y", "z")
HALF_CHIPS = ("xl", "y", "z")
PLANE_CHIPS = ("y", "z")
SWAP = [(0, 1), (1, 0)]
PAIR = [(0, 1), (1, 0), (2, 3), (3, 2)]

f32 = jnp.float32
bf16 = jnp.bfloat16


def dot(a, b, dims=((1,), (0,))):
    return lax.dot_general(a, b, (dims, ((), ())), preferred_element_type=f32)


NT = ((1,), (1,))
TN = ((0,), (0,))


def core_swap(value):
    return lax.ppermute(value, "c", SWAP)


def exchange(value, axes):
    return lax.all_to_all(value, axes, 0, 0, tiled=True)


def of_core(core, rows, own):
    upper, lower = jnp.split(rows, 2)
    return jnp.where((core == 0) == own, upper, lower)


def doc_begin(positions, doc_starts):
    before = doc_starts[None, :] <= positions[:, None]
    return jnp.max(jnp.where(before, doc_starts[None, :], 0), axis=-1)


def rope_tables(offset):
    column = jnp.arange(HEAD_SIZE, dtype=jnp.int32)
    half = HEAD_SIZE // 2
    inv_freq = jnp.exp((column % half).astype(f32) * (-2.0 * math.log(ROPE_BASE) / HEAD_SIZE))
    angle = offset.astype(f32)[:, None] * inv_freq[None, :]
    return jnp.cos(angle), jnp.where(column[None, :] < half, -1.0, 1.0) * jnp.sin(angle)


def norm_backward(values, inverse, gain_row, incoming_grad):
    scaled = incoming_grad * gain_row
    input_grad = inverse * scaled - values * inverse * inverse * inverse * jnp.mean(
        scaled * values, axis=-1, keepdims=True
    )
    gain_grad = jnp.sum(incoming_grad * values * inverse, axis=0, keepdims=True)
    return (input_grad, gain_grad)


def block_mask(low, t, blocks, rows, key_axis):
    key_at = lax.broadcasted_iota(jnp.int32, (rows, rows), key_axis)
    allowed = key_at >= low - t * rows
    if t == blocks - 1:
        allowed = allowed & (key_at <= lax.broadcasted_iota(jnp.int32, (rows, rows), 1 - key_axis))
    return allowed


def seen_block(spot, keys_ref, own_ref, t):
    spots = keys_ref.shape[0]
    return own_ref if t == spots else keys_ref.at[lax.rem(spot + t, spots)]


def side_block(place_ref, mine_ref, theirs_ref):
    mine = pl.program_id(0) // (GROUP // 2) == place_ref[2]
    return jnp.where(mine, mine_ref[...], theirs_ref[...])


def attend_kernel(
    place_ref, low_ref, mine_ref, theirs_ref, keys_ref, own_ref, out_ref, low_out_ref, log_ref, score_ref
):
    blocks, rows = keys_ref.shape[0] + 1, mine_ref.shape[0]
    query = side_block(place_ref, mine_ref, theirs_ref)
    spot = place_ref[1]
    low = low_ref[:, 0:1]
    top = None
    for t in range(blocks):
        score = dot(query, seen_block(spot, keys_ref, own_ref, t)[:, :HEAD_SIZE], NT)
        score = jnp.where(block_mask(low, t, blocks, rows, 1), score, MASKED)
        score_ref[t] = score
        part = jnp.maximum(score[:, :HEAD_SIZE], score[:, HEAD_SIZE:])
        top = part if top is None else jnp.maximum(top, part)
    top = jnp.max(top, axis=1, keepdims=True) * SCALE_LOG2
    total = jnp.zeros((rows, HEAD_SIZE), f32)
    mixed = jnp.zeros((rows, HEAD_SIZE), f32)
    for t in range(blocks):
        weights = jnp.exp2(score_ref[t] * SCALE_LOG2 - top)
        total = total + weights[:, :HEAD_SIZE] + weights[:, HEAD_SIZE:]
        value = seen_block(spot, keys_ref, own_ref, t)[:, HEAD_SIZE:]
        mixed = mixed + dot(weights.astype(bf16), value)
    total = jnp.sum(total, axis=1, keepdims=True)
    log_ref[0] = jnp.broadcast_to(top + jnp.log2(total), (rows, HEAD_SIZE)).T[:8]
    mixed = mixed / total
    out_ref[...] = mixed
    low_out_ref[...] = mixed.astype(bf16)


def attend(place, low, mine, theirs, keys, own):
    blocks, rows = keys.shape[0] + 1, mine.shape[0]
    whole = lambda *shape: pl.BlockSpec(shape, lambda h, place: (0,) * len(shape))
    by_head = pl.BlockSpec((rows, HEAD_SIZE), lambda h, place: (0, h))
    by_half = pl.BlockSpec((rows, HEAD_SIZE), lambda h, place: (0, lax.rem(h, GROUP // 2)))
    return pl.pallas_call(
        attend_kernel,
        grid_spec=pltpu.PrefetchScalarGridSpec(
            num_scalar_prefetch=1,
            grid=(GROUP,),
            in_specs=[whole(rows, HEAD_SIZE), by_half, by_half, whole(*keys.shape), whole(*own.shape)],
            out_specs=[by_head, by_head, pl.BlockSpec((1, 8, rows), lambda h, place: (h, 0, 0))],
            scratch_shapes=[pltpu.VMEM((blocks, rows, rows), f32)],
        ),
        out_shape=[
            jax.ShapeDtypeStruct((rows, HALF_WIDTH), f32),
            jax.ShapeDtypeStruct((rows, HALF_WIDTH), bf16),
            jax.ShapeDtypeStruct((GROUP, 8, rows), f32),
        ],
        compiler_params=pltpu.CompilerParams(vmem_limit_bytes=FAR_BYTES),
        cost_estimate=pl.CostEstimate(flops=20_000_000_000, bytes_accessed=4_000_000, transcendentals=7_000_000),
        name="attend",
    )(place, low, mine, theirs, keys, own)


def pack_kernel(core_ref, key_ref, value_ref, gain_ref, query_ref, out_weight_ref, own_ref, other_ref):
    for k in range(2):
        at = slice(k * HEAD_SIZE, (k + 1) * HEAD_SIZE)
        wide = slice(k * HALF_WIDTH, (k + 1) * HALF_WIDTH)
        parts = [key_ref[:, at], value_ref[:, at], gain_ref[...], query_ref[:, wide], out_weight_ref[:, wide]]
        part = jnp.concatenate(parts, axis=1)

        @pl.when(core_ref[0] == k)
        def _(part=part):
            own_ref[...] = part

        @pl.when(core_ref[0] != k)
        def _(part=part):
            other_ref[...] = part


def unpack_kernel(core_ref, own_ref, other_ref, weights_ref, out_ref):
    rows = own_ref.shape[0]
    at = lax.broadcasted_iota(jnp.int32, (2 * rows, rows), 0) - lax.broadcasted_iota(jnp.int32, (2 * rows, rows), 1)
    place = lambda first: jnp.where(at == first, 1.0, 0.0).astype(bf16)
    core = core_ref[0]
    full = (dot(place(core * rows), own_ref[...]) + dot(place((1 - core) * rows), other_ref[...])).astype(bf16)
    kv_width, quarter = 3 * HEAD_SIZE, HALF_WIDTH // 2
    for k in range(2):
        first = kv_width + k * quarter
        part = jnp.concatenate([full[:, :kv_width], full[:, first : first + quarter]], axis=1)
        for chip in range(k, weights_ref.shape[0], 2):
            weights_ref[chip] = part
    for spot in range(out_ref.shape[0]):
        out_ref[spot] = full[:, kv_width + HALF_WIDTH :]


def place_rows_kernel(route_ref, gate_ref, placed_ref, placed_by_token_ref, token_gate_ref, slot_gate_ref):
    tokens, top = route_ref.shape
    slots = EXPERTS * CAP
    expert = lax.broadcasted_iota(jnp.int32, (tokens, HEAD_SIZE), 1)
    chosen = jnp.zeros((tokens, HEAD_SIZE), f32)
    gate = jnp.zeros((tokens, HEAD_SIZE), f32)
    for k in range(top):
        hit = route_ref[:, k : k + 1] == expert
        chosen = chosen + jnp.where(hit, 1.0, 0.0)
        gate = gate + jnp.where(hit, gate_ref[:, k : k + 1], 0.0)
    square = (tokens, tokens)
    earlier = lax.broadcasted_iota(jnp.int32, square, 1) < lax.broadcasted_iota(jnp.int32, square, 0)
    chosen = chosen.astype(bf16)
    before = dot(jnp.where(earlier, 1.0, 0.0).astype(bf16), chosen)
    first = lax.broadcasted_iota(jnp.int32, (HEAD_SIZE, slots), 0) * CAP
    slot = lax.broadcasted_iota(jnp.int32, (HEAD_SIZE, slots), 1)
    within = (slot >= first) & (slot < first + CAP)
    spread = jnp.where(within, 1.0, 0.0).astype(bf16)
    slot_in = jnp.sum(jnp.where(within, slot - first, 0).astype(f32), axis=0, keepdims=True)
    here = (dot(chosen, spread) > 0.5) & (jnp.abs(dot(before.astype(bf16), spread) - slot_in) < 0.5)
    high = gate.astype(bf16)
    low = (gate - high.astype(f32)).astype(bf16)
    high_at = jnp.where(here, dot(high, spread), 0.0)
    low_at = jnp.where(here, dot(low, spread), 0.0)
    placed = jnp.where(here, 1.0, 0.0)
    placed_by_token_ref[...] = placed.astype(bf16)
    by_slot = placed.T.astype(bf16)
    placed_ref[:, :tokens] = by_slot
    placed_ref[:, tokens:] = by_slot
    token_gate_ref[:tokens] = high_at.astype(bf16)
    token_gate_ref[tokens:] = low_at.astype(bf16)
    total = jnp.sum((high_at + low_at).T, axis=1, keepdims=True)
    slot_gate_ref[...] = jnp.broadcast_to(total, (slots, HEAD_SIZE))


def place_rows(routes, gates):
    tokens, slots = routes.shape[0], EXPERTS * CAP
    by_token = jax.ShapeDtypeStruct((tokens, slots), bf16)
    return pl.pallas_call(
        place_rows_kernel,
        out_shape=[
            jax.ShapeDtypeStruct((slots, 2 * tokens), bf16),
            by_token,
            jax.ShapeDtypeStruct((2 * tokens, slots), bf16),
            jax.ShapeDtypeStruct((slots, HEAD_SIZE), f32),
        ],
        compiler_params=pltpu.CompilerParams(vmem_limit_bytes=NEAR_BYTES),
        name="place_rows",
    )(routes, gates)


def normed_rows(values, gain_row):
    inverse = lax.rsqrt(jnp.mean(values * values, axis=-1, keepdims=True) + NORM_EPS)
    return (values * inverse * gain_row).astype(bf16)


def put_rows(target_ref, core, own, other):
    rows = own.shape[0]
    target_ref[pl.ds(pl.multiple_of(core * rows, rows), rows), :] = own
    target_ref[pl.ds(pl.multiple_of((1 - core) * rows, rows), rows), :] = other


def project_keys_kernel(
    place_ref, own_ref, other_ref, before_own_ref, before_other_ref, weight_ref,
    cosine_ref, sine_ref, before_cosine_ref, before_sine_ref,
    normed_ref, kv_ref, sent_ref, gain_ref, before_normed_ref, before_kv_ref,
):
    core, spot = place_ref[0], place_ref[1]
    pick = lax.broadcasted_iota(jnp.int32, (16, HEAD_SIZE), 0) == lax.broadcasted_iota(jnp.int32, (16, HEAD_SIZE), 1)
    gains = dot(pick.astype(bf16), weight_ref[:, 2 * HEAD_SIZE :], NT)
    gain_ref[...] = gains[:8]
    for rows_refs, tables, normed, target in (
        ((own_ref, other_ref), (cosine_ref, sine_ref), normed_ref, kv_ref),
        ((before_own_ref, before_other_ref), (before_cosine_ref, before_sine_ref), before_normed_ref, before_kv_ref),
    ):
        put_rows(normed, core, *(normed_rows(ref[...].astype(f32), gains[0:1]) for ref in rows_refs))
        linear = dot(normed[...], weight_ref[:, : 2 * HEAD_SIZE])
        key = linear[:, :HEAD_SIZE]
        turned = key * tables[0][...] + pltpu.roll(key, HEAD_SIZE // 2, 1) * tables[1][...]
        target[:, :HEAD_SIZE] = turned.astype(bf16)
        target[:, HEAD_SIZE:] = linear[:, HEAD_SIZE:].astype(bf16)
    for j in range(sent_ref.shape[0]):

        @pl.when(j > spot)
        def _(j=j):
            sent_ref[j] = kv_ref[...]

        @pl.when(j <= spot)
        def _(j=j):
            sent_ref[j] = before_kv_ref[...]


def project_keys(place, acts, before_acts, weights, cosine, sine, spots):
    rows, width = 2 * acts[0].shape[0], acts[0].shape[1]
    whole = lambda *shape: pl.BlockSpec(shape, lambda i: (0,) * len(shape))
    table = lambda k: pl.BlockSpec((rows, HEAD_SIZE), lambda i: (k, 0))
    half = whole(rows // 2, width)
    return pl.pallas_call(
        project_keys_kernel,
        grid=(1,),
        in_specs=[pl.BlockSpec(memory_space=pltpu.SMEM)]
        + [half] * 4
        + [whole(width, 3 * HEAD_SIZE), table(0), table(0), table(2), table(2)],
        out_specs=[
            whole(rows, width), whole(rows, 2 * HEAD_SIZE), whole(spots, rows, 2 * HEAD_SIZE), whole(8, width),
        ],
        out_shape=[
            jax.ShapeDtypeStruct((rows, width), bf16),
            jax.ShapeDtypeStruct((rows, 2 * HEAD_SIZE), bf16),
            jax.ShapeDtypeStruct((spots, rows, 2 * HEAD_SIZE), bf16),
            jax.ShapeDtypeStruct((8, width), f32),
        ],
        scratch_shapes=[pltpu.VMEM((rows, width), bf16), pltpu.VMEM((rows, 2 * HEAD_SIZE), bf16)],
        compiler_params=pltpu.CompilerParams(vmem_limit_bytes=FAR_BYTES),
        name="project_keys",
    )(place, *acts, *before_acts, weights, cosine, sine, cosine, sine)


def project_kernel(
    place_ref, rows_ref, own_ref, other_ref, gain_ref, weight_ref, cosine_ref, sine_ref, pair_cosine_ref, pair_sine_ref,
    normed_ref, out_ref, pair_out_ref,
):
    gain = gain_ref[0:1, :]
    put_rows(normed_ref, place_ref[0], *(normed_rows(ref[...].astype(f32), gain) for ref in (own_ref, other_ref)))
    for values_ref, cos_ref, sin_ref, target in (
        (rows_ref, cosine_ref, sine_ref, out_ref),
        (normed_ref, pair_cosine_ref, pair_sine_ref, pair_out_ref),
    ):
        linear = dot(values_ref[...], weight_ref[...])
        for h in range(GROUP // 2):
            at = slice(h * HEAD_SIZE, (h + 1) * HEAD_SIZE)
            head = linear[:, at]
            turned = head * cos_ref[...] + pltpu.roll(head, HEAD_SIZE // 2, 1) * sin_ref[...]
            target[:, at] = turned.astype(bf16)


def project(place, rows, pair_acts, gains, weights, cosine, sine):
    count, width = rows.shape
    quarter = HALF_WIDTH // 2
    whole = lambda *shape: pl.BlockSpec(shape, lambda i: (0,) * len(shape))
    table = lambda k: pl.BlockSpec((count, HEAD_SIZE), lambda i: (k, 0))
    half = whole(count // 2, width)
    shape = jax.ShapeDtypeStruct((count, quarter), bf16)
    return pl.pallas_call(
        project_kernel,
        grid=(1,),
        in_specs=[
            pl.BlockSpec(memory_space=pltpu.SMEM), whole(count, width), half, half, whole(8, width),
            pl.BlockSpec((width, quarter), lambda i: (0, 1)), table(0), table(0), table(1), table(1),
        ],
        out_specs=[whole(count, width), whole(count, quarter), whole(count, quarter)],
        out_shape=[jax.ShapeDtypeStruct(rows.shape, bf16), shape, shape],
        compiler_params=pltpu.CompilerParams(vmem_limit_bytes=FAR_BYTES),
        name="project",
    )(place, rows, *pair_acts, gains, weights, cosine, sine, cosine, sine)


def dispatch_kernel(branch_ref, came_ref, acts_ref, gain_ref, placed_ref, hidden_ref, rows_ref):
    hidden = acts_ref[...].astype(f32) + branch_ref[...] + came_ref[...]
    hidden_ref[...] = hidden
    rows_ref[...] = dot(placed_ref[:, : hidden.shape[0]], normed_rows(hidden, gain_ref[1:2, :])).astype(bf16)


def combine_kernel(
    valid_ref, scale_ref, returned_ref, token_gate_ref, hidden_ref, teacher_ref, placed_ref, gate_ref,
    out_ref, grad_ref, rows_ref,
):
    mixture = dot(token_gate_ref[...], returned_ref[...])
    tokens = hidden_ref.shape[0]
    hidden = hidden_ref[...] + mixture[:tokens] + mixture[tokens:]
    out_ref[...] = hidden.astype(bf16)
    position = valid_ref[1] + lax.broadcasted_iota(jnp.int32, hidden.shape, 0)
    grad = jnp.where(position < valid_ref[0], scale_ref[0] * (hidden - teacher_ref[...].astype(f32)), 0.0)
    grad_ref[...] = grad
    high = grad.astype(bf16)
    low = (grad - high.astype(f32)).astype(bf16)
    picked = dot(placed_ref[...], jnp.concatenate([high, low]))
    rows_ref[...] = (gate_ref[:, 0:1] * picked).astype(bf16)


def combine(bounds, scale, returned, token_gate, hidden, teacher, placed, gate):
    (slots, width), rows, steps = returned.shape, hidden.shape[0], 3
    whole = lambda shape: pl.BlockSpec(shape, lambda i: (0,) * len(shape))
    columns = lambda count: pl.BlockSpec((count, width // steps), lambda i: (0, i))
    smem = pl.BlockSpec(memory_space=pltpu.SMEM)
    return pl.pallas_call(
        combine_kernel,
        grid=(steps,),
        in_specs=[
            smem, smem, columns(slots), whole(token_gate.shape), columns(rows), columns(rows),
            whole(placed.shape), whole(gate.shape),
        ],
        out_specs=[columns(rows), columns(rows), columns(slots)],
        out_shape=[
            jax.ShapeDtypeStruct(hidden.shape, bf16),
            jax.ShapeDtypeStruct(hidden.shape, f32),
            jax.ShapeDtypeStruct(returned.shape, bf16),
        ],
        compiler_params=pltpu.CompilerParams(vmem_limit_bytes=FAR_BYTES),
        name="combine",
    )(bounds, scale, returned, token_gate, hidden, teacher, placed, gate)


def norm_back_kernel(returned_ref, placed_ref, hidden_ref, gain_ref, grad_ref, out_ref, low_out_ref, gain_grad_ref):
    hidden = hidden_ref[...]
    inverse = lax.rsqrt(jnp.mean(hidden * hidden, axis=-1, keepdims=True) + NORM_EPS)
    input_grad, gain_grad = norm_backward(
        hidden, inverse, gain_ref[1:2, :], dot(placed_ref[...], returned_ref[...])
    )
    total = grad_ref[...] + input_grad
    out_ref[...] = total
    low_out_ref[...] = total.astype(bf16)
    gain_grad_ref[...] = jnp.broadcast_to(gain_grad, gain_grad_ref.shape)


def early_columns_kernel(rows_ref, pair_rows_ref, grad_ref, pair_grad_ref, gain_grad_ref, partial_ref):
    row = lax.broadcasted_iota(jnp.int32, (16, partial_ref.shape[0]), 0)
    gain_rows = jnp.where(row == 0, gain_grad_ref[0:1, :], 0.0)
    square = (16, HEAD_SIZE)
    unit = lax.broadcasted_iota(jnp.int32, square, 0) == lax.broadcasted_iota(jnp.int32, square, 1)
    partial_ref[:, :HEAD_SIZE] = dot(gain_rows.astype(bf16), unit.astype(bf16), TN).astype(bf16)
    queries = dot(rows_ref[...], grad_ref[...], TN) + dot(pair_rows_ref[...], pair_grad_ref[...], TN)
    partial_ref[:, HEAD_SIZE:] = queries.astype(bf16)


def add_pair_kernel(own_ref, other_ref, *out_refs):
    total = own_ref[...].astype(f32) + other_ref[...].astype(f32)
    width = out_refs[0].shape[1]
    for k, ref in enumerate(out_refs):
        ref[...] = total[:, k * width : (k + 1) * width]


def expert_sums(own, other, depth):
    width = own.shape[1]
    units = width // 2
    cost = pl.CostEstimate(flops=1, bytes_accessed=1, transcendentals=0)
    params = pltpu.CompilerParams(vmem_limit_bytes=FAR_BYTES)
    rows = depth // 6
    part = pl.BlockSpec((rows, width), lambda i: (i, 0))
    grad_gate, grad_up = pl.pallas_call(
        add_pair_kernel,
        grid=(6,),
        in_specs=[part, part],
        out_specs=[pl.BlockSpec((rows, units), lambda i: (i, 0))] * 2,
        out_shape=[jax.ShapeDtypeStruct((depth, units), f32)] * 2,
        compiler_params=params,
        cost_estimate=cost,
        name="add_gate_up",
    )(own, other)
    part = pl.BlockSpec((units, width), lambda i: (depth // units + i, 0))
    grad_down = pl.pallas_call(
        add_pair_kernel,
        grid=(2,),
        in_specs=[part, part],
        out_specs=pl.BlockSpec((units, width), lambda i: (0, i)),
        out_shape=jax.ShapeDtypeStruct((units, 2 * width), f32),
        compiler_params=params,
        cost_estimate=cost,
        name="add_down",
    )(own, other)
    return grad_gate, grad_up, grad_down


def split_grads_kernel(place_ref, came_ref, own_ref, later_ref, before_ref):
    spot, (spots, rows, width) = place_ref[1], came_ref.shape
    step = rows // 8
    for first in range(0, rows, step):
        at = slice(first, first + step)
        add = lambda j, total, at=at: total + came_ref[j, at, :].astype(f32)
        before = lax.fori_loop(0, spot + 1, add, jnp.zeros((step, width), f32))
        before_ref[at, :] = before.astype(bf16)
        later_ref[at, :] = lax.fori_loop(spot + 1, spots, add, own_ref[at, :].astype(f32))


def key_columns_kernel(later_ref, next_ref, cosine_ref, sine_ref, rows_ref, before_ref, partial_ref, linear_ref):
    del before_ref
    total = (later_ref[...] + next_ref[...].astype(f32)).astype(bf16)
    key = total[:, :HEAD_SIZE].astype(f32)
    turned = key * cosine_ref[...] - pltpu.roll(key, HEAD_SIZE // 2, 1) * sine_ref[...]
    linear = jnp.concatenate([turned.astype(bf16), total[:, HEAD_SIZE:]], axis=1)
    linear_ref[...] = linear
    partial_ref[...] = dot(rows_ref[...], linear, TN).astype(bf16)


def acts_back_kernel(own_ref, swapped_ref, pair_ref, acts_ref, gain_ref, grad_ref, out_ref):
    values = acts_ref[...].astype(f32)
    inverse = lax.rsqrt(jnp.mean(values * values, axis=-1, keepdims=True) + NORM_EPS)
    normed_grad = own_ref[...] + swapped_ref[...] + pair_ref[...].astype(f32)
    out_ref[...] = grad_ref[...] + norm_backward(values, inverse, gain_ref[0:1, :], normed_grad)[0]


def whole_call(
    kernel, name, out_shape, *args, words=0, scratch_shapes=(), blocks=(), out_blocks=(), aliases=(), near=True,
    cost=None,
):
    blocks, out_blocks = dict(blocks), dict(out_blocks)
    whole = lambda shape: pl.BlockSpec(shape, lambda i: (0,) * len(shape))
    specs = [
        pl.BlockSpec(memory_space=pltpu.SMEM) if k < words else blocks.get(k, whole(arg.shape))
        for k, arg in enumerate(args)
    ]
    return pl.pallas_call(
        kernel,
        grid=(1,),
        in_specs=specs,
        out_specs=[out_blocks.get(k, whole(out.shape)) for k, out in enumerate(out_shape)],
        out_shape=out_shape,
        input_output_aliases=dict(aliases),
        scratch_shapes=list(scratch_shapes),
        compiler_params=pltpu.CompilerParams(vmem_limit_bytes=NEAR_BYTES if near else FAR_BYTES),
        cost_estimate=cost,
        name=name,
    )(*args)


def piece_at(place_ref, k, shape):
    depth, width = shape
    row_half = lax.rem(place_ref[4] + k % 2, 2)
    column_half = lax.rem(place_ref[3] + k // 2, 2)
    return (
        pl.ds(pl.multiple_of(row_half * depth, HEAD_SIZE), depth),
        pl.ds(pl.multiple_of(column_half * width, HEAD_SIZE), width),
    )


def out_project_kernel(place_ref, attn_ref, *refs):
    pieces, (own_ref, other_ref, sum_ref) = refs[:-3], refs[-3:]
    rows = own_ref.shape[0]
    sum_ref[...] = jnp.zeros_like(sum_ref)
    for k, piece in enumerate(pieces):
        features, columns = piece_at(place_ref, k, piece.shape)
        sum_ref[:, columns] += dot(attn_ref[:, features], piece[...])
    core = place_ref[0]
    own_ref[...] = sum_ref[pl.ds(pl.multiple_of(core * rows, rows), rows), :]
    other_ref[...] = sum_ref[pl.ds(pl.multiple_of((1 - core) * rows, rows), rows), :]


def out_project(place, attn, pieces):
    rows, width = attn.shape[0], 2 * pieces[0].shape[1]
    shape = jax.ShapeDtypeStruct((rows // 2, width), f32)
    vmem = pl.BlockSpec(memory_space=pltpu.VMEM)
    return pl.pallas_call(
        out_project_kernel,
        in_specs=[pl.BlockSpec(memory_space=pltpu.SMEM)] + [vmem] * (1 + len(pieces)),
        out_specs=[vmem, vmem],
        out_shape=[shape, shape],
        scratch_shapes=[pltpu.VMEM((rows, width), f32)],
        compiler_params=pltpu.CompilerParams(vmem_limit_bytes=NEAR_BYTES),
        name="out_project",
    )(place, attn, *pieces)


def out_project_back_kernel(place_ref, own_ref, other_ref, attn_ref, *refs):
    pieces, (out_ref, partial_ref, grad_ref, sum_ref) = refs[:-4], refs[-4:]
    put_rows(grad_ref, place_ref[0], own_ref[...], other_ref[...])
    sum_ref[...] = jnp.zeros_like(sum_ref)
    for k, piece in enumerate(pieces):
        features, columns = piece_at(place_ref, k, piece.shape)
        sum_ref[:, features] += dot(grad_ref[:, columns], piece[...], NT)
    out_ref[...] = sum_ref[...].astype(bf16)
    spots, planes, rows, width = partial_ref.shape
    for h in range(2):
        partial = dot(attn_ref[...], grad_ref[:, h * width : (h + 1) * width], TN)
        for l in range(planes // 2):
            for j in range(spots):
                first = (l * spots + j) * rows
                partial_ref[j, h * (planes // 2) + l] = partial[first : first + rows].astype(bf16)


def out_project_back(place, own, other, attn, pieces, spots):
    rows, width = attn.shape
    vmem = pl.BlockSpec(memory_space=pltpu.VMEM)
    return pl.pallas_call(
        out_project_back_kernel,
        in_specs=[pl.BlockSpec(memory_space=pltpu.SMEM)] + [vmem] * (3 + len(pieces)),
        out_specs=[vmem, vmem],
        out_shape=[
            jax.ShapeDtypeStruct((rows, width), bf16),
            jax.ShapeDtypeStruct((spots, 4, width // (2 * spots), width), bf16),
        ],
        scratch_shapes=[pltpu.VMEM((rows, 2 * width), bf16), pltpu.VMEM((rows, width), f32)],
        compiler_params=pltpu.CompilerParams(vmem_limit_bytes=FAR_BYTES),
        name="out_project_back",
    )(place, own, other, attn, *pieces)


def attend_back_kernel(
    place_ref, low_ref, mine_ref, theirs_ref, cosine_ref, sine_ref, keys_ref, own_ref, out_ref, grad_ref, log_ref,
    query_grad_ref, keys_grad_ref, own_grad_ref, sum_ref, turned_key_ref, weight_ref, score_ref,
):
    h, heads = pl.program_id(0), pl.num_programs(0)
    blocks, rows = keys_ref.shape[0] + 1, mine_ref.shape[0]
    spot = place_ref[1]

    @pl.when(h == 0)
    def _():
        sum_ref[...] = jnp.zeros_like(sum_ref)
        for t in range(blocks):
            turned_key_ref[t] = seen_block(spot, keys_ref, own_ref, t)[:, :HEAD_SIZE].T

    query, out_grad = side_block(place_ref, mine_ref, theirs_ref), grad_ref[...]
    delta = jnp.sum((out_grad.astype(f32) * out_ref[...]).T, axis=0, keepdims=True)
    log_total, low = log_ref[0, 0:1, :], low_ref[0:1, :]
    for t in range(blocks):
        block = seen_block(spot, keys_ref, own_ref, t)
        key, value = block[:, :HEAD_SIZE], block[:, HEAD_SIZE:]
        weights = jnp.exp2(dot(key, query, NT) * SCALE_LOG2 - log_total)
        weights = jnp.where(block_mask(low, t, blocks, rows, 0), weights, 0.0)
        weight_ref[t] = weights.astype(bf16)
        score_ref[t] = (weights * (dot(value, out_grad, NT) - delta)).astype(bf16)
    query_grad = jnp.zeros((HEAD_SIZE, rows), f32)
    for t in range(blocks):
        query_grad = query_grad + dot(turned_key_ref[t], score_ref[t])
    query_grad = (query_grad * SCALE).T.astype(bf16).astype(f32)
    turned = query_grad * cosine_ref[...] - pltpu.roll(query_grad, HEAD_SIZE // 2, 1) * sine_ref[...]
    query_grad_ref[...] = turned.astype(bf16)
    for t in range(blocks):
        sum_ref[t, :, :HEAD_SIZE] += dot(score_ref[t], query)
        sum_ref[t, :, HEAD_SIZE:] += dot(weight_ref[t], out_grad)

    @pl.when(h == heads - 1)
    def _():
        for t in range(blocks):
            target = seen_block(spot, keys_grad_ref, own_grad_ref, t)
            target[:, :HEAD_SIZE] = (sum_ref[t, :, :HEAD_SIZE] * SCALE).astype(bf16)
            target[:, HEAD_SIZE:] = sum_ref[t, :, HEAD_SIZE:].astype(bf16)


def attend_back(place, low, mine, theirs, cosine, sine, keys, own, out, out_grad, log_total):
    blocks, rows = keys.shape[0] + 1, mine.shape[0]
    whole = lambda *shape: pl.BlockSpec(shape, lambda h, place: (0,) * len(shape))
    by_head = pl.BlockSpec((rows, HEAD_SIZE), lambda h, place: (0, h))
    by_half = pl.BlockSpec((rows, HEAD_SIZE), lambda h, place: (0, lax.rem(h, GROUP // 2)))
    table = pl.BlockSpec((rows, HEAD_SIZE), lambda h, place: (0, 0))
    return pl.pallas_call(
        attend_back_kernel,
        grid_spec=pltpu.PrefetchScalarGridSpec(
            num_scalar_prefetch=1,
            grid=(GROUP,),
            in_specs=[
                whole(8, rows), by_half, by_half, table, table, whole(*keys.shape), whole(*own.shape), by_head, by_head,
                pl.BlockSpec((1, 8, rows), lambda h, place: (h, 0, 0)),
            ],
            out_specs=[by_head, whole(*keys.shape), whole(*own.shape)],
            scratch_shapes=[
                pltpu.VMEM((blocks, rows, 2 * HEAD_SIZE), f32),
                pltpu.VMEM((blocks, HEAD_SIZE, rows), bf16),
                pltpu.VMEM((blocks, rows, rows), bf16),
                pltpu.VMEM((blocks, rows, rows), bf16),
            ],
        ),
        out_shape=[
            jax.ShapeDtypeStruct((rows, HALF_WIDTH), bf16),
            jax.ShapeDtypeStruct(keys.shape, bf16),
            jax.ShapeDtypeStruct(own.shape, bf16),
        ],
        compiler_params=pltpu.CompilerParams(vmem_limit_bytes=FAR_BYTES),
        cost_estimate=pl.CostEstimate(flops=28_000_000_000, bytes_accessed=8_000_000, transcendentals=7_000_000),
        name="attend_back",
    )(place, low, mine, theirs, cosine, sine, keys, own, out, out_grad, log_total)


def body(
    acts, teacher, valid, doc_starts, routes, gates,
    w_query, key_weight, value_weight, w_out, gain_attn, gain_ffn, w_gate, w_up, w_down,
):
    half, core = lax.axis_index("xh"), lax.axis_index("c")
    plane, spot = lax.axis_index(("xh", "xl")), lax.axis_index(PLANE_CHIPS)
    chip = lax.axis_index(CHIPS)
    tok_rows, model_dim = acts.shape
    chip_rows = 2 * tok_rows
    spots = lax.axis_size(PLANE_CHIPS)
    planes = lax.axis_size(("xh", "xl"))
    chips = spots * planes
    total_tokens = chips * chip_rows
    shard_rows = w_query.shape[0]

    side = chip % 2
    place = jnp.stack([core, spot, side, half, lax.axis_index("xl")]).astype(jnp.int32)
    gain_pair = jnp.pad(jnp.stack([gain_attn, gain_ffn], axis=1), ((0, 0), (0, HEAD_SIZE - 2)))
    kv_width = 3 * HEAD_SIZE
    quarter = HALF_WIDTH // 2
    core_word = core.astype(jnp.int32).reshape(1)
    packed = jax.ShapeDtypeStruct((shard_rows, kv_width + 2 * HALF_WIDTH), bf16)
    own_part, other_part = whole_call(
        pack_kernel, "pack", [packed, packed], core_word, key_weight, value_weight, gain_pair, w_query, w_out, words=1,
        near=False,
    )
    weights_sent, out_sent = whole_call(
        unpack_kernel, "unpack",
        [
            jax.ShapeDtypeStruct((chips, 2 * shard_rows, kv_width + quarter), bf16),
            jax.ShapeDtypeStruct((spots, 2 * shard_rows, HALF_WIDTH), bf16),
        ],
        core_word, own_part, core_swap(other_part), words=1, near=False,
    )
    pair_acts = lax.ppermute(acts, "z", PAIR)
    before_acts = lax.ppermute(acts, ("xh", "xl"), [(p, p + 1) for p in range(planes - 1)])
    weights_sent, pair_acts, before_acts = lax.optimization_barrier((weights_sent, pair_acts, before_acts))
    weights = exchange(weights_sent, CHIPS)
    chip_acts = (acts, core_swap(acts))
    pair_acts = (pair_acts, core_swap(pair_acts))
    before_acts = (before_acts, core_swap(before_acts))

    first_token = chip * chip_rows
    chip_pos = first_token + jnp.arange(chip_rows, dtype=jnp.int32)
    begin = doc_begin(chip_pos, doc_starts)
    table_pos = jnp.concatenate([chip_pos, chip_pos + (1 - 2 * side) * chip_rows, chip_pos - spots * chip_rows])
    cosine, sine = rope_tables(table_pos - doc_begin(table_pos, doc_starts))
    low = jnp.maximum(begin, chip_pos - (WINDOW - 1)) - (first_token - WINDOW)
    low_rows = jnp.broadcast_to(low[None, :], (8, chip_rows))
    low_columns = jnp.broadcast_to(low[:, None], (chip_rows, HEAD_SIZE))
    block_at = jnp.arange(spots, dtype=jnp.int32)

    weights, out_sent, chip_acts, pair_acts, before_acts, low_columns, cosine, sine = lax.optimization_barrier(
        (weights, out_sent, chip_acts, pair_acts, before_acts, low_columns, cosine, sine)
    )
    out_rows = exchange(out_sent, PLANE_CHIPS)
    weights = weights.reshape(model_dim, -1)

    normed_one, own_kv, kv_sent, gain_rows = project_keys(
        place, chip_acts, before_acts, weights, cosine, sine, spots
    )
    kv_sent, out_rows = lax.optimization_barrier((kv_sent, out_rows))
    seen_kv = exchange(kv_sent, PLANE_CHIPS)
    placed, placed_by_token, token_gate, slot_gate = place_rows(routes, gates)
    all_slots = EXPERTS * CAP

    out_rows = out_rows.reshape(-1, HALF_WIDTH)
    out_pieces = [
        lax.ppermute(
            out_rows,
            ("xh", "xl", "c"),
            [
                (c * 4 + (l ^ k % 2) * 2 + (h ^ k // 2), h * 4 + l * 2 + c)
                for h in range(2)
                for l in range(2)
                for c in range(2)
            ],
        )
        for k in range(4)
    ]
    seen_kv, out_pieces = lax.optimization_barrier((seen_kv, out_pieces))

    pair_normed, query_mine, query_theirs = project(
        place, normed_one, pair_acts, gain_rows, weights, cosine, sine
    )
    query_theirs = lax.ppermute(query_theirs, "z", PAIR)
    query_theirs, placed, slot_gate, token_gate, placed_by_token = lax.optimization_barrier(
        (query_theirs, placed, slot_gate, token_gate, placed_by_token)
    )
    attn_wide, attn, log_total = attend(place, low_columns, query_mine, query_theirs, seen_kv, own_kv)

    branch, other_branch = out_project(place, attn, out_pieces)
    wide = jax.ShapeDtypeStruct((tok_rows, model_dim), f32)
    slim = jax.ShapeDtypeStruct((tok_rows, model_dim), bf16)
    slot_rows = jax.ShapeDtypeStruct((all_slots, model_dim), bf16)
    hidden_one, sent_rows = whole_call(
        dispatch_kernel, "dispatch", [wide, slot_rows], branch, core_swap(other_branch), acts, gain_rows, placed
    )

    def to_experts(rows):
        mine = exchange(rows.reshape(EXPERTS, CAP, model_dim), HALF_CHIPS).reshape(all_slots, model_dim)
        return mine, core_swap(mine)

    def from_experts(mine, theirs):
        mine, came = lax.optimization_barrier((mine.astype(bf16), core_swap(theirs.astype(bf16))))
        both = mine.astype(f32) + came.astype(f32)
        both = both.astype(bf16).reshape(EXPERTS, CAP, model_dim)
        return exchange(both, HALF_CHIPS).reshape(all_slots, model_dim)

    units = w_gate.shape[1]
    gate_up = jnp.concatenate([w_gate, w_up], axis=1)

    def expert_hidden(rows):
        both = dot(rows, gate_up)
        gate_pre, up_pre = both[:, :units], both[:, units:]
        return gate_pre, up_pre, (jax.nn.silu(gate_pre) * up_pre).astype(bf16)

    def hidden_backward(kept, grad_rows):
        gate_pre, up_pre = kept[0], kept[1]
        grad_hidden = dot(grad_rows, w_down, NT)
        sigmoid = jax.nn.sigmoid(gate_pre)
        grad_gate = (grad_hidden * up_pre * sigmoid * (1.0 + gate_pre * (1.0 - sigmoid))).astype(bf16)
        grad_up = (grad_hidden * gate_pre * sigmoid).astype(bf16)
        return jnp.concatenate([grad_gate, grad_up], axis=1)

    def rows_backward(back):
        return dot(back, gate_up, NT)

    rows_mine, rows_theirs = to_experts(sent_rows)
    kept_mine = expert_hidden(rows_mine)
    kept_mine, rows_theirs = lax.optimization_barrier((kept_mine, rows_theirs))
    kept_theirs = expert_hidden(rows_theirs)
    returned = from_experts(dot(kept_mine[2], w_down), dot(kept_theirs[2], w_down))
    bounds = jnp.stack([valid[0], first_token + core * tok_rows]).astype(jnp.int32)
    loss_scale = (total_tokens / valid.astype(f32)).reshape(1)
    activations, grad_two, grad_slots = combine(
        bounds, loss_scale, returned, token_gate, hidden_one, teacher, placed, slot_gate
    )
    grads_mine, grads_theirs = to_experts(grad_slots)
    back_mine = hidden_backward(kept_mine, grads_mine)
    back_mine, grads_theirs = lax.optimization_barrier((back_mine, grads_theirs))
    back_theirs = hidden_backward(kept_theirs, grads_theirs)
    grad_returned = from_experts(rows_backward(back_mine), rows_backward(back_theirs))

    expert_parts = (
        (dot(rows_mine, back_mine, TN) + dot(rows_theirs, back_theirs, TN)).astype(bf16),
        (dot(kept_mine[2], grads_mine, TN) + dot(kept_theirs[2], grads_theirs, TN)).astype(bf16),
    )
    expert_part = jnp.concatenate(
        [expert_parts[0], expert_parts[1][:, :HALF_WIDTH], expert_parts[1][:, HALF_WIDTH:]]
    )

    expert_part, grad_returned = lax.optimization_barrier((expert_part, grad_returned))
    grad_one, grad_branch, gain_two_grad = whole_call(
        norm_back_kernel, "norm_back", [wide, slim, jax.ShapeDtypeStruct((8, model_dim), f32)],
        grad_returned, placed_by_token, hidden_one, gain_rows, grad_two, near=False,
    )
    grad_attn, out_partial = out_project_back(place, grad_branch, core_swap(grad_branch), attn, out_pieces, spots)

    def send_to_chips(partial):
        return exchange(partial.astype(bf16).reshape(chips, 2 * shard_rows, -1), CHIPS)

    expert_other = lax.ppermute(expert_part, "xh", SWAP)
    out_received = exchange(out_partial, PLANE_CHIPS)

    query_lin_grad, kv_grad, own_kv_grad = attend_back(
        place, low_rows, query_mine, query_theirs, cosine, sine, seen_kv, own_kv, attn_wide, grad_attn, log_total
    )
    query_left, query_right = query_lin_grad[:, :quarter], query_lin_grad[:, quarter:]
    pair_query_grad = lax.ppermute(jnp.where(side == 0, query_right, query_left), "z", PAIR)
    kv_grad, out_received = lax.optimization_barrier((kv_grad, out_received))
    came = exchange(kv_grad, PLANE_CHIPS)
    side_query_grad = jnp.where(side == 0, query_left, query_right)
    pair_normed_grad = dot(pair_query_grad, weights[:, kv_width:], NT)
    pair_normed_grad = of_core(core, pair_normed_grad, True) + core_swap(of_core(core, pair_normed_grad, False))
    back_normed_grad = lax.ppermute(pair_normed_grad.astype(bf16), "z", PAIR)
    side_normed_grad = dot(side_query_grad, weights[:, kv_width:], NT)
    came, expert_other, side_query_grad, pair_query_grad = lax.optimization_barrier(
        (came, expert_other, side_query_grad, pair_query_grad)
    )
    square = (chip_rows, 2 * HEAD_SIZE)
    later_grad, before_grad = whole_call(
        split_grads_kernel, "split_grads", [jax.ShapeDtypeStruct(square, f32), jax.ShapeDtypeStruct(square, bf16)],
        place, came, own_kv_grad, words=1,
    )
    next_grad = lax.ppermute(before_grad, ("xh", "xl"), [(p + 1, p) for p in range(planes - 1)])
    table = pl.BlockSpec((chip_rows, HEAD_SIZE), lambda i: (0, 0))
    next_grad, back_normed_grad = lax.optimization_barrier((next_grad, back_normed_grad))
    early = HEAD_SIZE + quarter
    partial_shape = jax.ShapeDtypeStruct((model_dim, early + 2 * HEAD_SIZE), bf16)
    (partial,) = whole_call(
        early_columns_kernel, "early_columns", [partial_shape],
        normed_one, pair_normed, side_query_grad, pair_query_grad, gain_two_grad,
        out_blocks={0: pl.BlockSpec((model_dim, early), lambda i: (0, 0))}, near=False,
    )
    partial, kv_lin_grad = whole_call(
        key_columns_kernel, "key_columns", [partial_shape, jax.ShapeDtypeStruct(square, bf16)],
        later_grad, next_grad, cosine, sine, normed_one, partial,
        blocks={2: table, 3: table, 5: pl.BlockSpec((16, HEAD_SIZE), lambda i: (0, 0))},
        out_blocks={0: pl.BlockSpec((model_dim, 2 * HEAD_SIZE), lambda i: (0, 2))}, aliases={5: 0}, near=False,
    )
    partial, expert_other, out_received, kv_lin_grad, side_normed_grad = lax.optimization_barrier(
        (partial, expert_other, out_received, kv_lin_grad, side_normed_grad)
    )
    normed_grad = side_normed_grad + dot(kv_lin_grad, weights[:, : 2 * HEAD_SIZE], NT)
    swapped_grad, expert_other = lax.optimization_barrier(
        (core_swap(of_core(core, normed_grad, False)), expert_other)
    )
    (grad_acts,) = whole_call(
        acts_back_kernel, "acts_back", [wide],
        of_core(core, normed_grad, True), swapped_grad, back_normed_grad, acts,
        gain_rows, grad_one, near=False, cost=pl.CostEstimate(flops=1, bytes_accessed=1, transcendentals=0),
    )
    received = send_to_chips(partial)
    expert_grads = expert_sums(expert_part, expert_other, model_dim)
    plane_sums = jnp.sum(out_received.astype(f32), axis=0).astype(bf16)
    plane_sums = plane_sums.reshape(2, 2, 2, shard_rows, -1)
    pieces = []
    for k in range(4):
        piece = lax.dynamic_index_in_dim(plane_sums, (lax.axis_index("xl") + k) % 2, 1, False)
        piece = lax.dynamic_index_in_dim(piece, (half + k // 2) % 2, 1, False)
        piece = lax.ppermute(
            piece,
            ("xh", "xl", "c"),
            [
                (h * 4 + l * 2 + c, c * 4 + (l ^ k % 2) * 2 + (h ^ k // 2))
                for h in range(2)
                for l in range(2)
                for c in range(2)
            ],
        )
        pieces.append(piece)
    pieces, expert_grads, grad_acts = lax.optimization_barrier((pieces, expert_grads, grad_acts))
    grad_w_out = sum(piece.astype(f32) for piece in pieces)
    grad_w_out = jnp.concatenate([grad_w_out[0], grad_w_out[1]], axis=1)
    received = received.astype(f32).reshape(chips // 2, 2, 2 * shard_rows, -1)
    sums = jnp.sum(received, axis=0)
    shared = sums[0] + sums[1]
    sums = jnp.concatenate(
        [shared[:, early:], shared[:, :HEAD_SIZE], sums[0, :, HEAD_SIZE:early], sums[1, :, HEAD_SIZE:early]], axis=1
    ).reshape(2, shard_rows, -1)
    given = core_swap(jnp.where(core == 0, sums[1], sums[0]))
    kept = jnp.where(core == 0, sums[0], sums[1])
    sums = (jnp.where(core == 0, kept, given), jnp.where(core == 0, given, kept))

    def columns(begin_at, width):
        return jnp.concatenate([part[:, begin_at : begin_at + width] for part in sums], axis=1)

    grad_query, grad_key, grad_value = columns(kv_width, HALF_WIDTH), columns(0, HEAD_SIZE), columns(HEAD_SIZE, HEAD_SIZE)
    weight_columns = np.arange(kv_width + HALF_WIDTH)
    weight_columns = (weight_columns < 2 * HEAD_SIZE) | (weight_columns >= kv_width)
    halves = (jnp.where(core == 0, own_part, other_part), jnp.where(core == 0, other_part, own_part))
    terms = [
        jnp.where(weight_columns[None], weight[:, : kv_width + HALF_WIDTH].astype(f32) * grad, 0.0)
        for weight, grad in zip(halves, sums)
    ]
    grad_gain_attn = jnp.sum(terms[0] + terms[1], axis=1) / gain_attn.astype(f32)
    return (
        activations,
        grad_acts,
        grad_query,
        grad_key,
        grad_value,
        grad_w_out,
        grad_gain_attn,
        sums[0][:, 2 * HEAD_SIZE] + sums[1][:, 2 * HEAD_SIZE],
        *expert_grads,
    )


def solution(mesh):
    fine_mesh = jax.sharding.Mesh(mesh.devices.reshape(2, 2, 4, 4, 2), ALL)
    rows, vector = P(ALL, None), P(ALL)
    wide, tall = P(None, ("xl", "y", "z", "c")), P(("xl", "y", "z", "c"), None)
    return jax.shard_map(
        body,
        mesh=fine_mesh,
        in_specs=(
            rows, rows, P(), P(), rows, rows, rows, rows, rows, rows, vector, vector, wide, wide, tall,
        ),
        out_specs=(rows, rows, rows, rows, rows, rows, vector, vector, wide, wide, tall),
        check_vma=False,
    )
```
